32 devices in a mesh: row: 4 (over y, core), col: 8 (over z, x).
Axes of the slice: x: 2, y: 2, z: 4, core: 2. Of those that a mesh axis runs over, the one named last changes fastest.
Arguments:
- matrix: float32 [4096, 4096], P('row', 'col'), may hold values from -4 to 4, as said below
- panel: float32 [4096, 64], P('row'), may hold values from -1200 to 1200
Outputs:
- updated: float32 [4096, 4096], P('row', 'col')
- w_rows: float32 [4096, 64], P('row')
- basis: float32 [4096, 64], P('row')
The draws below stay inside these ranges and needn't reach their ends.
Inputs may be any that keep to these rules, and one draw needn't show every extreme that they name: Read in global order (both indices mapped back through their cyclic orders) the matrix is exactly symmetric.
All inputs are finite; a program needn't handle non-finite values.
Results may differ from the reference program's by a relative error of at most 0.00007.
Values sent between devices are 32-bit elements; how exact they have to be, the bound alone decides.
No kernel may reach another device: no remote copies, remote signals or barrier semaphores. Data moves between devices by JAX's collectives and lax.ppermute only.
A program may use at most 64 MiB of HBM per device.

```python
import math
import jax
import jax.numpy as jnp
from jax import lax

NB = 64
M = 4096
N_ROW = 4
N_COL = 8


def draw_matrix(key, part):
    key = jax.random.fold_in(key, 11)
    first = jax.random.fold_in(key, 0)
    base = 0.5 * jnp.clip(jax.random.normal(first, (M, M), jnp.float32), -4.0, 4.0)
    row_ids = jnp.arange(M)[:, None]
    col_ids = jnp.arange(M)[None, :]
    sym = jnp.where(row_ids >= col_ids, base, base.T)
    row_blocks = M // (NB * N_ROW)
    col_blocks = M // (NB * N_COL)
    sym = sym.reshape(row_blocks, N_ROW, NB, M).transpose(1, 0, 2, 3).reshape(M, M)
    sym = sym.reshape(M, col_blocks, N_COL, NB).transpose(0, 2, 1, 3).reshape(M, M)
    return sym


def draw_panel(key, part):
    key = jax.random.fold_in(key, 12)
    first, second, third = jax.random.split(key, 3)
    base = jnp.clip(jax.random.normal(first, (M, NB), jnp.float32), -4.0, 4.0)
    col_scale = jnp.exp(jax.random.uniform(second, (NB,), jnp.float32, 0.0, math.log(10.0)))
    row_scale = jnp.exp(jax.random.uniform(third, (M,), jnp.float32, 0.0, math.log(10.0)))
    ramp = 1.0 + 2.0 * jnp.arange(M, dtype=jnp.float32) / M
    return base * col_scale[None, :] * (row_scale * ramp)[:, None]


def setup_inputs(seed: int = 0) -> dict:
    keys = jax.random.split(jax.random.key(seed), 3)
    matrix = draw_matrix(jax.random.fold_in(keys[2], 71), 0)
    panel = draw_panel(jax.random.fold_in(keys[2], 71), 0)
    return dict(matrix=matrix, panel=panel)


HIGH = lax.Precision.HIGHEST

def to_global(values, parts):
    total = values.shape[0]
    blocks = total // (NB * parts)
    return values.reshape(parts, blocks, NB, -1).transpose(1, 0, 2, 3).reshape(total, -1)

def to_stored(values, parts):
    total = values.shape[0]
    blocks = total // (NB * parts)
    return values.reshape(blocks, parts, NB, -1).transpose(1, 0, 2, 3).reshape(total, -1)

def reference(matrix, panel):
    gram = jnp.dot(panel.T.astype(jnp.float32), panel.astype(jnp.float32), precision=HIGH, preferred_element_type=jnp.float32)
    lower = lax.linalg.cholesky(gram)
    basis = lax.linalg.triangular_solve(lower, panel, left_side=False, lower=True, transpose_a=True)
    basis_cols = to_stored(to_global(basis, N_ROW), N_COL)
    product = jnp.dot(matrix.astype(jnp.float32), basis_cols.astype(jnp.float32), precision=HIGH, preferred_element_type=jnp.float32)
    correction = jnp.dot(basis.T.astype(jnp.float32), product.astype(jnp.float32), precision=HIGH, preferred_element_type=jnp.float32)
    w_rows = 2.0 * (product - jnp.dot(basis.astype(jnp.float32), correction.astype(jnp.float32), precision=HIGH, preferred_element_type=jnp.float32))
    w_cols = to_stored(to_global(w_rows, N_ROW), N_COL)
    left = jnp.concatenate([basis, w_rows], axis=1)
    right = jnp.concatenate([w_cols, basis_cols], axis=1)
    updated = matrix - jnp.dot(left.astype(jnp.float32), right.T.astype(jnp.float32), precision=HIGH, preferred_element_type=jnp.float32)
    return (updated, w_rows, basis)
```

```python
import jax
import jax.numpy as jnp
from jax import lax
from jax.sharding import PartitionSpec as P

HIGH = lax.Precision.HIGHEST


def dot(left, right, contract):
    return lax.dot_general(
        left, right, (contract, ((), ())), precision=HIGH, preferred_element_type=jnp.float32
    )


def exchange_sum(value, axis, radix):
    size = lax.axis_size(axis)
    step = 1
    while step < size:
        group = min(radix, size // step)
        parts = [value]
        for other in range(1, group):
            pairs = [(i, i ^ (other * step)) for i in range(size)]
            parts.append(lax.ppermute(value, axis, pairs))
        while len(parts) > 1:
            parts = [parts[i] + parts[i + 1] for i in range(0, len(parts), 2)]
        value = parts[0]
        step *= group
    return value


def transpose_grid(value, shift):
    n_row, n_col = lax.axis_size("row"), lax.axis_size("col")
    ratio = n_col // n_row
    pairs = []
    for r in range(n_row):
        for k in range(ratio):
            for q in range(n_row):
                source = q * n_col + ((k + shift) % ratio) * n_row + r
                pairs.append((source, r * n_col + k * n_row + q))
    return lax.ppermute(value, ("row", "col"), pairs)


def local(matrix, panel):
    n_row, n_col = lax.axis_size("row"), lax.axis_size("col")
    ratio = n_col // n_row
    width = panel.shape[1]
    cols_local = matrix.shape[1]
    which = lax.axis_index("col") // n_row

    panel_t = panel.T
    mine = panel_t.reshape(width, cols_local // width, ratio, width)
    mine = lax.dynamic_index_in_dim(mine, which, 2, keepdims=False).reshape(width, cols_local)
    panel_cols = transpose_grid(mine, 0)

    gram = exchange_sum(dot(panel, panel, ((0,), (0,))), "row", 4)
    product_cols = exchange_sum(dot(panel, matrix, ((0,), (0,))), "row", 4)

    lower = lax.linalg.cholesky(gram)
    inverse = lax.linalg.triangular_solve(
        lower, jnp.eye(width, dtype=jnp.float32), left_side=True, lower=True
    )

    halves = [transpose_grid(product_cols, shift) for shift in range(ratio)]
    inner = exchange_sum(dot(panel_cols, product_cols, ((1,), (1,))), "col", 8)
    halves = jnp.stack(halves)
    product_rows = jnp.stack(
        [
            lax.dynamic_index_in_dim(halves, (k - which) % ratio, 0, keepdims=False)
            for k in range(ratio)
        ]
    )
    product_rows = (
        product_rows.reshape(ratio, width, cols_local // width, width)
        .transpose(1, 2, 0, 3)
        .reshape(width, panel.shape[0])
    )

    correction = dot(dot(inverse, inner, ((1,), (0,))), inverse, ((1,), (1,)))
    basis = dot(panel, inverse, ((1,), (1,)))
    basis_cols = dot(inverse, panel_cols, ((1,), (0,)))
    w_rows = 2.0 * (
        dot(product_rows, inverse, ((0,), (1,))) - dot(basis, correction, ((1,), (0,)))
    )
    w_cols = 2.0 * (
        dot(inverse, product_cols, ((1,), (0,))) - dot(correction, basis_cols, ((0,), (0,)))
    )
    left = jnp.concatenate([basis, w_rows], axis=1)
    right = jnp.concatenate([w_cols, basis_cols], axis=0)
    updated = matrix - dot(left, right, ((1,), (0,)))
    return (updated, w_rows, basis)


def solution(mesh):
    return jax.shard_map(
        local,
        mesh=mesh,
        in_specs=(P("row", "col"), P("row", None)),
        out_specs=(P("row", "col"), P("row", None), P("row", None)),
        check_vma=False,
    )
```

```python
import functools

import jax
import jax.numpy as jnp
from jax import lax
from jax.experimental import pallas as pl
from jax.experimental.pallas import tpu as pltpu
from jax.sharding import PartitionSpec as P

HIGH = lax.Precision.HIGHEST
VMEM = pl.BlockSpec(memory_space=pltpu.VMEM)
SMEM = pl.BlockSpec(memory_space=pltpu.SMEM)
PARAMS = pltpu.CompilerParams(vmem_limit_bytes=40 * 1024 * 1024)


def dot(left, right, contract, precision=HIGH):
    return lax.dot_general(
        left, right, (contract, ((), ())), precision=precision, preferred_element_type=jnp.float32
    )


def partner(value, axis, step):
    size = lax.axis_size(axis)
    return lax.ppermute(value, axis, [(i, i ^ step) for i in range(size)])


def transpose_grid(value, shift):
    n_row, n_col = lax.axis_size("row"), lax.axis_size("col")
    ratio = n_col // n_row
    pairs = []
    for r in range(n_row):
        for k in range(ratio):
            for q in range(n_row):
                source = q * n_col + ((k + shift) % ratio) * n_row + r
                pairs.append((source, r * n_col + k * n_row + q))
    return lax.ppermute(value, ("row", "col"), pairs)


def pick_kernel(ratio, which_ref, panel_ref, mine_ref):
    width = panel_ref.shape[0]
    which = which_ref[0]
    count = mine_ref.shape[1] // width
    for j in range(count):
        block = panel_ref[:, j * ratio * width : (j * ratio + 1) * width]
        for k in range(1, ratio):
            start = (j * ratio + k) * width
            block = jnp.where(which == k, panel_ref[:, start : start + width], block)
        mine_ref[:, j * width : (j + 1) * width] = block


def product_kernel(panel_ref, matrix_ref, out_ref):
    width = panel_ref.shape[0]
    cols = matrix_ref.shape[1]
    panel = panel_ref[...]

    @pl.when(pl.program_id(0) == 0)
    def _():
        out_ref[...] = jnp.zeros_like(out_ref)

    out_ref[:, :cols] += dot(panel, matrix_ref[...], ((1,), (0,)))
    out_ref[:, cols : cols + width] += dot(panel, panel, ((1,), (1,)))


def inner_kernel(mine_ref, other_ref, panel_cols_ref, product_ref, gram_ref, inner_ref):
    cols = product_ref.shape[1]
    total = mine_ref[...] + other_ref[...]
    product = total[:, :cols]
    product_ref[...] = product
    gram_ref[...] = total[:, cols:]
    inner_ref[...] = dot(panel_cols_ref[...], product, ((1,), (1,)))


def factor_kernel(gram_ref, inverse_ref):
    size = inverse_ref.shape[0]
    batch = 4
    row = lax.broadcasted_iota(jnp.int32, (size, 2 * size), 0)
    lane = lax.broadcasted_iota(jnp.int32, (size, 2 * size), 1)
    eye = jnp.where(row == lane, 1.0, 0.0).astype(jnp.float32)
    table = jnp.concatenate([eye[:, :size], gram_ref[:, :size]], axis=1)
    for first in range(0, size, batch):
        base = first // 8 * 8
        height = size - base
        low = table[base:, :]
        low_row = row[base:, :]
        cols = [
            jnp.broadcast_to(low[:, size + first + t : size + first + t + 1], (height, 2 * size))
            for t in range(batch)
        ]
        rows = [low[first - base + t : first - base + t + 1, :] for t in range(batch)]
        for t in range(batch):
            at = first - base + t
            scale = 1.0 / cols[t][at : at + 1, :]
            factor = jnp.where(low_row > first + t, cols[t] * scale, 0.0)
            for s in range(t + 1, batch):
                cols[s] = cols[s] - factor * cols[s][at : at + 1, :]
                rows[s] = rows[s] - factor[first - base + s : first - base + s + 1, :] * rows[t]
            low = low - factor * rows[t]
        table = low if base == 0 else jnp.concatenate([table[:base, :], low], axis=0)
    diagonal = jnp.sum(jnp.where(lane == row + size, table, 0.0), axis=1, keepdims=True)
    inverse_ref[...] = (table / jnp.sqrt(diagonal))[:, :size]


def update_kernel(
    ratio,
    which_ref,
    matrix_ref,
    panel_ref,
    panel_cols_ref,
    product_cols_ref,
    inverse_ref,
    inner_ref,
    *refs,
):
    halves, (updated_ref, w_ref, basis_ref, left_ref, right_ref) = refs[:ratio], refs[ratio:]
    width = inverse_ref.shape[0]
    rows = matrix_ref.shape[0]
    step = pl.program_id(0)

    @pl.when(step == 0)
    def _():
        inverse = inverse_ref[...]
        which = which_ref[0]
        correction = dot(dot(inverse, inner_ref[...], ((1,), (0,))), inverse, ((1,), (1,)))
        basis = dot(inverse, panel_ref[...], ((1,), (0,)))
        basis_cols = dot(inverse, panel_cols_ref[...], ((1,), (0,)))
        parts = []
        for j in range(product_cols_ref.shape[1] // width):
            span = slice(j * width, (j + 1) * width)
            for k in range(ratio):
                block = halves[0][:, span]
                for shift in range(1, ratio):
                    block = jnp.where(
                        (which + shift) % ratio == k, halves[shift][:, span], block
                    )
                parts.append(block)
        product_rows = jnp.concatenate(parts, axis=1)
        w_rows = 2.0 * (
            dot(inverse, product_rows, ((1,), (0,))) - dot(correction, basis, ((0,), (0,)))
        )
        w_cols = 2.0 * (
            dot(inverse, product_cols_ref[...], ((1,), (0,)))
            - dot(correction, basis_cols, ((0,), (0,)))
        )
        basis_ref[...] = basis
        w_ref[...] = w_rows
        left_ref[:width, :] = basis
        left_ref[width:, :] = w_rows
        right_ref[:width, :] = w_cols
        right_ref[width:, :] = basis_cols

    span = pl.ds(pl.multiple_of(step * rows, rows), rows)
    updated_ref[...] = matrix_ref[...] - dot(left_ref[:, span], right_ref[...], ((0,), (0,)))


def shape(*dims):
    return jax.ShapeDtypeStruct(dims, jnp.float32)


def cost(flops, moved):
    return pl.CostEstimate(flops=flops, bytes_accessed=moved, transcendentals=0)


def local(matrix, panel):
    n_row, n_col = lax.axis_size("row"), lax.axis_size("col")
    ratio = n_col // n_row
    rows, width = panel.shape
    cols = matrix.shape[1]
    which = (lax.axis_index("col") // n_row).astype(jnp.int32).reshape(1)
    panel_t = panel.T
    chunks = 4

    mine = pl.pallas_call(
        functools.partial(pick_kernel, ratio),
        out_shape=shape(width, cols),
        in_specs=[SMEM, VMEM],
        out_specs=VMEM,
        compiler_params=PARAMS,
    )(which, panel_t)
    panel_cols = transpose_grid(mine, 0)

    total = pl.pallas_call(
        product_kernel,
        grid=(chunks,),
        out_shape=shape(width, cols + 2 * width),
        in_specs=[
            pl.BlockSpec((width, rows // chunks), lambda i: (0, i)),
            pl.BlockSpec((rows // chunks, cols), lambda i: (i, 0)),
        ],
        out_specs=pl.BlockSpec((width, cols + 2 * width), lambda i: (0, 0)),
        compiler_params=PARAMS,
        cost_estimate=cost(12 * width * rows * cols, 4 * rows * cols),
    )(panel_t, matrix)

    step = 1
    while 2 * step < n_row:
        total = total + partner(total, "row", step)
        step *= 2
    product_cols, gram, inner = pl.pallas_call(
        inner_kernel,
        out_shape=(shape(width, cols), shape(width, 2 * width), shape(width, width)),
        in_specs=[VMEM] * 3,
        out_specs=(VMEM,) * 3,
        compiler_params=PARAMS,
    )(total, partner(total, "row", step), panel_cols)

    halves = [transpose_grid(product_cols, shift) for shift in range(ratio)]
    inverse = pl.pallas_call(
        factor_kernel,
        out_shape=shape(width, width),
        in_specs=[VMEM],
        out_specs=VMEM,
        compiler_params=PARAMS,
        cost_estimate=cost(1 << 30, 1 << 16),
    )(gram)
    step = 1
    while step < n_col:
        inner = inner + partner(inner, "col", step)
        step *= 2

    whole = lambda a, b: pl.BlockSpec((a, b), lambda i: (0, 0))
    updated, w_rows, basis = pl.pallas_call(
        functools.partial(update_kernel, ratio),
        grid=(chunks,),
        out_shape=(shape(rows, cols), shape(width, rows), shape(width, rows)),
        in_specs=[
            SMEM,
            pl.BlockSpec((rows // chunks, cols), lambda i: (i, 0)),
            whole(width, rows),
            whole(width, cols),
            whole(width, cols),
            whole(width, width),
            whole(width, width),
        ]
        + [whole(width, cols)] * ratio,
        out_specs=(
            pl.BlockSpec((rows // chunks, cols), lambda i: (i, 0)),
            whole(width, rows),
            whole(width, rows),
        ),
        scratch_shapes=[
            pltpu.VMEM((2 * width, rows), jnp.float32),
            pltpu.VMEM((2 * width, cols), jnp.float32),
        ],
        compiler_params=PARAMS,
        cost_estimate=cost(24 * width * rows * cols, 8 * rows * cols),
    )(which, matrix, panel_t, panel_cols, product_cols, inverse, inner, *halves)
    return (updated, w_rows.T, basis.T)


def solution(mesh):
    return jax.shard_map(
        local,
        mesh=mesh,
        in_specs=(P("row", "col"), P("row", None)),
        out_specs=(P("row", "col"), P("row", None), P("row", None)),
        check_vma=False,
    )
```

```python
import functools

import jax
import jax.numpy as jnp
from jax import lax
from jax.experimental import pallas as pl
from jax.experimental.pallas import tpu as pltpu
from jax.sharding import PartitionSpec as P

HIGH = lax.Precision.HIGHEST
VMEM = pl.BlockSpec(memory_space=pltpu.VMEM)
SMEM = pl.BlockSpec(memory_space=pltpu.SMEM)
HBM = pl.BlockSpec(memory_space=pltpu.HBM)
PARAMS = pltpu.CompilerParams(vmem_limit_bytes=40 * 1024 * 1024)
STRIP = 8


def dot(left, right, contract, precision=HIGH):
    return lax.dot_general(
        left, right, (contract, ((), ())), precision=precision, preferred_element_type=jnp.float32
    )


def dot16(left, right, contract):
    return dot(left, right, contract, lax.Precision.DEFAULT)


def split(value, parts):
    terms = []
    for _ in range(parts):
        terms.append(value.astype(jnp.bfloat16))
        value = value - terms[-1].astype(jnp.float32)
    return terms


def partner(value, axis, step):
    size = lax.axis_size(axis)
    return lax.ppermute(value, axis, [(i, i ^ step) for i in range(size)])


def group_sum(value, axis, low, high):
    while low < high:
        radix = min(4, high // low)
        parts = [value] + [partner(value, axis, i * low) for i in range(1, radix)]
        while len(parts) > 1:
            parts = [parts[i] + parts[i + 1] for i in range(0, len(parts), 2)]
        value = parts[0]
        low *= radix
    return value


def transpose_grid(value, shift):
    n_row, n_col = lax.axis_size("row"), lax.axis_size("col")
    ratio = n_col // n_row
    pairs = []
    for r in range(n_row):
        for k in range(ratio):
            for q in range(n_row):
                source = q * n_col + ((k + shift) % ratio) * n_row + r
                pairs.append((source, r * n_col + k * n_row + q))
    return lax.ppermute(value, ("row", "col"), pairs)


def panel_kernel(
    ratio, which_ref, panel_ref, matrix_ref,
    mine_ref, held_ref, terms_ref, gram_ref, kept_ref, sems,
):
    width = panel_ref.shape[0]
    pieces = sems.shape[0] // 2
    copies = []
    for piece in range(pieces):
        size = width // pieces
        span = slice(piece * size, (piece + 1) * size)
        copies.append(
            pltpu.make_async_copy(panel_ref.at[span, :], held_ref.at[span, :], sems.at[piece])
        )
    for piece in range(pieces):
        size = matrix_ref.shape[0] // pieces
        span = slice(piece * size, (piece + 1) * size)
        copies.append(
            pltpu.make_async_copy(
                matrix_ref.at[span, :], kept_ref.at[span, :], sems.at[pieces + piece]
            )
        )
    for copy in copies:
        copy.start()
    for copy in copies[:pieces]:
        copy.wait()
    which = which_ref[0]
    for j in range(mine_ref.shape[1] // width):
        start = j * ratio * width
        block = held_ref[:, start : start + width]
        for k in range(1, ratio):
            start += width
            block = jnp.where(which == k, held_ref[:, start : start + width], block)
        mine_ref[:, j * width : (j + 1) * width] = block
    panel = held_ref[...]
    terms_ref[...] = jnp.concatenate(split(panel, 3), axis=0)
    gram = dot(panel, panel, ((1,), (1,)))
    to_strip(gram, gram_ref)
    for copy in copies[pieces:]:
        copy.wait()


def product_kernel(terms_ref, matrix_ref, gram_ref, out_ref):
    width = out_ref.shape[0] - STRIP
    rows = matrix_ref.shape[0]
    chunk = 256
    total = jnp.zeros((width, matrix_ref.shape[1]), jnp.float32)
    for start in range(0, rows, chunk):
        span = slice(start, start + chunk)
        parts = split(matrix_ref[span, :], 3)
        for i, part in enumerate(parts):
            count = 3 - i
            out = dot16(terms_ref[: count * width, span], part, ((1,), (0,)))
            for t in range(count):
                total = total + out[t * width : (t + 1) * width, :]
    out_ref[:width, :] = total
    out_ref[width:, :] = gram_ref[...]


def inner_kernel(panel_cols_ref, message_ref, inner_ref):
    width = inner_ref.shape[0]
    inner_ref[...] = dot(panel_cols_ref[...], message_ref[:width, :], ((1,), (1,)))


def to_strip(value, strip_ref):
    width = value.shape[0]
    for i in range(width // STRIP):
        strip_ref[:, i * width : (i + 1) * width] = value[i * STRIP : (i + 1) * STRIP, :]


def from_strip(strip, width):
    return jnp.concatenate(
        [strip[:, i * width : (i + 1) * width] for i in range(width // STRIP)], axis=0
    )


def finish_kernel(mine_ref, other_ref, inner_ref, inner_other_ref, product_ref, send_ref, gram_ref):
    width = product_ref.shape[0]
    product = mine_ref[:width, :] + other_ref[:width, :]
    product_ref[...] = product
    send_ref[:width, :] = product
    to_strip(inner_ref[...] + inner_other_ref[...], send_ref.at[width:, :])
    gram_ref[...] = from_strip(mine_ref[width:, :] + other_ref[width:, :], width)


def factor_kernel(gram_ref, inverse_ref):
    size = inverse_ref.shape[0]
    batch = 4
    row = lax.broadcasted_iota(jnp.int32, (size, 2 * size), 0)
    lane = lax.broadcasted_iota(jnp.int32, (size, 2 * size), 1)
    eye = jnp.where(row == lane, 1.0, 0.0).astype(jnp.float32)
    table = jnp.concatenate([eye[:, :size], gram_ref[...]], axis=1)
    for first in range(0, size, batch):
        base = first // 8 * 8
        height = size - base
        low = table[base:, :]
        low_row = row[base:, :]
        cols = [
            jnp.broadcast_to(low[:, size + first + t : size + first + t + 1], (height, 2 * size))
            for t in range(batch)
        ]
        rows = [low[first - base + t : first - base + t + 1, :] for t in range(batch)]
        for t in range(batch):
            at = first - base + t
            scale = 1.0 / cols[t][at : at + 1, :]
            factor = jnp.where(low_row > first + t, cols[t] * scale, 0.0)
            for s in range(t + 1, batch):
                cols[s] = cols[s] - factor * cols[s][at : at + 1, :]
                rows[s] = rows[s] - factor[first - base + s : first - base + s + 1, :] * rows[t]
            low = low - factor * rows[t]
        table = low if base == 0 else jnp.concatenate([table[:base, :], low], axis=0)
    diagonal = jnp.sum(jnp.where(lane == row + size, table, 0.0), axis=1, keepdims=True)
    inverse_ref[...] = (table / jnp.sqrt(diagonal))[:, :size]


def stack_left(value):
    high, low = split(value, 2)
    return jnp.concatenate([high, low, high], axis=0)


def stack_right(value):
    high, low = split(value, 2)
    return jnp.concatenate([high, high, low], axis=0)


def basis_kernel(
    matrix_ref, panel_ref, panel_cols_ref, product_cols_ref, inverse_ref,
    begun_ref, basis_ref, right_ref,
):
    inverse = inverse_ref[...]
    basis = dot(inverse, panel_ref[...], ((1,), (0,)))
    basis_cols = dot(inverse, panel_cols_ref[...], ((1,), (0,)))
    image_cols = dot(inverse, product_cols_ref[...], ((1,), (0,)))
    basis_ref[...] = basis
    right_ref[...] = stack_right(basis_cols)
    left = stack_left(basis)
    right = stack_right(2.0 * image_cols)
    chunk = 256
    for start in range(0, matrix_ref.shape[0], chunk):
        span = slice(start, start + chunk)
        begun_ref[span, :] = matrix_ref[span, :] - dot16(left[:, span], right, ((0,), (0,)))


def update_kernel(
    ratio, which_ref, begun_ref, basis_ref, right_ref, inverse_ref, sent_ref, *refs
):
    halves, (updated_ref, w_ref, buffer_ref, sems) = refs[:ratio], refs[ratio:]
    inverse = inverse_ref[...]
    width = inverse.shape[0]
    which = which_ref[0]
    parts = []
    for j in range(halves[0].shape[1] // width):
        span = slice(j * width, (j + 1) * width)
        for k in range(ratio):
            block = halves[0][:, span]
            for shift in range(1, ratio):
                block = jnp.where(
                    (which + shift) % ratio == k, halves[shift][:width, span], block
                )
            parts.append(block)
    image = dot(inverse, jnp.concatenate(parts, axis=1), ((1,), (0,)))
    strip = sent_ref[width:, :]
    for half in halves[1:]:
        strip = strip + half[width:, :]
    inner = from_strip(strip, width)
    correction = dot(dot(inverse, inner, ((1,), (0,))), inverse, ((1,), (1,)))
    removed = dot(correction, basis_ref[...], ((0,), (0,)))
    w_ref[...] = 2.0 * (image - removed)
    left = stack_left(2.0 * image - 4.0 * removed)
    right = right_ref[...]
    count = sems.shape[0]
    chunk = begun_ref.shape[0] // count
    copies = []
    for i in range(count):
        span = slice(i * chunk, (i + 1) * chunk)
        buffer_ref[span, :] = begun_ref[span, :] - dot16(left[:, span], right, ((0,), (0,)))
        copies.append(
            pltpu.make_async_copy(buffer_ref.at[span, :], updated_ref.at[span, :], sems.at[i])
        )
        copies[-1].start()
    for copy in copies:
        copy.wait()


def shape(*dims, dtype=jnp.float32):
    return jax.ShapeDtypeStruct(dims, dtype)


def call(kernel, outs, args, in_specs=None, out_specs=None, scratch=(), flops=0):
    return pl.pallas_call(
        kernel,
        out_shape=outs,
        in_specs=in_specs or [VMEM] * len(args),
        out_specs=out_specs or ((VMEM,) * len(outs) if isinstance(outs, tuple) else VMEM),
        scratch_shapes=scratch,
        compiler_params=PARAMS,
        cost_estimate=pl.CostEstimate(flops=flops, bytes_accessed=1 << 18, transcendentals=0),
    )(*args)


def local(matrix, panel):
    n_row, n_col = lax.axis_size("row"), lax.axis_size("col")
    ratio = n_col // n_row
    rows, width = panel.shape
    cols = matrix.shape[1]
    which = (lax.axis_index("col") // n_row).astype(jnp.int32).reshape(1)
    chunks = 8

    mine, panel_t, terms, gram, kept = call(
        functools.partial(panel_kernel, ratio),
        (
            shape(width, cols),
            shape(width, rows),
            shape(3 * width, rows, dtype=jnp.bfloat16),
            shape(STRIP, cols),
            shape(rows, cols),
        ),
        (
            which,
            pltpu.with_memory_space_constraint(panel.T, pltpu.HBM),
            pltpu.with_memory_space_constraint(matrix, pltpu.HBM),
        ),
        in_specs=[SMEM, HBM, HBM],
        scratch=[pltpu.SemaphoreType.DMA((2 * chunks,))],
        flops=1 << 28,
    )
    panel_cols = transpose_grid(mine, 0)
    message = call(
        product_kernel, shape(width + STRIP, cols), (terms, kept, gram), flops=1 << 30
    )
    step = 1
    while 2 * step < n_row:
        message = message + partner(message, "row", step)
        step *= 2
    last = partner(message, "row", step)
    inner = call(inner_kernel, shape(width, width), (panel_cols, message), flops=1 << 24)
    inner = group_sum(inner, "col", 1, n_row)
    product_cols, sent, gram = call(
        finish_kernel,
        (shape(width, cols), shape(width + STRIP, cols), shape(width, width)),
        (message, last, inner, partner(inner, "row", step)),
        flops=1 << 24,
    )
    halves = [transpose_grid(product_cols, 0)]
    halves += [transpose_grid(sent, shift) for shift in range(1, ratio)]
    inverse = call(factor_kernel, shape(width, width), (gram,), flops=1 << 30)
    begun, basis, right = call(
        basis_kernel,
        (shape(rows, cols), shape(width, rows), shape(3 * width, cols, dtype=jnp.bfloat16)),
        (kept, panel_t, panel_cols, product_cols, inverse),
        flops=1 << 30,
    )
    updated, w_rows = call(
        functools.partial(update_kernel, ratio),
        (shape(rows, cols), shape(width, rows)),
        (which, begun, basis, right, inverse, sent, *halves),
        in_specs=[SMEM] + [VMEM] * (5 + ratio),
        out_specs=(HBM, VMEM),
        scratch=[
            pltpu.VMEM((rows, cols), jnp.float32),
            pltpu.SemaphoreType.DMA((chunks,)),
        ],
        flops=1 << 30,
    )
    return (updated, w_rows.T, basis.T)


def solution(mesh):
    return jax.shard_map(
        local,
        mesh=mesh,
        in_specs=(P("row", "col"), P("row", None)),
        out_specs=(P("row", "col"), P("row", None), P("row", None)),
        check_vma=False,
    )
```

```python
import functools

import jax
import jax.numpy as jnp
from jax import lax
from jax.experimental import pallas as pl
from jax.experimental.pallas import tpu as pltpu
from jax.sharding import PartitionSpec as P

HIGH = lax.Precision.HIGHEST
VMEM = pl.BlockSpec(memory_space=pltpu.VMEM)
SMEM = pl.BlockSpec(memory_space=pltpu.SMEM)
HBM = pl.BlockSpec(memory_space=pltpu.HBM)
PARAMS = pltpu.CompilerParams(vmem_limit_bytes=40 * 1024 * 1024)
STRIP = 8


def dot(left, right, contract, precision=HIGH):
    return lax.dot_general(
        left, right, (contract, ((), ())), precision=precision, preferred_element_type=jnp.float32
    )


def dot16(left, right, contract):
    return dot(left, right, contract, lax.Precision.DEFAULT)


def split(value, parts):
    terms = []
    for _ in range(parts):
        terms.append(value.astype(jnp.bfloat16))
        value = value - terms[-1].astype(jnp.float32)
    return terms


def partner(value, axis, step):
    size = lax.axis_size(axis)
    return lax.ppermute(value, axis, [(i, i ^ step) for i in range(size)])


def transpose_grid(value, shift):
    n_row, n_col = lax.axis_size("row"), lax.axis_size("col")
    ratio = n_col // n_row
    pairs = []
    for r in range(n_row):
        for k in range(ratio):
            for q in range(n_row):
                source = q * n_col + ((k + shift) % ratio) * n_row + r
                pairs.append((source, r * n_col + k * n_row + q))
    return lax.ppermute(value, ("row", "col"), pairs)


def copy_rows(source, target, sems, first, pieces):
    size = source.shape[0] // pieces
    copies = []
    for piece in range(pieces):
        span = slice(piece * size, (piece + 1) * size)
        copies.append(
            pltpu.make_async_copy(source.at[span, :], target.at[span, :], sems.at[first + piece])
        )
        copies[-1].start()
    return copies


def product_kernel(
    ratio, which_ref, panel_ref, matrix_ref, out_ref, mine_ref, held_ref, kept_ref, sems
):
    width, rows = panel_ref.shape
    pieces = sems.shape[0] // 2
    panel_copies = copy_rows(panel_ref, held_ref, sems, 0, pieces)
    matrix_copies = copy_rows(matrix_ref, kept_ref, sems, pieces, pieces)
    for copy in panel_copies:
        copy.wait()
    panel = held_ref[...]
    terms = jnp.concatenate(split(panel, 3), axis=0)
    to_strip(dot(panel, panel, ((1,), (1,))), out_ref.at[width:, :])
    which = which_ref[0]
    for j in range(mine_ref.shape[1] // width):
        start = j * ratio * width
        block = panel[:, start : start + width]
        for k in range(1, ratio):
            start += width
            block = jnp.where(which == k, panel[:, start : start + width], block)
        mine_ref[:, j * width : (j + 1) * width] = block
    chunk = rows // pieces
    total = jnp.zeros((width, matrix_ref.shape[1]), jnp.float32)
    for piece in range(pieces):
        matrix_copies[piece].wait()
        span = slice(piece * chunk, (piece + 1) * chunk)
        parts = split(kept_ref[span, :], 3)
        for i, part in enumerate(parts):
            count = 3 - i
            out = dot16(terms[: count * width, span], part, ((1,), (0,)))
            for t in range(count):
                total = total + out[t * width : (t + 1) * width, :]
    out_ref[:width, :] = total


def to_strip(value, strip_ref):
    width = value.shape[0]
    for i in range(width // STRIP):
        strip_ref[:, i * width : (i + 1) * width] = value[i * STRIP : (i + 1) * STRIP, :]


def from_strip(strip, width):
    return jnp.concatenate(
        [strip[:, i * width : (i + 1) * width] for i in range(width // STRIP)], axis=0
    )


def finish_kernel(mine_ref, other_ref, product_ref, gram_ref):
    width = product_ref.shape[0]
    product_ref[...] = mine_ref[:width, :] + other_ref[:width, :]
    gram_ref[...] = from_strip(mine_ref[width:, :] + other_ref[width:, :], width)


def factor_kernel(gram_ref, inverse_ref):
    size = inverse_ref.shape[0]
    batch = 4
    row = lax.broadcasted_iota(jnp.int32, (size, 2 * size), 0)
    lane = lax.broadcasted_iota(jnp.int32, (size, 2 * size), 1)
    eye = jnp.where(row == lane, 1.0, 0.0).astype(jnp.float32)
    table = jnp.concatenate([eye[:, :size], gram_ref[...]], axis=1)
    for first in range(0, size, batch):
        base = first // 8 * 8
        height = size - base
        low = table[base:, :]
        low_row = row[base:, :]
        cols = [
            jnp.broadcast_to(low[:, size + first + t : size + first + t + 1], (height, 2 * size))
            for t in range(batch)
        ]
        rows = [low[first - base + t : first - base + t + 1, :] for t in range(batch)]
        for t in range(batch):
            at = first - base + t
            scale = 1.0 / cols[t][at : at + 1, :]
            factor = jnp.where(low_row > first + t, cols[t] * scale, 0.0)
            for s in range(t + 1, batch):
                cols[s] = cols[s] - factor * cols[s][at : at + 1, :]
                rows[s] = rows[s] - factor[first - base + s : first - base + s + 1, :] * rows[t]
            low = low - factor * rows[t]
        table = low if base == 0 else jnp.concatenate([table[:base, :], low], axis=0)
    diagonal = jnp.sum(jnp.where(lane == row + size, table, 0.0), axis=1, keepdims=True)
    inverse_ref[...] = (table / jnp.sqrt(diagonal))[:, :size]


def stack_left(value):
    high, low = split(value, 2)
    return jnp.concatenate([high, low, high], axis=0)


def stack_right(value):
    high, low = split(value, 2)
    return jnp.concatenate([high, high, low], axis=0)


def basis_kernel(
    matrix_ref, panel_ref, panel_cols_ref, product_cols_ref, inverse_ref,
    begun_ref, basis_ref, kept_ref, cols_ref,
):
    inverse = inverse_ref[...]
    basis = dot(inverse, panel_ref[...], ((1,), (0,)))
    image_cols = dot(inverse, product_cols_ref[...], ((1,), (0,)))
    basis_ref[...] = basis
    kept_ref[...] = basis
    cols_ref[...] = dot(inverse, panel_cols_ref[...], ((1,), (0,)))
    left = stack_left(basis)
    right = stack_right(2.0 * image_cols)
    chunk = 256
    for start in range(0, matrix_ref.shape[0], chunk):
        span = slice(start, start + chunk)
        begun_ref[span, :] = matrix_ref[span, :] - dot16(left[:, span], right, ((0,), (0,)))


def inner_kernel(ratio, which_ref, panel_ref, *refs):
    halves, (rows_ref, inner_ref) = refs[:ratio], refs[ratio:]
    width = inner_ref.shape[0]
    which = which_ref[0]
    parts = []
    for j in range(halves[0].shape[1] // width):
        span = slice(j * width, (j + 1) * width)
        for k in range(ratio):
            block = halves[0][:, span]
            for shift in range(1, ratio):
                block = jnp.where((which + shift) % ratio == k, halves[shift][:, span], block)
            parts.append(block)
    product_rows = jnp.concatenate(parts, axis=1)
    rows_ref[...] = product_rows
    inner_ref[...] = dot(panel_ref[...], product_rows, ((1,), (1,)))


def image_kernel(begun_ref, rows_ref, cols_ref, inverse_ref, further_ref, image_ref):
    image = dot(inverse_ref[...], rows_ref[...], ((1,), (0,)))
    image_ref[...] = image
    left = stack_left(2.0 * image)
    right = stack_right(cols_ref[...])
    chunk = 256
    for start in range(0, begun_ref.shape[0], chunk):
        span = slice(start, start + chunk)
        further_ref[span, :] = begun_ref[span, :] - dot16(left[:, span], right, ((0,), (0,)))


def update_kernel(
    further_ref, image_ref, basis_ref, cols_ref, inverse_ref, inner_ref, other_ref,
    updated_ref, w_ref, buffer_ref, w_buffer_ref, sems,
):
    inverse = inverse_ref[...]
    basis = basis_ref[...]
    inner = inner_ref[...] + other_ref[...]
    correction = dot(dot(inverse, inner, ((1,), (0,))), inverse, ((1,), (1,)))
    right = stack_right(4.0 * dot(correction, cols_ref[...], ((1,), (0,))))
    left = stack_left(basis)
    count = sems.shape[0] - 1
    chunk = further_ref.shape[0] // count
    copies = []
    for i in range(count):
        span = slice(i * chunk, (i + 1) * chunk)
        buffer_ref[span, :] = further_ref[span, :] + dot16(left[:, span], right, ((0,), (0,)))
        copies.append(
            pltpu.make_async_copy(buffer_ref.at[span, :], updated_ref.at[span, :], sems.at[i])
        )
        copies[-1].start()
    w_buffer_ref[...] = 2.0 * (image_ref[...] - dot(correction, basis, ((0,), (0,))))
    copies.append(pltpu.make_async_copy(w_buffer_ref, w_ref, sems.at[count]))
    copies[-1].start()
    for copy in copies:
        copy.wait()


def shape(*dims, dtype=jnp.float32):
    return jax.ShapeDtypeStruct(dims, dtype)


def call(kernel, outs, args, in_specs=None, out_specs=None, scratch=(), flops=0):
    return pl.pallas_call(
        kernel,
        out_shape=outs,
        in_specs=in_specs or [VMEM] * len(args),
        out_specs=out_specs or ((VMEM,) * len(outs) if isinstance(outs, tuple) else VMEM),
        scratch_shapes=scratch,
        compiler_params=PARAMS,
        cost_estimate=pl.CostEstimate(flops=flops, bytes_accessed=1 << 18, transcendentals=0),
    )(*args)


def local(matrix, panel):
    n_row, n_col = lax.axis_size("row"), lax.axis_size("col")
    ratio = n_col // n_row
    rows, width = panel.shape
    cols = matrix.shape[1]
    which = (lax.axis_index("col") // n_row).astype(jnp.int32).reshape(1)
    chunks = 8

    message, mine, panel_t, kept = call(
        functools.partial(product_kernel, ratio),
        (shape(width + STRIP, cols), shape(width, cols), shape(width, rows), shape(rows, cols)),
        (
            which,
            pltpu.with_memory_space_constraint(panel.T, pltpu.HBM),
            pltpu.with_memory_space_constraint(matrix, pltpu.HBM),
        ),
        in_specs=[SMEM, HBM, HBM],
        scratch=[pltpu.SemaphoreType.DMA((2 * chunks,))],
        flops=1 << 30,
    )
    step = 1
    while 2 * step < n_row:
        message = message + partner(message, "row", step)
        step *= 2
    message, mine = lax.optimization_barrier((message, mine))
    last = partner(message, "row", step)
    panel_cols = transpose_grid(mine, 0)
    product_cols, gram = call(
        finish_kernel, (shape(width, cols), shape(width, width)), (message, last), flops=1 << 24
    )
    product_cols, panel_cols = lax.optimization_barrier((product_cols, panel_cols))
    halves = [transpose_grid(product_cols, shift) for shift in range(ratio)]
    inverse = call(factor_kernel, shape(width, width), (gram,), flops=1 << 30)
    begun, basis, basis_kept, basis_cols = call(
        basis_kernel,
        (shape(rows, cols), shape(width, rows), shape(width, rows), shape(width, cols)),
        (kept, panel_t, panel_cols, product_cols, inverse),
        flops=1 << 30,
    )
    product_rows, inner = call(
        functools.partial(inner_kernel, ratio),
        (shape(width, rows), shape(width, width)),
        (which, panel_t, *halves),
        in_specs=[SMEM] + [VMEM] * (1 + ratio),
        flops=1 << 24,
    )
    further, image = call(
        image_kernel,
        (shape(rows, cols), shape(width, rows)),
        (begun, product_rows, basis_cols, inverse),
        flops=1 << 30,
    )
    step = 1
    while 2 * step < n_row:
        inner = inner + partner(inner, "row", step)
        step *= 2
    updated, w_rows = call(
        update_kernel,
        (shape(rows, cols), shape(width, rows)),
        (further, image, basis_kept, basis_cols, inverse, inner, partner(inner, "row", step)),
        out_specs=(HBM, HBM),
        scratch=[
            pltpu.VMEM((rows, cols), jnp.float32),
            pltpu.VMEM((width, rows), jnp.float32),
            pltpu.SemaphoreType.DMA((chunks + 1,)),
        ],
        flops=1 << 30,
    )
    return (updated, w_rows.T, basis.T)


def solution(mesh):
    return jax.shard_map(
        local,
        mesh=mesh,
        in_specs=(P("row", "col"), P("row", None)),
        out_specs=(P("row", "col"), P("row", None), P("row", None)),
        check_vma=False,
    )
```

```python
import functools

import jax
import jax.numpy as jnp
from jax import lax
from jax.experimental import pallas as pl
from jax.experimental.pallas import tpu as pltpu
from jax.sharding import PartitionSpec as P

HIGH = lax.Precision.HIGHEST
VMEM = pl.BlockSpec(memory_space=pltpu.VMEM)
SMEM = pl.BlockSpec(memory_space=pltpu.SMEM)
HBM = pl.BlockSpec(memory_space=pltpu.HBM)
PARAMS = pltpu.CompilerParams(vmem_limit_bytes=40 * 1024 * 1024)
STRIP = 8


def dot(left, right, contract, precision=HIGH):
    return lax.dot_general(
        left, right, (contract, ((), ())), precision=precision, preferred_element_type=jnp.float32
    )


def dot16(left, right, contract):
    return dot(left, right, contract, lax.Precision.DEFAULT)


def split(value, parts):
    terms = []
    for _ in range(parts):
        terms.append(value.astype(jnp.bfloat16))
        value = value - terms[-1].astype(jnp.float32)
    return terms


def partner(value, axis, step):
    size = lax.axis_size(axis)
    return lax.ppermute(value, axis, [(i, i ^ step) for i in range(size)])


def tree_sum(parts):
    while len(parts) > 1:
        parts = [parts[i] + parts[i + 1] for i in range(0, len(parts), 2)]
    return parts[0]


def group_parts(value, axis, low, high):
    parts = [value]
    while low < high:
        value = tree_sum(parts)
        radix = min(4, high // low)
        parts = [value] + [partner(value, axis, i * low) for i in range(1, radix)]
        low *= radix
    return parts


def spread_rows(value):
    n_row, n_col = lax.axis_size("row"), lax.axis_size("col")
    apart = lax.axis_index("row") ^ (lax.axis_index("col") % n_row)
    bit = n_row // 2
    while bit:
        pairs = []
        for c in range(n_col):
            for offset in range(0, n_row, 2 * bit):
                source = (c % n_row) ^ offset
                pairs.append((source * n_col + c, (source ^ bit) * n_col + c))
        received = lax.ppermute(value, ("row", "col"), pairs)
        value = jnp.where(apart & bit != 0, received, value)
        bit //= 2
    return value


def transpose_grid(value):
    n_row, n_col = lax.axis_size("row"), lax.axis_size("col")
    pairs = []
    for r in range(n_row):
        for k in range(n_col // n_row):
            for q in range(n_row):
                source = (q ^ (n_row // 2)) * n_col + k * n_row + r
                pairs.append((source, r * n_col + k * n_row + q))
    return lax.ppermute(value, ("row", "col"), pairs)


def other_half(value, shift):
    n_row, n_col = lax.axis_size("row"), lax.axis_size("col")
    pairs = [((c + shift * n_row) % n_col, c) for c in range(n_col)]
    return lax.ppermute(value, "col", pairs)


def copy_rows(source, target, sems, first, pieces):
    size = source.shape[0] // pieces
    copies = []
    for piece in range(pieces):
        span = slice(piece * size, (piece + 1) * size)
        copies.append(
            pltpu.make_async_copy(source.at[span, :], target.at[span, :], sems.at[first + piece])
        )
        copies[-1].start()
    return copies


def panel_kernel(
    ratio, which_ref, panel_ref, matrix_ref,
    mine_ref, held_ref, terms_ref, gram_ref, kept_ref, sems,
):
    width = panel_ref.shape[0]
    pieces = sems.shape[0] // 2
    panel_copies = copy_rows(panel_ref, held_ref, sems, 0, pieces)
    matrix_copies = copy_rows(matrix_ref, kept_ref, sems, pieces, pieces)
    for copy in panel_copies:
        copy.wait()
    which = which_ref[0]
    for j in range(mine_ref.shape[1] // width):
        start = j * ratio * width
        block = held_ref[:, start : start + width]
        for k in range(1, ratio):
            start += width
            block = jnp.where(which == k, held_ref[:, start : start + width], block)
        mine_ref[:, j * width : (j + 1) * width] = block
    panel = held_ref[...]
    terms_ref[...] = jnp.concatenate(split(panel, 3), axis=0)
    to_strip(dot(panel, panel, ((1,), (1,))), gram_ref)
    for copy in matrix_copies:
        copy.wait()


def product_kernel(terms_ref, matrix_ref, gram_ref, out_ref):
    width = out_ref.shape[0] - STRIP
    rows = matrix_ref.shape[0]
    chunk = 256
    total = jnp.zeros((width, matrix_ref.shape[1]), jnp.float32)
    for start in range(0, rows, chunk):
        span = slice(start, start + chunk)
        parts = split(matrix_ref[span, :], 3)
        for i, part in enumerate(parts):
            count = 3 - i
            out = dot16(terms_ref[: count * width, span], part, ((1,), (0,)))
            for t in range(count):
                total = total + out[t * width : (t + 1) * width, :]
    out_ref[:width, :] = total
    out_ref[width:, :] = gram_ref[...]


def to_strip(value, strip_ref):
    width = value.shape[0]
    for i in range(width // STRIP):
        strip_ref[:, i * width : (i + 1) * width] = value[i * STRIP : (i + 1) * STRIP, :]


def from_strip(strip, width):
    return jnp.concatenate(
        [strip[:, i * width : (i + 1) * width] for i in range(width // STRIP)], axis=0
    )


def finish_kernel(mine_ref, other_ref, panel_cols_ref, product_ref, gram_ref, inner_ref):
    width = product_ref.shape[0]
    product = mine_ref[:width, :] + other_ref[:width, :]
    product_ref[...] = product
    gram_ref[...] = from_strip(mine_ref[width:, :] + other_ref[width:, :], width)
    inner_ref[...] = dot(panel_cols_ref[...], product, ((1,), (1,)))


def pack_kernel(near_ref, *refs):
    parts, sent_ref = refs[:-1], refs[-1]
    width = near_ref.shape[0]
    sent_ref[:width, :] = near_ref[...]
    to_strip(tree_sum([part[...] for part in parts]), sent_ref.at[width:, :])


def factor_kernel(gram_ref, inverse_ref):
    size = inverse_ref.shape[0]
    batch = 4
    row = lax.broadcasted_iota(jnp.int32, (size, 2 * size), 0)
    lane = lax.broadcasted_iota(jnp.int32, (size, 2 * size), 1)
    eye = jnp.where(row == lane, 1.0, 0.0).astype(jnp.float32)
    table = jnp.concatenate([eye[:, :size], gram_ref[...]], axis=1)
    for first in range(0, size, batch):
        base = first // 8 * 8
        height = size - base
        low = table[base:, :]
        low_row = row[base:, :]
        cols = [
            jnp.broadcast_to(low[:, size + first + t : size + first + t + 1], (height, 2 * size))
            for t in range(batch)
        ]
        rows = [low[first - base + t : first - base + t + 1, :] for t in range(batch)]
        for t in range(batch):
            at = first - base + t
            scale = 1.0 / cols[t][at : at + 1, :]
            factor = jnp.where(low_row > first + t, cols[t] * scale, 0.0)
            for s in range(t + 1, batch):
                cols[s] = cols[s] - factor * cols[s][at : at + 1, :]
                rows[s] = rows[s] - factor[first - base + s : first - base + s + 1, :] * rows[t]
            low = low - factor * rows[t]
        table = low if base == 0 else jnp.concatenate([table[:base, :], low], axis=0)
    diagonal = jnp.sum(jnp.where(lane == row + size, table, 0.0), axis=1, keepdims=True)
    inverse_ref[...] = (table / jnp.sqrt(diagonal))[:, :size]


def stack_left(value):
    high, low = split(value, 2)
    return jnp.concatenate([high, low, high], axis=0)


def stack_right(value):
    high, low = split(value, 2)
    return jnp.concatenate([high, high, low], axis=0)


def basis_kernel(
    matrix_ref, panel_ref, panel_cols_ref, product_cols_ref, inverse_ref,
    begun_ref, basis_ref, kept_ref, right_ref,
):
    inverse = inverse_ref[...]
    basis = dot(inverse, panel_ref[...], ((1,), (0,)))
    image_cols = dot(inverse, product_cols_ref[...], ((1,), (0,)))
    basis_ref[...] = basis
    kept_ref[...] = basis
    right_ref[...] = stack_right(dot(inverse, panel_cols_ref[...], ((1,), (0,))))
    left = stack_left(basis)
    right = stack_right(2.0 * image_cols)
    chunk = 256
    for start in range(0, matrix_ref.shape[0], chunk):
        span = slice(start, start + chunk)
        begun_ref[span, :] = matrix_ref[span, :] - dot16(left[:, span], right, ((0,), (0,)))


def update_kernel(
    ratio, which_ref, begun_ref, basis_ref, right_ref, inverse_ref, *refs
):
    halves, (updated_ref, w_ref, buffer_ref, w_buffer_ref, sems) = refs[:ratio], refs[ratio:]
    inverse = inverse_ref[...]
    width = inverse.shape[0]
    strip = halves[0][width:, :]
    for half in halves[1:]:
        strip = strip + half[width:, :]
    correction = dot(
        dot(inverse, from_strip(strip, width), ((1,), (0,))), inverse, ((1,), (1,))
    )
    removed = dot(correction, basis_ref[...], ((0,), (0,)))
    which = which_ref[0]
    parts = []
    for j in range(halves[0].shape[1] // width):
        span = slice(j * width, (j + 1) * width)
        for k in range(ratio):
            block = halves[0][:width, span]
            for shift in range(1, ratio):
                block = jnp.where(
                    (which + shift) % ratio == k, halves[shift][:width, span], block
                )
            parts.append(block)
    image = dot(inverse, jnp.concatenate(parts, axis=1), ((1,), (0,)))
    left = stack_left(2.0 * image - 4.0 * removed)
    right = right_ref[...]
    count = sems.shape[0] - 1
    chunk = begun_ref.shape[0] // count
    w_buffer_ref[...] = 2.0 * (image - removed)
    copies = [pltpu.make_async_copy(w_buffer_ref, w_ref, sems.at[count])]
    copies[-1].start()
    for i in range(count):
        span = slice(i * chunk, (i + 1) * chunk)
        buffer_ref[span, :] = begun_ref[span, :] - dot16(left[:, span], right, ((0,), (0,)))
        copies.append(
            pltpu.make_async_copy(buffer_ref.at[span, :], updated_ref.at[span, :], sems.at[i])
        )
        copies[-1].start()
    for copy in copies:
        copy.wait()


def shape(*dims, dtype=jnp.float32):
    return jax.ShapeDtypeStruct(dims, dtype)


def call(kernel, outs, args, in_specs=None, out_specs=None, scratch=(), flops=0):
    return pl.pallas_call(
        kernel,
        out_shape=outs,
        in_specs=in_specs or [VMEM] * len(args),
        out_specs=out_specs or ((VMEM,) * len(outs) if isinstance(outs, tuple) else VMEM),
        scratch_shapes=scratch,
        compiler_params=PARAMS,
        cost_estimate=pl.CostEstimate(flops=flops, bytes_accessed=1 << 18, transcendentals=0),
    )(*args)


def local(matrix, panel):
    n_row, n_col = lax.axis_size("row"), lax.axis_size("col")
    ratio = n_col // n_row
    rows, width = panel.shape
    cols = matrix.shape[1]
    which = (lax.axis_index("col") // n_row).astype(jnp.int32).reshape(1)
    chunks = 8

    mine, panel_t, terms, gram, kept = call(
        functools.partial(panel_kernel, ratio),
        (
            shape(width, cols),
            shape(width, rows),
            shape(3 * width, rows, dtype=jnp.bfloat16),
            shape(STRIP, cols),
            shape(rows, cols),
        ),
        (
            which,
            pltpu.with_memory_space_constraint(panel.T, pltpu.HBM),
            pltpu.with_memory_space_constraint(matrix, pltpu.HBM),
        ),
        in_specs=[SMEM, HBM, HBM],
        scratch=[pltpu.SemaphoreType.DMA((2 * chunks,))],
        flops=1 << 28,
    )
    panel_cols = spread_rows(mine)
    message = call(
        product_kernel, shape(width + STRIP, cols), (terms, kept, gram), flops=1 << 30
    )
    step = 1
    while 2 * step < n_row:
        message = message + partner(message, "row", step)
        step *= 2
    last = partner(message, "row", step)
    product_cols, gram, inner = call(
        finish_kernel,
        (shape(width, cols), shape(width, width), shape(width, width)),
        (message, last, panel_cols),
        flops=1 << 24,
    )
    near = transpose_grid(product_cols)
    parts = group_parts(inner, "col", 1, n_row)
    sent = call(pack_kernel, shape(width + STRIP, cols), (near, *parts), flops=1 << 18)
    halves = [sent] + [other_half(sent, shift) for shift in range(1, ratio)]
    inverse = call(factor_kernel, shape(width, width), (gram,), flops=1 << 30)
    begun, basis, basis_kept, right = call(
        basis_kernel,
        (
            shape(rows, cols),
            shape(width, rows),
            shape(width, rows),
            shape(3 * width, cols, dtype=jnp.bfloat16),
        ),
        (kept, panel_t, panel_cols, product_cols, inverse),
        flops=1 << 30,
    )
    updated, w_rows = call(
        functools.partial(update_kernel, ratio),
        (shape(rows, cols), shape(width, rows)),
        (which, begun, basis_kept, right, inverse, *halves),
        in_specs=[SMEM] + [VMEM] * (4 + ratio),
        out_specs=(HBM, HBM),
        scratch=[
            pltpu.VMEM((rows, cols), jnp.float32),
            pltpu.VMEM((width, rows), jnp.float32),
            pltpu.SemaphoreType.DMA((chunks + 1,)),
        ],
        flops=1 << 30,
    )
    return (updated, w_rows.T, basis.T)


def solution(mesh):
    return jax.shard_map(
        local,
        mesh=mesh,
        in_specs=(P("row", "col"), P("row", None)),
        out_specs=(P("row", "col"), P("row", None), P("row", None)),
        check_vma=False,
    )
```

```python
import functools

import jax
import jax.numpy as jnp
from jax import lax
from jax.experimental import pallas as pl
from jax.experimental.pallas import tpu as pltpu
from jax.sharding import PartitionSpec as P

HIGH = lax.Precision.HIGHEST
VMEM = pl.BlockSpec(memory_space=pltpu.VMEM)
SMEM = pl.BlockSpec(memory_space=pltpu.SMEM)
HBM = pl.BlockSpec(memory_space=pltpu.HBM)
PARAMS = pltpu.CompilerParams(vmem_limit_bytes=40 * 1024 * 1024)
STRIP = 8


def dot(left, right, contract, precision=HIGH):
    return lax.dot_general(
        left, right, (contract, ((), ())), precision=precision, preferred_element_type=jnp.float32
    )


def dot16(left, right, contract):
    return dot(left, right, contract, lax.Precision.DEFAULT)


def split(value, parts):
    terms = []
    for _ in range(parts):
        terms.append(value.astype(jnp.bfloat16))
        value = value - terms[-1].astype(jnp.float32)
    return terms


def partner(value, axis, step):
    size = lax.axis_size(axis)
    return lax.ppermute(value, axis, [(i, i ^ step) for i in range(size)])


def spread_rows(value):
    n_row, n_col = lax.axis_size("row"), lax.axis_size("col")
    apart = lax.axis_index("row") ^ (lax.axis_index("col") % n_row)
    bit = n_row // 2
    while bit:
        pairs = []
        for c in range(n_col):
            for offset in range(0, n_row, 2 * bit):
                source = (c % n_row) ^ offset
                pairs.append((source * n_col + c, (source ^ bit) * n_col + c))
        received = lax.ppermute(value, ("row", "col"), pairs)
        value = jnp.where(apart & bit != 0, received, value)
        bit //= 2
    return value


def transpose_grid(value):
    n_row, n_col = lax.axis_size("row"), lax.axis_size("col")
    pairs = []
    for r in range(n_row):
        for k in range(n_col // n_row):
            for q in range(n_row):
                source = (q ^ (n_row // 2)) * n_col + k * n_row + r
                pairs.append((source, r * n_col + k * n_row + q))
    return lax.ppermute(value, ("row", "col"), pairs)


def other_half(value, shift):
    n_row, n_col = lax.axis_size("row"), lax.axis_size("col")
    pairs = [((c + shift * n_row) % n_col, c) for c in range(n_col)]
    return lax.ppermute(value, "col", pairs)


def copy_rows(source, target, sems, first, pieces):
    size = source.shape[0] // pieces
    copies = []
    for piece in range(pieces):
        span = slice(piece * size, (piece + 1) * size)
        copies.append(
            pltpu.make_async_copy(source.at[span, :], target.at[span, :], sems.at[first + piece])
        )
        copies[-1].start()
    return copies


def panel_kernel(
    ratio, which_ref, panel_ref, matrix_ref,
    mine_ref, held_ref, terms_ref, gram_ref, kept_ref, sems,
):
    width = panel_ref.shape[0]
    pieces = sems.shape[0] // 2
    panel_copies = copy_rows(panel_ref, held_ref, sems, 0, pieces)
    matrix_copies = copy_rows(matrix_ref, kept_ref, sems, pieces, pieces)
    for copy in panel_copies:
        copy.wait()
    which = which_ref[0]
    for j in range(mine_ref.shape[1] // width):
        start = j * ratio * width
        block = held_ref[:, start : start + width]
        for k in range(1, ratio):
            start += width
            block = jnp.where(which == k, held_ref[:, start : start + width], block)
        mine_ref[:, j * width : (j + 1) * width] = block
    panel = held_ref[...]
    terms_ref[...] = jnp.concatenate(split(panel, 3), axis=0)
    to_strip(dot(panel, panel, ((1,), (1,))), gram_ref)
    for copy in matrix_copies:
        copy.wait()


def product_kernel(terms_ref, matrix_ref, gram_ref, out_ref):
    width = out_ref.shape[0] - STRIP
    rows = matrix_ref.shape[0]
    chunk = 256
    total = jnp.zeros((width, matrix_ref.shape[1]), jnp.float32)
    for start in range(0, rows, chunk):
        span = slice(start, start + chunk)
        parts = split(matrix_ref[span, :], 3)
        for i, part in enumerate(parts):
            count = 3 - i
            out = dot16(terms_ref[: count * width, span], part, ((1,), (0,)))
            for t in range(count):
                total = total + out[t * width : (t + 1) * width, :]
    out_ref[:width, :] = total
    out_ref[width:, :] = gram_ref[...]


def to_strip(value, strip_ref):
    width = value.shape[0]
    for i in range(width // STRIP):
        strip_ref[:, i * width : (i + 1) * width] = value[i * STRIP : (i + 1) * STRIP, :]


def from_strip(strip, width):
    return jnp.concatenate(
        [strip[:, i * width : (i + 1) * width] for i in range(width // STRIP)], axis=0
    )


def finish_kernel(mine_ref, other_ref, product_ref, gram_ref):
    width = product_ref.shape[0]
    product_ref[...] = mine_ref[:width, :] + other_ref[:width, :]
    gram_ref[...] = from_strip(mine_ref[width:, :] + other_ref[width:, :], width)


def factor_kernel(gram_ref, inverse_ref):
    size = inverse_ref.shape[0]
    batch = 4
    row = lax.broadcasted_iota(jnp.int32, (size, 2 * size), 0)
    lane = lax.broadcasted_iota(jnp.int32, (size, 2 * size), 1)
    eye = jnp.where(row == lane, 1.0, 0.0).astype(jnp.float32)
    table = jnp.concatenate([eye[:, :size], gram_ref[...]], axis=1)
    for first in range(0, size, batch):
        base = first // 8 * 8
        height = size - base
        low = table[base:, :]
        low_row = row[base:, :]
        cols = [
            jnp.broadcast_to(low[:, size + first + t : size + first + t + 1], (height, 2 * size))
            for t in range(batch)
        ]
        rows = [low[first - base + t : first - base + t + 1, :] for t in range(batch)]
        for t in range(batch):
            at = first - base + t
            scale = 1.0 / cols[t][at : at + 1, :]
            factor = jnp.where(low_row > first + t, cols[t] * scale, 0.0)
            for s in range(t + 1, batch):
                cols[s] = cols[s] - factor * cols[s][at : at + 1, :]
                rows[s] = rows[s] - factor[first - base + s : first - base + s + 1, :] * rows[t]
            low = low - factor * rows[t]
        table = low if base == 0 else jnp.concatenate([table[:base, :], low], axis=0)
    diagonal = jnp.sum(jnp.where(lane == row + size, table, 0.0), axis=1, keepdims=True)
    inverse_ref[...] = (table / jnp.sqrt(diagonal))[:, :size]


def stack_left(value):
    high, low = split(value, 2)
    return jnp.concatenate([high, low, high], axis=0)


def stack_right(value):
    high, low = split(value, 2)
    return jnp.concatenate([high, high, low], axis=0)


def basis_kernel(
    matrix_ref, panel_ref, panel_cols_ref, product_cols_ref, inverse_ref,
    begun_ref, basis_ref, kept_ref, cols_ref,
):
    inverse = inverse_ref[...]
    basis = dot(inverse, panel_ref[...], ((1,), (0,)))
    image_cols = dot(inverse, product_cols_ref[...], ((1,), (0,)))
    basis_ref[...] = basis
    kept_ref[...] = basis
    cols_ref[...] = dot(inverse, panel_cols_ref[...], ((1,), (0,)))
    left = stack_left(basis)
    right = stack_right(2.0 * image_cols)
    chunk = 256
    for start in range(0, matrix_ref.shape[0], chunk):
        span = slice(start, start + chunk)
        begun_ref[span, :] = matrix_ref[span, :] - dot16(left[:, span], right, ((0,), (0,)))


def inner_kernel(ratio, which_ref, panel_ref, *refs):
    halves, (rows_ref, inner_ref) = refs[:ratio], refs[ratio:]
    width = inner_ref.shape[0]
    which = which_ref[0]
    parts = []
    for j in range(halves[0].shape[1] // width):
        span = slice(j * width, (j + 1) * width)
        for k in range(ratio):
            block = halves[0][:, span]
            for shift in range(1, ratio):
                block = jnp.where((which + shift) % ratio == k, halves[shift][:, span], block)
            parts.append(block)
    product_rows = jnp.concatenate(parts, axis=1)
    rows_ref[...] = product_rows
    inner_ref[...] = dot(panel_ref[...], product_rows, ((1,), (1,)))


def image_kernel(begun_ref, rows_ref, cols_ref, inverse_ref, further_ref, image_ref):
    image = dot(inverse_ref[...], rows_ref[...], ((1,), (0,)))
    image_ref[...] = image
    left = stack_left(2.0 * image)
    right = stack_right(cols_ref[...])
    chunk = 256
    for start in range(0, begun_ref.shape[0], chunk):
        span = slice(start, start + chunk)
        further_ref[span, :] = begun_ref[span, :] - dot16(left[:, span], right, ((0,), (0,)))


def update_kernel(
    further_ref, image_ref, basis_ref, cols_ref, inverse_ref, inner_ref, other_ref,
    updated_ref, w_ref, buffer_ref, w_buffer_ref, sems,
):
    inverse = inverse_ref[...]
    basis = basis_ref[...]
    inner = inner_ref[...] + other_ref[...]
    correction = dot(dot(inverse, inner, ((1,), (0,))), inverse, ((1,), (1,)))
    right = stack_right(4.0 * dot(correction, cols_ref[...], ((1,), (0,))))
    left = stack_left(basis)
    count = sems.shape[0] - 1
    chunk = further_ref.shape[0] // count
    copies = []
    for i in range(count):
        span = slice(i * chunk, (i + 1) * chunk)
        buffer_ref[span, :] = further_ref[span, :] + dot16(left[:, span], right, ((0,), (0,)))
        copies.append(
            pltpu.make_async_copy(buffer_ref.at[span, :], updated_ref.at[span, :], sems.at[i])
        )
        copies[-1].start()
    w_buffer_ref[...] = 2.0 * (image_ref[...] - dot(correction, basis, ((0,), (0,))))
    copies.append(pltpu.make_async_copy(w_buffer_ref, w_ref, sems.at[count]))
    copies[-1].start()
    for copy in copies:
        copy.wait()


def shape(*dims, dtype=jnp.float32):
    return jax.ShapeDtypeStruct(dims, dtype)


def call(kernel, outs, args, in_specs=None, out_specs=None, scratch=(), flops=0):
    return pl.pallas_call(
        kernel,
        out_shape=outs,
        in_specs=in_specs or [VMEM] * len(args),
        out_specs=out_specs or ((VMEM,) * len(outs) if isinstance(outs, tuple) else VMEM),
        scratch_shapes=scratch,
        compiler_params=PARAMS,
        cost_estimate=pl.CostEstimate(flops=flops, bytes_accessed=1 << 18, transcendentals=0),
    )(*args)


def local(matrix, panel):
    n_row, n_col = lax.axis_size("row"), lax.axis_size("col")
    ratio = n_col // n_row
    rows, width = panel.shape
    cols = matrix.shape[1]
    which = (lax.axis_index("col") // n_row).astype(jnp.int32).reshape(1)
    chunks = 8

    mine, panel_t, terms, gram, kept = call(
        functools.partial(panel_kernel, ratio),
        (
            shape(width, cols),
            shape(width, rows),
            shape(3 * width, rows, dtype=jnp.bfloat16),
            shape(STRIP, cols),
            shape(rows, cols),
        ),
        (
            which,
            pltpu.with_memory_space_constraint(panel.T, pltpu.HBM),
            pltpu.with_memory_space_constraint(matrix, pltpu.HBM),
        ),
        in_specs=[SMEM, HBM, HBM],
        scratch=[pltpu.SemaphoreType.DMA((2 * chunks,))],
        flops=1 << 28,
    )
    message = call(
        product_kernel, shape(width + STRIP, cols), (terms, kept, gram), flops=1 << 30
    )
    step = 1
    while 2 * step < n_row:
        message = message + partner(message, "row", step)
        step *= 2
    message, mine = lax.optimization_barrier((message, mine))
    last = partner(message, "row", step)
    panel_cols = spread_rows(mine)
    product_cols, gram = call(
        finish_kernel, (shape(width, cols), shape(width, width)), (message, last), flops=1 << 24
    )
    near = transpose_grid(product_cols)
    inverse = call(factor_kernel, shape(width, width), (gram,), flops=1 << 30)
    near, inverse = lax.optimization_barrier((near, inverse))
    halves = [near] + [other_half(near, shift) for shift in range(1, ratio)]
    begun, basis, basis_kept, basis_cols = call(
        basis_kernel,
        (shape(rows, cols), shape(width, rows), shape(width, rows), shape(width, cols)),
        (kept, panel_t, panel_cols, product_cols, inverse),
        flops=1 << 30,
    )
    halves, begun = lax.optimization_barrier((halves, begun))
    product_rows, inner = call(
        functools.partial(inner_kernel, ratio),
        (shape(width, rows), shape(width, width)),
        (which, panel_t, *halves),
        in_specs=[SMEM] + [VMEM] * (1 + ratio),
        flops=1 << 24,
    )
    further, image = call(
        image_kernel,
        (shape(rows, cols), shape(width, rows)),
        (begun, product_rows, basis_cols, inverse),
        flops=1 << 30,
    )
    step = 1
    while 2 * step < n_row:
        inner = inner + partner(inner, "row", step)
        step *= 2
    updated, w_rows = call(
        update_kernel,
        (shape(rows, cols), shape(width, rows)),
        (further, image, basis_kept, basis_cols, inverse, inner, partner(inner, "row", step)),
        out_specs=(HBM, HBM),
        scratch=[
            pltpu.VMEM((rows, cols), jnp.float32),
            pltpu.VMEM((width, rows), jnp.float32),
            pltpu.SemaphoreType.DMA((chunks + 1,)),
        ],
        flops=1 << 30,
    )
    return (updated, w_rows.T, basis.T)


def solution(mesh):
    return jax.shard_map(
        local,
        mesh=mesh,
        in_specs=(P("row", "col"), P("row", None)),
        out_specs=(P("row", "col"), P("row", None), P("row", None)),
        check_vma=False,
    )
```

```python
import functools

import jax
import jax.numpy as jnp
from jax import lax
from jax.experimental import pallas as pl
from jax.experimental.pallas import tpu as pltpu
from jax.sharding import PartitionSpec as P

HIGH = lax.Precision.HIGHEST
VMEM = pl.BlockSpec(memory_space=pltpu.VMEM)
SMEM = pl.BlockSpec(memory_space=pltpu.SMEM)
HBM = pl.BlockSpec(memory_space=pltpu.HBM)
PARAMS = pltpu.CompilerParams(vmem_limit_bytes=40 * 1024 * 1024)
STRIP = 8


def dot(left, right, contract, precision=HIGH):
    return lax.dot_general(
        left, right, (contract, ((), ())), precision=precision, preferred_element_type=jnp.float32
    )


def dot16(left, right, contract):
    return dot(left, right, contract, lax.Precision.DEFAULT)


def split(value, parts):
    terms = []
    for _ in range(parts):
        terms.append(value.astype(jnp.bfloat16))
        value = value - terms[-1].astype(jnp.float32)
    return terms


def partner(value, axis, step):
    size = lax.axis_size(axis)
    return lax.ppermute(value, axis, [(i, i ^ step) for i in range(size)])


def tree_sum(parts):
    while len(parts) > 1:
        parts = [parts[i] + parts[i + 1] for i in range(0, len(parts), 2)]
    return parts[0]


def group_parts(value, axis, low, high):
    parts = [value]
    while low < high:
        value = tree_sum(parts)
        radix = min(4, high // low)
        parts = [value] + [partner(value, axis, i * low) for i in range(1, radix)]
        low *= radix
    return parts


def spread_rows(value):
    n_row, n_col = lax.axis_size("row"), lax.axis_size("col")
    apart = lax.axis_index("row") ^ (lax.axis_index("col") % n_row)
    bit = n_row // 2
    while bit:
        pairs = []
        for c in range(n_col):
            for offset in range(0, n_row, 2 * bit):
                source = (c % n_row) ^ offset
                pairs.append((source * n_col + c, (source ^ bit) * n_col + c))
        received = lax.ppermute(value, ("row", "col"), pairs)
        if bit == 1:
            return value, received, (apart & 1).astype(jnp.int32).reshape(1)
        value = jnp.where(apart & bit != 0, received, value)
        bit //= 2


def transpose_grid(value):
    n_row, n_col = lax.axis_size("row"), lax.axis_size("col")
    pairs = []
    for r in range(n_row):
        for k in range(n_col // n_row):
            for q in range(n_row):
                source = (q ^ (n_row // 2)) * n_col + k * n_row + r
                pairs.append((source, r * n_col + k * n_row + q))
    return lax.ppermute(value, ("row", "col"), pairs)


def other_half(value, shift):
    n_row, n_col = lax.axis_size("row"), lax.axis_size("col")
    pairs = [((c + shift * n_row) % n_col, c) for c in range(n_col)]
    return lax.ppermute(value, "col", pairs)


def copy_rows(source, target, sems, first, pieces):
    size = source.shape[0] // pieces
    copies = []
    for piece in range(pieces):
        span = slice(piece * size, (piece + 1) * size)
        copies.append(
            pltpu.make_async_copy(source.at[span, :], target.at[span, :], sems.at[first + piece])
        )
        copies[-1].start()
    return copies


def product_kernel(
    ratio, which_ref, panel_ref, matrix_ref, out_ref, mine_ref, held_ref, kept_ref, sems
):
    width, rows = panel_ref.shape
    pieces = sems.shape[0] // 2
    panel_copies = copy_rows(panel_ref, held_ref, sems, 0, pieces)
    matrix_copies = copy_rows(matrix_ref, kept_ref, sems, pieces, pieces)
    for copy in panel_copies:
        copy.wait()
    panel = held_ref[...]
    to_strip(dot(panel, panel, ((1,), (1,))), out_ref.at[width:, :])
    which = which_ref[0]
    for j in range(mine_ref.shape[1] // width):
        start = j * ratio * width
        block = held_ref[:, start : start + width]
        for k in range(1, ratio):
            start += width
            block = jnp.where(which == k, held_ref[:, start : start + width], block)
        mine_ref[:, j * width : (j + 1) * width] = block
    chunk = rows // pieces
    total = jnp.zeros((width, matrix_ref.shape[1]), jnp.float32)
    for piece in range(pieces):
        matrix_copies[piece].wait()
        span = slice(piece * chunk, (piece + 1) * chunk)
        terms = jnp.concatenate(split(held_ref[:, span], 3), axis=0)
        for i, part in enumerate(split(kept_ref[span, :], 3)):
            count = 3 - i
            out = dot16(terms[: count * width, :], part, ((1,), (0,)))
            for t in range(count):
                total = total + out[t * width : (t + 1) * width, :]
    out_ref[:width, :] = total


def to_strip(value, strip_ref):
    width = value.shape[0]
    for i in range(width // STRIP):
        strip_ref[:, i * width : (i + 1) * width] = value[i * STRIP : (i + 1) * STRIP, :]


def from_strip(strip, width):
    return jnp.concatenate(
        [strip[:, i * width : (i + 1) * width] for i in range(width // STRIP)], axis=0
    )


def finish_kernel(
    other_ref, received_ref, mine_ref, held_ref, takes_ref,
    product_ref, gram_ref, inner_ref, panel_cols_ref,
):
    width = product_ref.shape[0]
    product = mine_ref[:width, :] + other_ref[:width, :]
    product_ref[...] = product
    gram_ref[...] = from_strip(mine_ref[width:, :] + other_ref[width:, :], width)
    panel_cols = jnp.where(takes_ref[0] != 0, received_ref[...], held_ref[...])
    panel_cols_ref[...] = panel_cols
    inner_ref[...] = dot(panel_cols, product, ((1,), (1,)))


def pack_kernel(near_ref, *refs):
    parts, sent_ref = refs[:-1], refs[-1]
    width = near_ref.shape[0]
    sent_ref[:width, :] = near_ref[...]
    to_strip(tree_sum([part[...] for part in parts]), sent_ref.at[width:, :])


def factor_kernel(gram_ref, inverse_ref):
    size = inverse_ref.shape[0]
    batch = 4
    row = lax.broadcasted_iota(jnp.int32, (size, 2 * size), 0)
    lane = lax.broadcasted_iota(jnp.int32, (size, 2 * size), 1)
    eye = jnp.where(row == lane, 1.0, 0.0).astype(jnp.float32)
    table = jnp.concatenate([eye[:, :size], gram_ref[...]], axis=1)
    for first in range(0, size, batch):
        base = first // 8 * 8
        height = size - base
        low = table[base:, :]
        low_row = row[base:, :]
        cols = [
            jnp.broadcast_to(low[:, size + first + t : size + first + t + 1], (height, 2 * size))
            for t in range(batch)
        ]
        rows = [low[first - base + t : first - base + t + 1, :] for t in range(batch)]
        for t in range(batch):
            at = first - base + t
            scale = 1.0 / cols[t][at : at + 1, :]
            factor = jnp.where(low_row > first + t, cols[t] * scale, 0.0)
            for s in range(t + 1, batch):
                cols[s] = cols[s] - factor * cols[s][at : at + 1, :]
                rows[s] = rows[s] - factor[first - base + s : first - base + s + 1, :] * rows[t]
            low = low - factor * rows[t]
        table = low if base == 0 else jnp.concatenate([table[:base, :], low], axis=0)
    diagonal = jnp.sum(jnp.where(lane == row + size, table, 0.0), axis=1, keepdims=True)
    inverse_ref[...] = (table / jnp.sqrt(diagonal))[:, :size]


def stack_left(value):
    high, low = split(value, 2)
    return jnp.concatenate([high, low, high], axis=0)


def stack_right(value):
    high, low = split(value, 2)
    return jnp.concatenate([high, high, low], axis=0)


def basis_kernel(
    matrix_ref, panel_ref, panel_cols_ref, product_cols_ref, inverse_ref,
    begun_ref, basis_ref, kept_ref, right_ref,
):
    inverse = inverse_ref[...]
    basis = dot(inverse, panel_ref[...], ((1,), (0,)))
    image_cols = dot(inverse, product_cols_ref[...], ((1,), (0,)))
    basis_ref[...] = basis
    kept_ref[...] = basis
    right_ref[...] = stack_right(dot(inverse, panel_cols_ref[...], ((1,), (0,))))
    left = stack_left(basis)
    right = stack_right(2.0 * image_cols)
    chunk = 256
    for start in range(0, matrix_ref.shape[0], chunk):
        span = slice(start, start + chunk)
        begun_ref[span, :] = matrix_ref[span, :] - dot16(left[:, span], right, ((0,), (0,)))


def update_kernel(
    ratio, which_ref, begun_ref, basis_ref, right_ref, inverse_ref, *refs
):
    halves, (updated_ref, w_ref, buffer_ref, w_buffer_ref, sems) = refs[:ratio], refs[ratio:]
    inverse = inverse_ref[...]
    width = inverse.shape[0]
    strip = halves[0][width:, :]
    for half in halves[1:]:
        strip = strip + half[width:, :]
    correction = dot(
        dot(inverse, from_strip(strip, width), ((1,), (0,))), inverse, ((1,), (1,))
    )
    removed = dot(correction, basis_ref[...], ((0,), (0,)))
    which = which_ref[0]
    parts = []
    for j in range(halves[0].shape[1] // width):
        span = slice(j * width, (j + 1) * width)
        for k in range(ratio):
            block = halves[0][:width, span]
            for shift in range(1, ratio):
                block = jnp.where(
                    (which + shift) % ratio == k, halves[shift][:width, span], block
                )
            parts.append(block)
    image = dot(inverse, jnp.concatenate(parts, axis=1), ((1,), (0,)))
    left = stack_left(2.0 * image - 4.0 * removed)
    right = right_ref[...]
    count = sems.shape[0] - 1
    chunk = begun_ref.shape[0] // count
    w_buffer_ref[...] = 2.0 * (image - removed)
    copies = [pltpu.make_async_copy(w_buffer_ref, w_ref, sems.at[count])]
    copies[-1].start()
    for i in range(count):
        span = slice(i * chunk, (i + 1) * chunk)
        buffer_ref[span, :] = begun_ref[span, :] - dot16(left[:, span], right, ((0,), (0,)))
        copies.append(
            pltpu.make_async_copy(buffer_ref.at[span, :], updated_ref.at[span, :], sems.at[i])
        )
        copies[-1].start()
    for copy in copies:
        copy.wait()


def shape(*dims, dtype=jnp.float32):
    return jax.ShapeDtypeStruct(dims, dtype)


def call(kernel, outs, args, in_specs=None, out_specs=None, scratch=(), flops=0):
    return pl.pallas_call(
        kernel,
        out_shape=outs,
        in_specs=in_specs or [VMEM] * len(args),
        out_specs=out_specs or ((VMEM,) * len(outs) if isinstance(outs, tuple) else VMEM),
        scratch_shapes=scratch,
        compiler_params=PARAMS,
        cost_estimate=pl.CostEstimate(flops=flops, bytes_accessed=1 << 18, transcendentals=0),
    )(*args)


def local(matrix, panel):
    n_row, n_col = lax.axis_size("row"), lax.axis_size("col")
    ratio = n_col // n_row
    rows, width = panel.shape
    cols = matrix.shape[1]
    which = (lax.axis_index("col") // n_row).astype(jnp.int32).reshape(1)
    chunks = 8

    message, mine, panel_t, kept = call(
        functools.partial(product_kernel, ratio),
        (shape(width + STRIP, cols), shape(width, cols), shape(width, rows), shape(rows, cols)),
        (
            which,
            pltpu.with_memory_space_constraint(panel.T, pltpu.HBM),
            pltpu.with_memory_space_constraint(matrix, pltpu.HBM),
        ),
        in_specs=[SMEM, HBM, HBM],
        scratch=[pltpu.SemaphoreType.DMA((8,))],
        flops=1 << 30,
    )
    held, received, takes = spread_rows(mine)
    step = 1
    while 2 * step < n_row:
        message = message + partner(message, "row", step)
        step *= 2
    last = partner(message, "row", step)
    product_cols, gram, inner, panel_cols = call(
        finish_kernel,
        (shape(width, cols), shape(width, width), shape(width, width), shape(width, cols)),
        (last, received, message, held, takes),
        in_specs=[VMEM] * 4 + [SMEM],
        flops=1 << 24,
    )
    near = transpose_grid(product_cols)
    parts = group_parts(inner, "col", 1, n_row)
    sent = call(pack_kernel, shape(width + STRIP, cols), (near, *parts), flops=1 << 18)
    halves = [sent] + [other_half(sent, shift) for shift in range(1, ratio)]
    inverse = call(factor_kernel, shape(width, width), (gram,), flops=1 << 30)
    begun, basis, basis_kept, right = call(
        basis_kernel,
        (
            shape(rows, cols),
            shape(width, rows),
            shape(width, rows),
            shape(3 * width, cols, dtype=jnp.bfloat16),
        ),
        (kept, panel_t, panel_cols, product_cols, inverse),
        flops=1 << 30,
    )
    updated, w_rows = call(
        functools.partial(update_kernel, ratio),
        (shape(rows, cols), shape(width, rows)),
        (which, begun, basis_kept, right, inverse, *halves),
        in_specs=[SMEM] + [VMEM] * (4 + ratio),
        out_specs=(HBM, HBM),
        scratch=[
            pltpu.VMEM((rows, cols), jnp.float32),
            pltpu.VMEM((width, rows), jnp.float32),
            pltpu.SemaphoreType.DMA((chunks + 1,)),
        ],
        flops=1 << 30,
    )
    return (updated, w_rows.T, basis.T)


def solution(mesh):
    return jax.shard_map(
        local,
        mesh=mesh,
        in_specs=(P("row", "col"), P("row", None)),
        out_specs=(P("row", "col"), P("row", None), P("row", None)),
        check_vma=False,
    )
```

```python
import functools

import jax
import jax.numpy as jnp
from jax import lax
from jax.experimental import pallas as pl
from jax.experimental.pallas import tpu as pltpu
from jax.sharding import PartitionSpec as P

HIGH = lax.Precision.HIGHEST
VMEM = pl.BlockSpec(memory_space=pltpu.VMEM)
SMEM = pl.BlockSpec(memory_space=pltpu.SMEM)
HBM = pl.BlockSpec(memory_space=pltpu.HBM)
PARAMS = pltpu.CompilerParams(vmem_limit_bytes=40 * 1024 * 1024)
STRIP = 8


def dot(left, right, contract, precision=HIGH):
    return lax.dot_general(
        left, right, (contract, ((), ())), precision=precision, preferred_element_type=jnp.float32
    )


def dot16(left, right, contract):
    return dot(left, right, contract, lax.Precision.DEFAULT)


def split(value, parts):
    terms = []
    for _ in range(parts):
        terms.append(value.astype(jnp.bfloat16))
        value = value - terms[-1].astype(jnp.float32)
    return terms


def partner(value, axis, step):
    size = lax.axis_size(axis)
    return lax.ppermute(value, axis, [(i, i ^ step) for i in range(size)])


def spread_hop(value, bit):
    n_row, n_col = lax.axis_size("row"), lax.axis_size("col")
    pairs = []
    for c in range(n_col):
        for offset in range(0, n_row, 2 * bit):
            source = (c % n_row) ^ offset
            pairs.append((source * n_col + c, (source ^ bit) * n_col + c))
    return lax.ppermute(value, ("row", "col"), pairs)


def transpose_grid(value):
    n_row, n_col = lax.axis_size("row"), lax.axis_size("col")
    pairs = []
    for r in range(n_row):
        for k in range(n_col // n_row):
            for q in range(n_row):
                source = (q ^ (n_row // 2)) * n_col + k * n_row + r
                pairs.append((source, r * n_col + k * n_row + q))
    return lax.ppermute(value, ("row", "col"), pairs)


def other_half(value, shift):
    n_row, n_col = lax.axis_size("row"), lax.axis_size("col")
    pairs = [((c + shift * n_row) % n_col, c) for c in range(n_col)]
    return lax.ppermute(value, "col", pairs)


def copy_rows(source, target, sems, first, pieces):
    size = source.shape[0] // pieces
    copies = []
    for piece in range(pieces):
        span = slice(piece * size, (piece + 1) * size)
        copies.append(
            pltpu.make_async_copy(source.at[span, :], target.at[span, :], sems.at[first + piece])
        )
        copies[-1].start()
    return copies


def product_kernel(
    ratio, which_ref, panel_ref, matrix_ref, out_ref, mine_ref, held_ref, kept_ref, sems
):
    width, rows = panel_ref.shape
    pieces = sems.shape[0] // 2
    panel_copies = copy_rows(panel_ref, held_ref, sems, 0, pieces)
    matrix_copies = copy_rows(matrix_ref, kept_ref, sems, pieces, pieces)
    for copy in panel_copies:
        copy.wait()
    panel = held_ref[...]
    to_strip(dot(panel, panel, ((1,), (1,))), out_ref.at[width:, :])
    which = which_ref[0]
    for j in range(mine_ref.shape[1] // width):
        start = j * ratio * width
        block = held_ref[:, start : start + width]
        for k in range(1, ratio):
            start += width
            block = jnp.where(which == k, held_ref[:, start : start + width], block)
        mine_ref[:, j * width : (j + 1) * width] = block
    chunk = rows // pieces
    total = jnp.zeros((width, matrix_ref.shape[1]), jnp.float32)
    for piece in range(pieces):
        matrix_copies[piece].wait()
        span = slice(piece * chunk, (piece + 1) * chunk)
        terms = jnp.concatenate(split(held_ref[:, span], 3), axis=0)
        for i, part in enumerate(split(kept_ref[span, :], 3)):
            count = 3 - i
            out = dot16(terms[: count * width, :], part, ((1,), (0,)))
            for t in range(count):
                total = total + out[t * width : (t + 1) * width, :]
    out_ref[:width, :] = total


def to_strip(value, strip_ref):
    width = value.shape[0]
    for i in range(width // STRIP):
        strip_ref[:, i * width : (i + 1) * width] = value[i * STRIP : (i + 1) * STRIP, :]


def from_strip(strip, width):
    return jnp.concatenate(
        [strip[:, i * width : (i + 1) * width] for i in range(width // STRIP)], axis=0
    )


def finish_kernel(mine_ref, other_ref, product_ref, gram_ref):
    width = product_ref.shape[0]
    product_ref[...] = mine_ref[:width, :] + other_ref[:width, :]
    gram_ref[...] = from_strip(mine_ref[width:, :] + other_ref[width:, :], width)


def inner_kernel(near_ref, mine_ref, inner_ref):
    inner_ref[...] = dot(mine_ref[...], near_ref[...], ((1,), (1,)))


def factor_kernel(gram_ref, inverse_ref):
    size = inverse_ref.shape[0]
    batch = 4
    row = lax.broadcasted_iota(jnp.int32, (size, 2 * size), 0)
    lane = lax.broadcasted_iota(jnp.int32, (size, 2 * size), 1)
    eye = jnp.where(row == lane, 1.0, 0.0).astype(jnp.float32)
    table = jnp.concatenate([eye[:, :size], gram_ref[...]], axis=1)
    for first in range(0, size, batch):
        base = first // 8 * 8
        height = size - base
        low = table[base:, :]
        low_row = row[base:, :]
        cols = [
            jnp.broadcast_to(low[:, size + first + t : size + first + t + 1], (height, 2 * size))
            for t in range(batch)
        ]
        rows = [low[first - base + t : first - base + t + 1, :] for t in range(batch)]
        for t in range(batch):
            at = first - base + t
            scale = 1.0 / cols[t][at : at + 1, :]
            factor = jnp.where(low_row > first + t, cols[t] * scale, 0.0)
            for s in range(t + 1, batch):
                cols[s] = cols[s] - factor * cols[s][at : at + 1, :]
                rows[s] = rows[s] - factor[first - base + s : first - base + s + 1, :] * rows[t]
            low = low - factor * rows[t]
        table = low if base == 0 else jnp.concatenate([table[:base, :], low], axis=0)
    diagonal = jnp.sum(jnp.where(lane == row + size, table, 0.0), axis=1, keepdims=True)
    inverse_ref[...] = (table / jnp.sqrt(diagonal))[:, :size]


def stack_left(value):
    high, low = split(value, 2)
    return jnp.concatenate([high, low, high], axis=0)


def stack_right(value):
    high, low = split(value, 2)
    return jnp.concatenate([high, high, low], axis=0)


def basis_kernel(
    matrix_ref, panel_ref, product_cols_ref, inverse_ref, received_ref, held_ref, apart_ref,
    begun_ref, basis_ref, kept_ref, cols_ref,
):
    inverse = inverse_ref[...]
    basis = dot(inverse, panel_ref[...], ((1,), (0,)))
    image_cols = dot(inverse, product_cols_ref[...], ((1,), (0,)))
    basis_ref[...] = basis
    kept_ref[...] = basis
    panel_cols = jnp.where((apart_ref[0] & 1) != 0, received_ref[...], held_ref[...])
    cols_ref[...] = dot(inverse, panel_cols, ((1,), (0,)))
    left = stack_left(basis)
    right = stack_right(2.0 * image_cols)
    chunk = 256
    for start in range(0, matrix_ref.shape[0], chunk):
        span = slice(start, start + chunk)
        begun_ref[span, :] = matrix_ref[span, :] - dot16(left[:, span], right, ((0,), (0,)))


def image_kernel(ratio, which_ref, begun_ref, cols_ref, inverse_ref, *refs):
    halves, (further_ref, image_ref) = refs[:ratio], refs[ratio:]
    width = inverse_ref.shape[0]
    which = which_ref[0]
    parts = []
    for j in range(halves[0].shape[1] // width):
        span = slice(j * width, (j + 1) * width)
        for k in range(ratio):
            block = halves[0][:, span]
            for shift in range(1, ratio):
                block = jnp.where((which + shift) % ratio == k, halves[shift][:, span], block)
            parts.append(block)
    image = dot(inverse_ref[...], jnp.concatenate(parts, axis=1), ((1,), (0,)))
    image_ref[...] = image
    left = stack_left(2.0 * image)
    right = stack_right(cols_ref[...])
    chunk = 256
    for start in range(0, begun_ref.shape[0], chunk):
        span = slice(start, start + chunk)
        further_ref[span, :] = begun_ref[span, :] - dot16(left[:, span], right, ((0,), (0,)))


def update_kernel(further_ref, image_ref, basis_ref, cols_ref, inverse_ref, *refs):
    inners, (updated_ref, w_ref, buffer_ref, w_buffer_ref, sems) = refs[:-5], refs[-5:]
    inverse = inverse_ref[...]
    basis = basis_ref[...]
    inner = inners[0][...]
    for other in inners[1:]:
        inner = inner + other[...]
    correction = dot(dot(inverse, inner, ((1,), (0,))), inverse, ((1,), (1,)))
    right = stack_right(4.0 * dot(correction, cols_ref[...], ((1,), (0,))))
    left = stack_left(basis)
    count = sems.shape[0] - 1
    chunk = further_ref.shape[0] // count
    copies = []
    for i in range(count):
        span = slice(i * chunk, (i + 1) * chunk)
        buffer_ref[span, :] = further_ref[span, :] + dot16(left[:, span], right, ((0,), (0,)))
        copies.append(
            pltpu.make_async_copy(buffer_ref.at[span, :], updated_ref.at[span, :], sems.at[i])
        )
        copies[-1].start()
    w_buffer_ref[...] = 2.0 * (image_ref[...] - dot(correction, basis, ((0,), (0,))))
    copies.append(pltpu.make_async_copy(w_buffer_ref, w_ref, sems.at[count]))
    copies[-1].start()
    for copy in copies:
        copy.wait()


def shape(*dims, dtype=jnp.float32):
    return jax.ShapeDtypeStruct(dims, dtype)


def call(kernel, outs, args, in_specs=None, out_specs=None, scratch=(), flops=0):
    return pl.pallas_call(
        kernel,
        out_shape=outs,
        in_specs=in_specs or [VMEM] * len(args),
        out_specs=out_specs or ((VMEM,) * len(outs) if isinstance(outs, tuple) else VMEM),
        scratch_shapes=scratch,
        compiler_params=PARAMS,
        cost_estimate=pl.CostEstimate(flops=flops, bytes_accessed=1 << 18, transcendentals=0),
    )(*args)


def local(matrix, panel):
    n_row, n_col = lax.axis_size("row"), lax.axis_size("col")
    ratio = n_col // n_row
    rows, width = panel.shape
    cols = matrix.shape[1]
    which = (lax.axis_index("col") // n_row).astype(jnp.int32).reshape(1)
    chunks = 8

    message, mine, panel_t, kept = call(
        functools.partial(product_kernel, ratio),
        (shape(width + STRIP, cols), shape(width, cols), shape(width, rows), shape(rows, cols)),
        (
            which,
            pltpu.with_memory_space_constraint(panel.T, pltpu.HBM),
            pltpu.with_memory_space_constraint(matrix, pltpu.HBM),
        ),
        in_specs=[SMEM, HBM, HBM],
        scratch=[pltpu.SemaphoreType.DMA((8,))],
        flops=1 << 30,
    )
    step = 1
    while 2 * step < n_row:
        message = message + partner(message, "row", step)
        step *= 2
    last = partner(message, "row", step)
    product_cols, gram = call(
        finish_kernel, (shape(width, cols), shape(width, width)), (message, last), flops=1 << 24
    )
    product_cols, held = lax.optimization_barrier((product_cols, mine))
    apart = lax.axis_index("row") ^ (lax.axis_index("col") % n_row)
    flag = apart.astype(jnp.int32).reshape(1)
    near = transpose_grid(product_cols)
    bit = n_row // 2
    while bit > 2:
        held = jnp.where(apart & bit != 0, spread_hop(held, bit), held)
        bit //= 2
    received = spread_hop(held, 2)
    near, gram = lax.optimization_barrier((near, gram))
    halves = [near] + [other_half(near, shift) for shift in range(1, ratio)]
    inner = call(inner_kernel, shape(width, width), (near, mine), flops=1 << 24)
    step = 1
    while step < n_row:
        inner = inner + partner(inner, "row", step)
        if step == 1:
            inner, received = lax.optimization_barrier((inner, received))
            held = jnp.where(apart & 2 != 0, received, held)
            received = spread_hop(held, 1)
        step *= 2
    inner, halves = lax.optimization_barrier((inner, halves))
    inners = [inner] + [other_half(inner, shift) for shift in range(1, ratio)]
    inverse = call(factor_kernel, shape(width, width), (gram,), flops=1 << 30)
    begun, basis, basis_kept, basis_cols = call(
        basis_kernel,
        (shape(rows, cols), shape(width, rows), shape(width, rows), shape(width, cols)),
        (kept, panel_t, product_cols, inverse, received, held, flag),
        in_specs=[VMEM] * 6 + [SMEM],
        flops=1 << 30,
    )
    further, image = call(
        functools.partial(image_kernel, ratio),
        (shape(rows, cols), shape(width, rows)),
        (which, begun, basis_cols, inverse, *halves),
        in_specs=[SMEM] + [VMEM] * (3 + ratio),
        flops=1 << 30,
    )
    updated, w_rows = call(
        update_kernel,
        (shape(rows, cols), shape(width, rows)),
        (further, image, basis_kept, basis_cols, inverse, *inners),
        out_specs=(HBM, HBM),
        scratch=[
            pltpu.VMEM((rows, cols), jnp.float32),
            pltpu.VMEM((width, rows), jnp.float32),
            pltpu.SemaphoreType.DMA((chunks + 1,)),
        ],
        flops=1 << 30,
    )
    return (updated, w_rows.T, basis.T)


def solution(mesh):
    return jax.shard_map(
        local,
        mesh=mesh,
        in_specs=(P("row", "col"), P("row", None)),
        out_specs=(P("row", "col"), P("row", None), P("row", None)),
        check_vma=False,
    )
```

```python
import functools

import jax
import jax.numpy as jnp
from jax import lax
from jax.experimental import pallas as pl
from jax.experimental.pallas import tpu as pltpu
from jax.sharding import PartitionSpec as P

HIGH = lax.Precision.HIGHEST
VMEM = pl.BlockSpec(memory_space=pltpu.VMEM)
SMEM = pl.BlockSpec(memory_space=pltpu.SMEM)
HBM = pl.BlockSpec(memory_space=pltpu.HBM)
PARAMS = pltpu.CompilerParams(vmem_limit_bytes=40 * 1024 * 1024)
STRIP = 8


def dot(left, right, contract, precision=HIGH):
    return lax.dot_general(
        left, right, (contract, ((), ())), precision=precision, preferred_element_type=jnp.float32
    )


def dot16(left, right, contract):
    return dot(left, right, contract, lax.Precision.DEFAULT)


def split(value, parts):
    terms = []
    for _ in range(parts):
        terms.append(value.astype(jnp.bfloat16))
        value = value - terms[-1].astype(jnp.float32)
    return terms


def partner(value, axis, step):
    size = lax.axis_size(axis)
    return lax.ppermute(value, axis, [(i, i ^ step) for i in range(size)])


def tree_sum(parts):
    while len(parts) > 1:
        parts = [parts[i] + parts[i + 1] for i in range(0, len(parts), 2)]
    return parts[0]


def group_parts(value, axis, low, high):
    parts = [value]
    while low < high:
        value = tree_sum(parts)
        radix = min(4, high // low)
        parts = [value] + [partner(value, axis, i * low) for i in range(1, radix)]
        low *= radix
    return parts


def spread_rows(value):
    n_row, n_col = lax.axis_size("row"), lax.axis_size("col")
    apart = lax.axis_index("row") ^ (lax.axis_index("col") % n_row)
    bit = n_row // 2
    while bit:
        pairs = []
        for c in range(n_col):
            for offset in range(0, n_row, 2 * bit):
                source = (c % n_row) ^ offset
                pairs.append((source * n_col + c, (source ^ bit) * n_col + c))
        received = lax.ppermute(value, ("row", "col"), pairs)
        if bit == 1:
            return value, received, (apart & 1).astype(jnp.int32).reshape(1)
        value = jnp.where(apart & bit != 0, received, value)
        bit //= 2


def transpose_grid(value):
    n_row, n_col = lax.axis_size("row"), lax.axis_size("col")
    pairs = []
    for r in range(n_row):
        for k in range(n_col // n_row):
            for q in range(n_row):
                source = (q ^ (n_row // 2)) * n_col + k * n_row + r
                pairs.append((source, r * n_col + k * n_row + q))
    return lax.ppermute(value, ("row", "col"), pairs)


def other_half(value, shift):
    n_row, n_col = lax.axis_size("row"), lax.axis_size("col")
    pairs = [((c + shift * n_row) % n_col, c) for c in range(n_col)]
    return lax.ppermute(value, "col", pairs)


def row_copies(source, target, sems, first, pieces):
    size = source.shape[0] // pieces
    copies = []
    for piece in range(pieces):
        span = slice(piece * size, (piece + 1) * size)
        copies.append(
            pltpu.make_async_copy(source.at[span, :], target.at[span, :], sems.at[first + piece])
        )
    return copies


def product_kernel(
    ratio, which_ref, panel_ref, matrix_ref, out_ref, mine_ref, held_ref, kept_ref, sems
):
    width, rows = panel_ref.shape
    pieces = sems.shape[0] // 2
    window = 4
    panel_copies = row_copies(panel_ref, held_ref, sems, 0, pieces)
    matrix_copies = row_copies(matrix_ref, kept_ref, sems, pieces, pieces)
    for copy in panel_copies + matrix_copies[:window]:
        copy.start()
    for copy in panel_copies:
        copy.wait()
    panel = held_ref[...]
    to_strip(dot(panel, panel, ((1,), (1,))), out_ref.at[width:, :])
    which = which_ref[0]
    for j in range(mine_ref.shape[1] // width):
        start = j * ratio * width
        block = held_ref[:, start : start + width]
        for k in range(1, ratio):
            start += width
            block = jnp.where(which == k, held_ref[:, start : start + width], block)
        mine_ref[:, j * width : (j + 1) * width] = block
    chunk = 2 * rows // pieces
    total = jnp.zeros((width, matrix_ref.shape[1]), jnp.float32)
    for piece in range(0, pieces, 2):
        for at in (piece, piece + 1):
            matrix_copies[at].wait()
            if at + window < pieces:
                matrix_copies[at + window].start()
        span = slice(piece // 2 * chunk, (piece // 2 + 1) * chunk)
        terms = jnp.concatenate(split(held_ref[:, span], 3), axis=0)
        for i, part in enumerate(split(kept_ref[span, :], 3)):
            count = 3 - i
            out = dot16(terms[: count * width, :], part, ((1,), (0,)))
            for t in range(count):
                total = total + out[t * width : (t + 1) * width, :]
    out_ref[:width, :] = total


def to_strip(value, strip_ref):
    width = value.shape[0]
    for i in range(width // STRIP):
        strip_ref[:, i * width : (i + 1) * width] = value[i * STRIP : (i + 1) * STRIP, :]


def from_strip(strip, width):
    return jnp.concatenate(
        [strip[:, i * width : (i + 1) * width] for i in range(width // STRIP)], axis=0
    )


def finish_kernel(other_ref, mine_ref, product_ref, gram_ref):
    width = product_ref.shape[0]
    product_ref[...] = mine_ref[:width, :] + other_ref[:width, :]
    gram_ref[...] = from_strip(mine_ref[width:, :] + other_ref[width:, :], width)


def inner_kernel(product_ref, received_ref, held_ref, takes_ref, inner_ref, panel_cols_ref):
    panel_cols = jnp.where(takes_ref[0] != 0, received_ref[...], held_ref[...])
    panel_cols_ref[...] = panel_cols
    inner_ref[...] = dot(panel_cols, product_ref[...], ((1,), (1,)))


def pack_kernel(near_ref, *refs):
    parts, sent_ref = refs[:-1], refs[-1]
    width = near_ref.shape[0]
    sent_ref[:width, :] = near_ref[...]
    to_strip(tree_sum([part[...] for part in parts]), sent_ref.at[width:, :])


def factor_kernel(gram_ref, inverse_ref):
    size = inverse_ref.shape[0]
    batch = 4
    row = lax.broadcasted_iota(jnp.int32, (size, 2 * size), 0)
    lane = lax.broadcasted_iota(jnp.int32, (size, 2 * size), 1)
    eye = jnp.where(row == lane, 1.0, 0.0).astype(jnp.float32)
    table = jnp.concatenate([eye[:, :size], gram_ref[...]], axis=1)
    for first in range(0, size, batch):
        base = first // 8 * 8
        height = size - base
        low = table[base:, :]
        low_row = row[base:, :]
        cols = [
            jnp.broadcast_to(low[:, size + first + t : size + first + t + 1], (height, 2 * size))
            for t in range(batch)
        ]
        rows = [low[first - base + t : first - base + t + 1, :] for t in range(batch)]
        for t in range(batch):
            at = first - base + t
            scale = 1.0 / cols[t][at : at + 1, :]
            factor = jnp.where(low_row > first + t, cols[t] * scale, 0.0)
            for s in range(t + 1, batch):
                cols[s] = cols[s] - factor * cols[s][at : at + 1, :]
                rows[s] = rows[s] - factor[first - base + s : first - base + s + 1, :] * rows[t]
            low = low - factor * rows[t]
        table = low if base == 0 else jnp.concatenate([table[:base, :], low], axis=0)
    diagonal = jnp.sum(jnp.where(lane == row + size, table, 0.0), axis=1, keepdims=True)
    inverse_ref[...] = (table / jnp.sqrt(diagonal))[:, :size]


def stack_left(value):
    high, low = split(value, 2)
    return jnp.concatenate([high, low, high], axis=0)


def stack_right(value):
    high, low = split(value, 2)
    return jnp.concatenate([high, high, low], axis=0)


def basis_kernel(
    matrix_ref, panel_ref, panel_cols_ref, product_cols_ref, inverse_ref,
    begun_ref, basis_ref, kept_ref, right_ref,
):
    inverse = inverse_ref[...]
    basis = dot(inverse, panel_ref[...], ((1,), (0,)))
    image_cols = dot(inverse, product_cols_ref[...], ((1,), (0,)))
    basis_ref[...] = basis
    kept_ref[...] = basis
    right_ref[...] = stack_right(dot(inverse, panel_cols_ref[...], ((1,), (0,))))
    left = stack_left(basis)
    right = stack_right(2.0 * image_cols)
    chunk = 256
    for start in range(0, matrix_ref.shape[0], chunk):
        span = slice(start, start + chunk)
        begun_ref[span, :] = matrix_ref[span, :] - dot16(left[:, span], right, ((0,), (0,)))


def update_kernel(
    ratio, which_ref, begun_ref, basis_ref, right_ref, inverse_ref, *refs
):
    halves, (updated_ref, w_ref, buffer_ref, w_buffer_ref, sems) = refs[:ratio], refs[ratio:]
    inverse = inverse_ref[...]
    width = inverse.shape[0]
    strip = halves[0][width:, :]
    for half in halves[1:]:
        strip = strip + half[width:, :]
    correction = dot(
        dot(inverse, from_strip(strip, width), ((1,), (0,))), inverse, ((1,), (1,))
    )
    removed = dot(correction, basis_ref[...], ((0,), (0,)))
    which = which_ref[0]
    parts = []
    for j in range(halves[0].shape[1] // width):
        span = slice(j * width, (j + 1) * width)
        for k in range(ratio):
            block = halves[0][:width, span]
            for shift in range(1, ratio):
                block = jnp.where(
                    (which + shift) % ratio == k, halves[shift][:width, span], block
                )
            parts.append(block)
    image = dot(inverse, jnp.concatenate(parts, axis=1), ((1,), (0,)))
    left = stack_left(2.0 * image - 4.0 * removed)
    right = right_ref[...]
    count = sems.shape[0] - 1
    chunk = begun_ref.shape[0] // count
    w_buffer_ref[...] = 2.0 * (image - removed)
    copies = [pltpu.make_async_copy(w_buffer_ref, w_ref, sems.at[count])]
    copies[-1].start()
    for i in range(count):
        span = slice(i * chunk, (i + 1) * chunk)
        buffer_ref[span, :] = begun_ref[span, :] - dot16(left[:, span], right, ((0,), (0,)))
        copies.append(
            pltpu.make_async_copy(buffer_ref.at[span, :], updated_ref.at[span, :], sems.at[i])
        )
        copies[-1].start()
    for copy in copies:
        copy.wait()


def shape(*dims, dtype=jnp.float32):
    return jax.ShapeDtypeStruct(dims, dtype)


def call(kernel, outs, args, in_specs=None, out_specs=None, scratch=(), flops=0):
    return pl.pallas_call(
        kernel,
        out_shape=outs,
        in_specs=in_specs or [VMEM] * len(args),
        out_specs=out_specs or ((VMEM,) * len(outs) if isinstance(outs, tuple) else VMEM),
        scratch_shapes=scratch,
        compiler_params=PARAMS,
        cost_estimate=pl.CostEstimate(flops=flops, bytes_accessed=1 << 18, transcendentals=0),
    )(*args)


def local(matrix, panel):
    n_row, n_col = lax.axis_size("row"), lax.axis_size("col")
    ratio = n_col // n_row
    rows, width = panel.shape
    cols = matrix.shape[1]
    which = (lax.axis_index("col") // n_row).astype(jnp.int32).reshape(1)
    chunks = 8

    message, mine, panel_t, kept = call(
        functools.partial(product_kernel, ratio),
        (shape(width + STRIP, cols), shape(width, cols), shape(width, rows), shape(rows, cols)),
        (
            which,
            pltpu.with_memory_space_constraint(panel.T, pltpu.HBM),
            pltpu.with_memory_space_constraint(matrix, pltpu.HBM),
        ),
        in_specs=[SMEM, HBM, HBM],
        scratch=[pltpu.SemaphoreType.DMA((2 * chunks,))],
        flops=1 << 30,
    )
    held, received, takes = spread_rows(mine)
    step = 1
    while 2 * step < n_row:
        message = message + partner(message, "row", step)
        step *= 2
    last = partner(message, "row", step)
    product_cols, gram = call(
        finish_kernel, (shape(width, cols), shape(width, width)), (last, message), flops=1 << 24
    )
    near = transpose_grid(product_cols)
    inner, panel_cols = call(
        inner_kernel,
        (shape(width, width), shape(width, cols)),
        (product_cols, received, held, takes),
        in_specs=[VMEM] * 3 + [SMEM],
        flops=1 << 24,
    )
    parts = group_parts(inner, "col", 1, n_row)
    sent = call(pack_kernel, shape(width + STRIP, cols), (near, *parts), flops=1 << 18)
    halves = [sent] + [other_half(sent, shift) for shift in range(1, ratio)]
    inverse = call(factor_kernel, shape(width, width), (gram,), flops=1 << 30)
    begun, basis, basis_kept, right = call(
        basis_kernel,
        (
            shape(rows, cols),
            shape(width, rows),
            shape(width, rows),
            shape(3 * width, cols, dtype=jnp.bfloat16),
        ),
        (kept, panel_t, panel_cols, product_cols, inverse),
        flops=1 << 30,
    )
    updated, w_rows = call(
        functools.partial(update_kernel, ratio),
        (shape(rows, cols), shape(width, rows)),
        (which, begun, basis_kept, right, inverse, *halves),
        in_specs=[SMEM] + [VMEM] * (4 + ratio),
        out_specs=(HBM, HBM),
        scratch=[
            pltpu.VMEM((rows, cols), jnp.float32),
            pltpu.VMEM((width, rows), jnp.float32),
            pltpu.SemaphoreType.DMA((chunks + 1,)),
        ],
        flops=1 << 30,
    )
    return (updated, w_rows.T, basis.T)


def solution(mesh):
    return jax.shard_map(
        local,
        mesh=mesh,
        in_specs=(P("row", "col"), P("row", None)),
        out_specs=(P("row", "col"), P("row", None), P("row", None)),
        check_vma=False,
    )
```

```python
import functools

import jax
import jax.numpy as jnp
from jax import lax
from jax.experimental import pallas as pl
from jax.experimental.pallas import tpu as pltpu
from jax.sharding import PartitionSpec as P

HIGH = lax.Precision.HIGHEST
VMEM = pl.BlockSpec(memory_space=pltpu.VMEM)
SMEM = pl.BlockSpec(memory_space=pltpu.SMEM)
HBM = pl.BlockSpec(memory_space=pltpu.HBM)
PARAMS = pltpu.CompilerParams(vmem_limit_bytes=40 * 1024 * 1024)
STRIP = 8


def dot(left, right, contract, precision=HIGH):
    return lax.dot_general(
        left, right, (contract, ((), ())), precision=precision, preferred_element_type=jnp.float32
    )


def dot16(left, right, contract):
    return dot(left, right, contract, lax.Precision.DEFAULT)


def split(value, parts):
    terms = []
    for _ in range(parts):
        terms.append(value.astype(jnp.bfloat16))
        value = value - terms[-1].astype(jnp.float32)
    return terms


def partner(value, axis, step):
    size = lax.axis_size(axis)
    return lax.ppermute(value, axis, [(i, i ^ step) for i in range(size)])


def tree_sum(parts):
    while len(parts) > 1:
        parts = [parts[i] + parts[i + 1] for i in range(0, len(parts), 2)]
    return parts[0]


def group_parts(value, axis, low, high):
    parts = [value]
    while low < high:
        value = tree_sum(parts)
        radix = min(4, high // low)
        parts = [value] + [partner(value, axis, i * low) for i in range(1, radix)]
        low *= radix
    return parts


def spread_rows(value, after):
    n_row, n_col = lax.axis_size("row"), lax.axis_size("col")
    apart = lax.axis_index("row") ^ (lax.axis_index("col") % n_row)
    bits = [1] + [1 << i for i in reversed(range(1, n_row.bit_length() - 1))]
    reached = [0]
    for bit in bits:
        pairs = []
        for c in range(n_col):
            for offset in reached:
                source = (c % n_row) ^ offset
                pairs.append((source * n_col + c, (source ^ bit) * n_col + c))
        reached += [offset ^ bit for offset in reached]
        received = lax.ppermute(value, ("row", "col"), pairs)
        takes = apart & bit != 0
        if bit == bits[-1]:
            return value, received, takes.astype(jnp.int32).reshape(1)
        received, _ = lax.optimization_barrier((received, after))
        value = jnp.where(takes, received, value)


def transpose_grid(value):
    n_row, n_col = lax.axis_size("row"), lax.axis_size("col")
    pairs = []
    for r in range(n_row):
        for k in range(n_col // n_row):
            for q in range(n_row):
                source = (q ^ (n_row // 2)) * n_col + k * n_row + r
                pairs.append((source, r * n_col + k * n_row + q))
    return lax.ppermute(value, ("row", "col"), pairs)


def other_half(value, shift):
    n_row, n_col = lax.axis_size("row"), lax.axis_size("col")
    pairs = [((c + shift * n_row) % n_col, c) for c in range(n_col)]
    return lax.ppermute(value, "col", pairs)


def copy_rows(source, target, sems, first, pieces):
    size = source.shape[0] // pieces
    copies = []
    for piece in range(pieces):
        span = slice(piece * size, (piece + 1) * size)
        copies.append(
            pltpu.make_async_copy(source.at[span, :], target.at[span, :], sems.at[first + piece])
        )
        copies[-1].start()
    return copies


def panel_kernel(
    ratio, which_ref, panel_ref, matrix_ref,
    mine_ref, held_ref, terms_ref, gram_ref, kept_ref, sems,
):
    width = panel_ref.shape[0]
    pieces = sems.shape[0] // 2
    panel_copies = copy_rows(panel_ref, held_ref, sems, 0, pieces)
    matrix_copies = copy_rows(matrix_ref, kept_ref, sems, pieces, pieces)
    for copy in panel_copies:
        copy.wait()
    which = which_ref[0]
    for j in range(mine_ref.shape[1] // width):
        start = j * ratio * width
        block = held_ref[:, start : start + width]
        for k in range(1, ratio):
            start += width
            block = jnp.where(which == k, held_ref[:, start : start + width], block)
        mine_ref[:, j * width : (j + 1) * width] = block
    panel = held_ref[...]
    terms_ref[...] = jnp.concatenate(split(panel, 3), axis=0)
    to_strip(dot(panel, panel, ((1,), (1,))), gram_ref)
    for copy in matrix_copies:
        copy.wait()


def product_kernel(terms_ref, matrix_ref, gram_ref, out_ref):
    width = out_ref.shape[0] - STRIP
    rows = matrix_ref.shape[0]
    chunk = 256
    total = jnp.zeros((width, matrix_ref.shape[1]), jnp.float32)
    for start in range(0, rows, chunk):
        span = slice(start, start + chunk)
        parts = split(matrix_ref[span, :], 3)
        for i, part in enumerate(parts):
            count = 3 - i
            out = dot16(terms_ref[: count * width, span], part, ((1,), (0,)))
            for t in range(count):
                total = total + out[t * width : (t + 1) * width, :]
    out_ref[:width, :] = total
    out_ref[width:, :] = gram_ref[...]


def to_strip(value, strip_ref):
    width = value.shape[0]
    for i in range(width // STRIP):
        strip_ref[:, i * width : (i + 1) * width] = value[i * STRIP : (i + 1) * STRIP, :]


def from_strip(strip, width):
    return jnp.concatenate(
        [strip[:, i * width : (i + 1) * width] for i in range(width // STRIP)], axis=0
    )


def finish_kernel(other_ref, mine_ref, product_ref, gram_ref):
    width = product_ref.shape[0]
    product_ref[...] = mine_ref[:width, :] + other_ref[:width, :]
    gram_ref[...] = from_strip(mine_ref[width:, :] + other_ref[width:, :], width)


def inner_kernel(product_ref, received_ref, held_ref, takes_ref, inner_ref, panel_cols_ref):
    panel_cols = jnp.where(takes_ref[0] != 0, received_ref[...], held_ref[...])
    panel_cols_ref[...] = panel_cols
    inner_ref[...] = dot(panel_cols, product_ref[...], ((1,), (1,)))


def pack_kernel(near_ref, *refs):
    parts, sent_ref = refs[:-1], refs[-1]
    width = near_ref.shape[0]
    sent_ref[:width, :] = near_ref[...]
    to_strip(tree_sum([part[...] for part in parts]), sent_ref.at[width:, :])


def factor_kernel(gram_ref, inverse_ref):
    size = inverse_ref.shape[0]
    batch = 4
    row = lax.broadcasted_iota(jnp.int32, (size, 2 * size), 0)
    lane = lax.broadcasted_iota(jnp.int32, (size, 2 * size), 1)
    eye = jnp.where(row == lane, 1.0, 0.0).astype(jnp.float32)
    table = jnp.concatenate([eye[:, :size], gram_ref[...]], axis=1)
    for first in range(0, size, batch):
        base = first // 8 * 8
        height = size - base
        low = table[base:, :]
        low_row = row[base:, :]
        cols = [
            jnp.broadcast_to(low[:, size + first + t : size + first + t + 1], (height, 2 * size))
            for t in range(batch)
        ]
        rows = [low[first - base + t : first - base + t + 1, :] for t in range(batch)]
        for t in range(batch):
            at = first - base + t
            scale = 1.0 / cols[t][at : at + 1, :]
            factor = jnp.where(low_row > first + t, cols[t] * scale, 0.0)
            for s in range(t + 1, batch):
                cols[s] = cols[s] - factor * cols[s][at : at + 1, :]
                rows[s] = rows[s] - factor[first - base + s : first - base + s + 1, :] * rows[t]
            low = low - factor * rows[t]
        table = low if base == 0 else jnp.concatenate([table[:base, :], low], axis=0)
    diagonal = jnp.sum(jnp.where(lane == row + size, table, 0.0), axis=1, keepdims=True)
    inverse_ref[...] = (table / jnp.sqrt(diagonal))[:, :size]


def stack_left(value):
    high, low = split(value, 2)
    return jnp.concatenate([high, low, high], axis=0)


def stack_right(value):
    high, low = split(value, 2)
    return jnp.concatenate([high, high, low], axis=0)


def basis_kernel(
    matrix_ref, panel_ref, panel_cols_ref, product_cols_ref, inverse_ref,
    begun_ref, basis_ref, kept_ref, right_ref,
):
    inverse = inverse_ref[...]
    basis = dot(inverse, panel_ref[...], ((1,), (0,)))
    image_cols = dot(inverse, product_cols_ref[...], ((1,), (0,)))
    basis_ref[...] = basis
    kept_ref[...] = basis
    right_ref[...] = stack_right(dot(inverse, panel_cols_ref[...], ((1,), (0,))))
    left = stack_left(basis)
    right = stack_right(2.0 * image_cols)
    chunk = 256
    for start in range(0, matrix_ref.shape[0], chunk):
        span = slice(start, start + chunk)
        begun_ref[span, :] = matrix_ref[span, :] - dot16(left[:, span], right, ((0,), (0,)))


def update_kernel(
    ratio, which_ref, begun_ref, basis_ref, right_ref, inverse_ref, *refs
):
    halves, (updated_ref, w_ref, buffer_ref, w_buffer_ref, sems) = refs[:ratio], refs[ratio:]
    inverse = inverse_ref[...]
    width = inverse.shape[0]
    strip = halves[0][width:, :]
    for half in halves[1:]:
        strip = strip + half[width:, :]
    correction = dot(
        dot(inverse, from_strip(strip, width), ((1,), (0,))), inverse, ((1,), (1,))
    )
    removed = dot(correction, basis_ref[...], ((0,), (0,)))
    which = which_ref[0]
    parts = []
    for j in range(halves[0].shape[1] // width):
        span = slice(j * width, (j + 1) * width)
        for k in range(ratio):
            block = halves[0][:width, span]
            for shift in range(1, ratio):
                block = jnp.where(
                    (which + shift) % ratio == k, halves[shift][:width, span], block
                )
            parts.append(block)
    image = dot(inverse, jnp.concatenate(parts, axis=1), ((1,), (0,)))
    left = stack_left(2.0 * image - 4.0 * removed)
    right = right_ref[...]
    count = sems.shape[0] - 1
    chunk = begun_ref.shape[0] // count
    w_buffer_ref[...] = 2.0 * (image - removed)
    copies = [pltpu.make_async_copy(w_buffer_ref, w_ref, sems.at[count])]
    copies[-1].start()
    for i in range(count):
        span = slice(i * chunk, (i + 1) * chunk)
        buffer_ref[span, :] = begun_ref[span, :] - dot16(left[:, span], right, ((0,), (0,)))
        copies.append(
            pltpu.make_async_copy(buffer_ref.at[span, :], updated_ref.at[span, :], sems.at[i])
        )
        copies[-1].start()
    for copy in copies:
        copy.wait()


def shape(*dims, dtype=jnp.float32):
    return jax.ShapeDtypeStruct(dims, dtype)


def call(kernel, outs, args, in_specs=None, out_specs=None, scratch=(), flops=0):
    return pl.pallas_call(
        kernel,
        out_shape=outs,
        in_specs=in_specs or [VMEM] * len(args),
        out_specs=out_specs or ((VMEM,) * len(outs) if isinstance(outs, tuple) else VMEM),
        scratch_shapes=scratch,
        compiler_params=PARAMS,
        cost_estimate=pl.CostEstimate(flops=flops, bytes_accessed=1 << 18, transcendentals=0),
    )(*args)


def local(matrix, panel):
    n_row, n_col = lax.axis_size("row"), lax.axis_size("col")
    ratio = n_col // n_row
    rows, width = panel.shape
    cols = matrix.shape[1]
    which = (lax.axis_index("col") // n_row).astype(jnp.int32).reshape(1)
    chunks = 8

    mine, panel_t, terms, gram, kept = call(
        functools.partial(panel_kernel, ratio),
        (
            shape(width, cols),
            shape(width, rows),
            shape(3 * width, rows, dtype=jnp.bfloat16),
            shape(STRIP, cols),
            shape(rows, cols),
        ),
        (
            which,
            pltpu.with_memory_space_constraint(panel.T, pltpu.HBM),
            pltpu.with_memory_space_constraint(matrix, pltpu.HBM),
        ),
        in_specs=[SMEM, HBM, HBM],
        scratch=[pltpu.SemaphoreType.DMA((2 * chunks,))],
        flops=1 << 28,
    )
    message = call(
        product_kernel, shape(width + STRIP, cols), (terms, kept, gram), flops=1 << 30
    )
    step = 1
    while 2 * step < n_row:
        message = message + partner(message, "row", step)
        step *= 2
    last = partner(message, "row", step)
    held, received, takes = spread_rows(mine, message)
    product_cols, gram = call(
        finish_kernel, (shape(width, cols), shape(width, width)), (last, message), flops=1 << 24
    )
    near = transpose_grid(product_cols)
    inner, panel_cols = call(
        inner_kernel,
        (shape(width, width), shape(width, cols)),
        (product_cols, received, held, takes),
        in_specs=[VMEM] * 3 + [SMEM],
        flops=1 << 24,
    )
    parts = group_parts(inner, "col", 1, n_row)
    sent = call(pack_kernel, shape(width + STRIP, cols), (near, *parts), flops=1 << 18)
    halves = [sent] + [other_half(sent, shift) for shift in range(1, ratio)]
    inverse = call(factor_kernel, shape(width, width), (gram,), flops=1 << 30)
    begun, basis, basis_kept, right = call(
        basis_kernel,
        (
            shape(rows, cols),
            shape(width, rows),
            shape(width, rows),
            shape(3 * width, cols, dtype=jnp.bfloat16),
        ),
        (kept, panel_t, panel_cols, product_cols, inverse),
        flops=1 << 30,
    )
    updated, w_rows = call(
        functools.partial(update_kernel, ratio),
        (shape(rows, cols), shape(width, rows)),
        (which, begun, basis_kept, right, inverse, *halves),
        in_specs=[SMEM] + [VMEM] * (4 + ratio),
        out_specs=(HBM, HBM),
        scratch=[
            pltpu.VMEM((rows, cols), jnp.float32),
            pltpu.VMEM((width, rows), jnp.float32),
            pltpu.SemaphoreType.DMA((chunks + 1,)),
        ],
        flops=1 << 30,
    )
    return (updated, w_rows.T, basis.T)


def solution(mesh):
    return jax.shard_map(
        local,
        mesh=mesh,
        in_specs=(P("row", "col"), P("row", None)),
        out_specs=(P("row", "col"), P("row", None), P("row", None)),
        check_vma=False,
    )
```

```python
import functools

import jax
import jax.numpy as jnp
from jax import lax
from jax.experimental import pallas as pl
from jax.experimental.pallas import tpu as pltpu
from jax.sharding import PartitionSpec as P

HIGH = lax.Precision.HIGHEST
VMEM = pl.BlockSpec(memory_space=pltpu.VMEM)
SMEM = pl.BlockSpec(memory_space=pltpu.SMEM)
HBM = pl.BlockSpec(memory_space=pltpu.HBM)
PARAMS = pltpu.CompilerParams(vmem_limit_bytes=40 * 1024 * 1024)
STRIP = 8


def dot(left, right, contract, precision=HIGH):
    return lax.dot_general(
        left, right, (contract, ((), ())), precision=precision, preferred_element_type=jnp.float32
    )


def dot16(left, right, contract):
    return dot(left, right, contract, lax.Precision.DEFAULT)


def split(value, parts):
    terms = []
    for _ in range(parts):
        terms.append(value.astype(jnp.bfloat16))
        value = value - terms[-1].astype(jnp.float32)
    return terms


def partner(value, axis, step):
    size = lax.axis_size(axis)
    return lax.ppermute(value, axis, [(i, i ^ step) for i in range(size)])


def tree_sum(parts):
    while len(parts) > 1:
        parts = [parts[i] + parts[i + 1] for i in range(0, len(parts), 2)]
    return parts[0]


def group_parts(value, axis, low, high):
    parts = [value]
    while low < high:
        value = tree_sum(parts)
        radix = min(4, high // low)
        parts = [value] + [partner(value, axis, i * low) for i in range(1, radix)]
        low *= radix
    return parts


def spread_hop(value, bit):
    n_row, n_col = lax.axis_size("row"), lax.axis_size("col")
    pairs = []
    for c in range(n_col):
        for offset in range(0, n_row, 2 * bit):
            source = (c % n_row) ^ offset
            pairs.append((source * n_col + c, (source ^ bit) * n_col + c))
    return lax.ppermute(value, ("row", "col"), pairs)


def transpose_grid(value):
    n_row, n_col = lax.axis_size("row"), lax.axis_size("col")
    pairs = []
    for r in range(n_row):
        for k in range(n_col // n_row):
            for q in range(n_row):
                source = (q ^ (n_row // 2)) * n_col + k * n_row + r
                pairs.append((source, r * n_col + k * n_row + q))
    return lax.ppermute(value, ("row", "col"), pairs)


def other_half(value, shift):
    n_row, n_col = lax.axis_size("row"), lax.axis_size("col")
    pairs = [((c + shift * n_row) % n_col, c) for c in range(n_col)]
    return lax.ppermute(value, "col", pairs)


def copy_rows(source, target, sems, first, pieces):
    size = source.shape[0] // pieces
    copies = []
    for piece in range(pieces):
        span = slice(piece * size, (piece + 1) * size)
        copies.append(
            pltpu.make_async_copy(source.at[span, :], target.at[span, :], sems.at[first + piece])
        )
        copies[-1].start()
    return copies


def panel_kernel(
    ratio, which_ref, panel_ref, matrix_ref,
    mine_ref, held_ref, terms_ref, gram_ref, kept_ref, sems,
):
    width = panel_ref.shape[0]
    pieces = sems.shape[0] // 2
    panel_copies = copy_rows(panel_ref, held_ref, sems, 0, pieces)
    matrix_copies = copy_rows(matrix_ref, kept_ref, sems, pieces, pieces)
    for copy in panel_copies:
        copy.wait()
    which = which_ref[0]
    for j in range(mine_ref.shape[1] // width):
        start = j * ratio * width
        block = held_ref[:, start : start + width]
        for k in range(1, ratio):
            start += width
            block = jnp.where(which == k, held_ref[:, start : start + width], block)
        mine_ref[:, j * width : (j + 1) * width] = block
    panel = held_ref[...]
    terms_ref[...] = jnp.concatenate(split(panel, 3), axis=0)
    to_strip(dot(panel, panel, ((1,), (1,))), gram_ref)
    for copy in matrix_copies:
        copy.wait()


def product_kernel(terms_ref, matrix_ref, gram_ref, out_ref):
    width = out_ref.shape[0] - STRIP
    rows = matrix_ref.shape[0]
    chunk = 256
    total = jnp.zeros((width, matrix_ref.shape[1]), jnp.float32)
    for start in range(0, rows, chunk):
        span = slice(start, start + chunk)
        parts = split(matrix_ref[span, :], 3)
        for i, part in enumerate(parts):
            count = 3 - i
            out = dot16(terms_ref[: count * width, span], part, ((1,), (0,)))
            for t in range(count):
                total = total + out[t * width : (t + 1) * width, :]
    out_ref[:width, :] = total
    out_ref[width:, :] = gram_ref[...]


def to_strip(value, strip_ref):
    width = value.shape[0]
    for i in range(width // STRIP):
        strip_ref[:, i * width : (i + 1) * width] = value[i * STRIP : (i + 1) * STRIP, :]


def from_strip(strip, width):
    return jnp.concatenate(
        [strip[:, i * width : (i + 1) * width] for i in range(width // STRIP)], axis=0
    )


def finish_kernel(other_ref, mine_ref, product_ref, gram_ref):
    width = product_ref.shape[0]
    product_ref[...] = mine_ref[:width, :] + other_ref[:width, :]
    gram_ref[...] = from_strip(mine_ref[width:, :] + other_ref[width:, :], width)


def inner_kernel(message_ref, received_ref, held_ref, takes_ref, inner_ref, panel_cols_ref):
    width = inner_ref.shape[0]
    panel_cols = jnp.where(takes_ref[0] != 0, received_ref[...], held_ref[...])
    panel_cols_ref[...] = panel_cols
    inner_ref[...] = dot(panel_cols, message_ref[:width, :], ((1,), (1,)))


def pack_kernel(near_ref, inner_ref, other_ref, sent_ref):
    width = near_ref.shape[0]
    sent_ref[:width, :] = near_ref[...]
    to_strip(inner_ref[...] + other_ref[...], sent_ref.at[width:, :])


def factor_kernel(gram_ref, inverse_ref):
    size = inverse_ref.shape[0]
    batch = 4
    row = lax.broadcasted_iota(jnp.int32, (size, 2 * size), 0)
    lane = lax.broadcasted_iota(jnp.int32, (size, 2 * size), 1)
    eye = jnp.where(row == lane, 1.0, 0.0).astype(jnp.float32)
    table = jnp.concatenate([eye[:, :size], gram_ref[...]], axis=1)
    for first in range(0, size, batch):
        base = first // 8 * 8
        height = size - base
        low = table[base:, :]
        low_row = row[base:, :]
        cols = [
            jnp.broadcast_to(low[:, size + first + t : size + first + t + 1], (height, 2 * size))
            for t in range(batch)
        ]
        rows = [low[first - base + t : first - base + t + 1, :] for t in range(batch)]
        for t in range(batch):
            at = first - base + t
            scale = 1.0 / cols[t][at : at + 1, :]
            factor = jnp.where(low_row > first + t, cols[t] * scale, 0.0)
            for s in range(t + 1, batch):
                cols[s] = cols[s] - factor * cols[s][at : at + 1, :]
                rows[s] = rows[s] - factor[first - base + s : first - base + s + 1, :] * rows[t]
            low = low - factor * rows[t]
        table = low if base == 0 else jnp.concatenate([table[:base, :], low], axis=0)
    diagonal = jnp.sum(jnp.where(lane == row + size, table, 0.0), axis=1, keepdims=True)
    inverse_ref[...] = (table / jnp.sqrt(diagonal))[:, :size]


def stack_left(value):
    high, low = split(value, 2)
    return jnp.concatenate([high, low, high], axis=0)


def stack_right(value):
    high, low = split(value, 2)
    return jnp.concatenate([high, high, low], axis=0)


def basis_kernel(
    matrix_ref, panel_ref, panel_cols_ref, product_cols_ref, inverse_ref,
    begun_ref, basis_ref, kept_ref, right_ref,
):
    inverse = inverse_ref[...]
    basis = dot(inverse, panel_ref[...], ((1,), (0,)))
    image_cols = dot(inverse, product_cols_ref[...], ((1,), (0,)))
    basis_ref[...] = basis
    kept_ref[...] = basis
    right_ref[...] = stack_right(dot(inverse, panel_cols_ref[...], ((1,), (0,))))
    left = stack_left(basis)
    right = stack_right(2.0 * image_cols)
    chunk = 256
    for start in range(0, matrix_ref.shape[0], chunk):
        span = slice(start, start + chunk)
        begun_ref[span, :] = matrix_ref[span, :] - dot16(left[:, span], right, ((0,), (0,)))


def update_kernel(
    ratio, which_ref, begun_ref, basis_ref, right_ref, inverse_ref, *refs
):
    halves, (updated_ref, w_ref, buffer_ref, w_buffer_ref, sems) = refs[:ratio], refs[ratio:]
    inverse = inverse_ref[...]
    width = inverse.shape[0]
    strip = halves[0][width:, :]
    for half in halves[1:]:
        strip = strip + half[width:, :]
    correction = dot(
        dot(inverse, from_strip(strip, width), ((1,), (0,))), inverse, ((1,), (1,))
    )
    removed = dot(correction, basis_ref[...], ((0,), (0,)))
    which = which_ref[0]
    parts = []
    for j in range(halves[0].shape[1] // width):
        span = slice(j * width, (j + 1) * width)
        for k in range(ratio):
            block = halves[0][:width, span]
            for shift in range(1, ratio):
                block = jnp.where(
                    (which + shift) % ratio == k, halves[shift][:width, span], block
                )
            parts.append(block)
    image = dot(inverse, jnp.concatenate(parts, axis=1), ((1,), (0,)))
    left = stack_left(2.0 * image - 4.0 * removed)
    right = right_ref[...]
    count = sems.shape[0] - 1
    chunk = begun_ref.shape[0] // count
    w_buffer_ref[...] = 2.0 * (image - removed)
    copies = [pltpu.make_async_copy(w_buffer_ref, w_ref, sems.at[count])]
    copies[-1].start()
    for i in range(count):
        span = slice(i * chunk, (i + 1) * chunk)
        buffer_ref[span, :] = begun_ref[span, :] - dot16(left[:, span], right, ((0,), (0,)))
        copies.append(
            pltpu.make_async_copy(buffer_ref.at[span, :], updated_ref.at[span, :], sems.at[i])
        )
        copies[-1].start()
    for copy in copies:
        copy.wait()


def shape(*dims, dtype=jnp.float32):
    return jax.ShapeDtypeStruct(dims, dtype)


def call(kernel, outs, args, in_specs=None, out_specs=None, scratch=(), flops=0):
    return pl.pallas_call(
        kernel,
        out_shape=outs,
        in_specs=in_specs or [VMEM] * len(args),
        out_specs=out_specs or ((VMEM,) * len(outs) if isinstance(outs, tuple) else VMEM),
        scratch_shapes=scratch,
        compiler_params=PARAMS,
        cost_estimate=pl.CostEstimate(flops=flops, bytes_accessed=1 << 18, transcendentals=0),
    )(*args)


def local(matrix, panel):
    n_row, n_col = lax.axis_size("row"), lax.axis_size("col")
    ratio = n_col // n_row
    rows, width = panel.shape
    cols = matrix.shape[1]
    which = (lax.axis_index("col") // n_row).astype(jnp.int32).reshape(1)
    chunks = 8

    mine, panel_t, terms, gram, kept = call(
        functools.partial(panel_kernel, ratio),
        (
            shape(width, cols),
            shape(width, rows),
            shape(3 * width, rows, dtype=jnp.bfloat16),
            shape(STRIP, cols),
            shape(rows, cols),
        ),
        (
            which,
            pltpu.with_memory_space_constraint(panel.T, pltpu.HBM),
            pltpu.with_memory_space_constraint(matrix, pltpu.HBM),
        ),
        in_specs=[SMEM, HBM, HBM],
        scratch=[pltpu.SemaphoreType.DMA((2 * chunks,))],
        flops=1 << 28,
    )
    message = call(
        product_kernel, shape(width + STRIP, cols), (terms, kept, gram), flops=1 << 30
    )
    apart = lax.axis_index("row") ^ (lax.axis_index("col") % n_row)
    held = mine
    bit = n_row // 2
    while bit > 1:
        held = jnp.where(apart & bit != 0, spread_hop(held, bit), held)
        bit //= 2
    message, held = lax.optimization_barrier((message, held))
    received = spread_hop(held, 1)
    takes = (apart & 1).astype(jnp.int32).reshape(1)
    step = 1
    while 2 * step < n_row:
        message = message + partner(message, "row", step)
        step *= 2
    last = partner(message, "row", step)
    product_cols, gram = call(
        finish_kernel, (shape(width, cols), shape(width, width)), (last, message), flops=1 << 24
    )
    near = transpose_grid(product_cols)
    inner, panel_cols = call(
        inner_kernel,
        (shape(width, width), shape(width, cols)),
        (message, received, held, takes),
        in_specs=[VMEM] * 3 + [SMEM],
        flops=1 << 24,
    )
    inner = tree_sum(group_parts(inner, "col", 1, n_row))
    sent = call(
        pack_kernel,
        shape(width + STRIP, cols),
        (near, inner, partner(inner, "row", step)),
        flops=1 << 18,
    )
    halves = [sent] + [other_half(sent, shift) for shift in range(1, ratio)]
    inverse = call(factor_kernel, shape(width, width), (gram,), flops=1 << 30)
    begun, basis, basis_kept, right = call(
        basis_kernel,
        (
            shape(rows, cols),
            shape(width, rows),
            shape(width, rows),
            shape(3 * width, cols, dtype=jnp.bfloat16),
        ),
        (kept, panel_t, panel_cols, product_cols, inverse),
        flops=1 << 30,
    )
    updated, w_rows = call(
        functools.partial(update_kernel, ratio),
        (shape(rows, cols), shape(width, rows)),
        (which, begun, basis_kept, right, inverse, *halves),
        in_specs=[SMEM] + [VMEM] * (4 + ratio),
        out_specs=(HBM, HBM),
        scratch=[
            pltpu.VMEM((rows, cols), jnp.float32),
            pltpu.VMEM((width, rows), jnp.float32),
            pltpu.SemaphoreType.DMA((chunks + 1,)),
        ],
        flops=1 << 30,
    )
    return (updated, w_rows.T, basis.T)


def solution(mesh):
    return jax.shard_map(
        local,
        mesh=mesh,
        in_specs=(P("row", "col"), P("row", None)),
        out_specs=(P("row", "col"), P("row", None), P("row", None)),
        check_vma=False,
    )
```

```python
import functools

import jax
import jax.numpy as jnp
from jax import lax
from jax.experimental import pallas as pl
from jax.experimental.pallas import tpu as pltpu
from jax.sharding import PartitionSpec as P

HIGH = lax.Precision.HIGHEST
VMEM = pl.BlockSpec(memory_space=pltpu.VMEM)
SMEM = pl.BlockSpec(memory_space=pltpu.SMEM)
HBM = pl.BlockSpec(memory_space=pltpu.HBM)
PARAMS = pltpu.CompilerParams(vmem_limit_bytes=40 * 1024 * 1024)
STRIP = 8


def dot(left, right, contract, precision=HIGH):
    return lax.dot_general(
        left, right, (contract, ((), ())), precision=precision, preferred_element_type=jnp.float32
    )


def dot16(left, right, contract):
    return dot(left, right, contract, lax.Precision.DEFAULT)


def split(value, parts):
    terms = []
    for _ in range(parts):
        terms.append(value.astype(jnp.bfloat16))
        value = value - terms[-1].astype(jnp.float32)
    return terms


def partner(value, axis, step):
    size = lax.axis_size(axis)
    return lax.ppermute(value, axis, [(i, i ^ step) for i in range(size)])


def tree_sum(parts):
    while len(parts) > 1:
        parts = [parts[i] + parts[i + 1] for i in range(0, len(parts), 2)]
    return parts[0]


def group_sum(value, axis, bits, after):
    while bits:
        steps = [0]
        for bit in bits[:2]:
            steps += [step | bit for step in steps]
        parts = [partner(value, axis, step) if step else value for step in steps]
        bits = bits[2:]
        if not bits:
            parts, _ = lax.optimization_barrier((parts[::-1], after))
            parts = parts[::-1]
        value = tree_sum(parts)
    return value


def spread_rows(value, after):
    n_row, n_col = lax.axis_size("row"), lax.axis_size("col")
    apart = lax.axis_index("row") ^ (lax.axis_index("col") % n_row)
    bits = [1] + [1 << i for i in reversed(range(1, n_row.bit_length() - 1))]
    reached = [0]
    for bit in bits:
        pairs = []
        for c in range(n_col):
            for offset in reached:
                source = (c % n_row) ^ offset
                pairs.append((source * n_col + c, (source ^ bit) * n_col + c))
        reached += [offset ^ bit for offset in reached]
        received = lax.ppermute(value, ("row", "col"), pairs)
        takes = apart & bit != 0
        if bit == bits[-1]:
            return value, received, takes.astype(jnp.int32).reshape(1)
        received, _ = lax.optimization_barrier((received, after))
        value = jnp.where(takes, received, value)


def transpose_grid(value):
    n_row, n_col = lax.axis_size("row"), lax.axis_size("col")
    pairs = []
    for r in range(n_row):
        for k in range(n_col // n_row):
            for q in range(n_row):
                source = (q ^ (n_row // 2)) * n_col + k * n_row + r
                pairs.append((source, r * n_col + k * n_row + q))
    return lax.ppermute(value, ("row", "col"), pairs)


def other_half(value, shift):
    n_row, n_col = lax.axis_size("row"), lax.axis_size("col")
    pairs = [((c + shift * n_row) % n_col, c) for c in range(n_col)]
    return lax.ppermute(value, "col", pairs)


def copy_rows(source, target, sems, first, pieces):
    size = source.shape[0] // pieces
    copies = []
    for piece in range(pieces):
        span = slice(piece * size, (piece + 1) * size)
        copies.append(
            pltpu.make_async_copy(source.at[span, :], target.at[span, :], sems.at[first + piece])
        )
        copies[-1].start()
    return copies


def panel_kernel(
    ratio, which_ref, panel_ref, matrix_ref,
    mine_ref, held_ref, terms_ref, gram_ref, kept_ref, sems,
):
    width = panel_ref.shape[0]
    pieces = sems.shape[0] // 2
    panel_copies = copy_rows(panel_ref, held_ref, sems, 0, pieces)
    matrix_copies = copy_rows(matrix_ref, kept_ref, sems, pieces, pieces)
    for copy in panel_copies:
        copy.wait()
    which = which_ref[0]
    for j in range(mine_ref.shape[1] // width):
        start = j * ratio * width
        block = held_ref[:, start : start + width]
        for k in range(1, ratio):
            start += width
            block = jnp.where(which == k, held_ref[:, start : start + width], block)
        mine_ref[:, j * width : (j + 1) * width] = block
    panel = held_ref[...]
    terms_ref[...] = jnp.concatenate(split(panel, 3), axis=0)
    to_strip(dot(panel, panel, ((1,), (1,))), gram_ref)
    for copy in matrix_copies:
        copy.wait()


def product_kernel(terms_ref, matrix_ref, gram_ref, out_ref):
    width = out_ref.shape[0] - STRIP
    rows = matrix_ref.shape[0]
    chunk = 256
    total = jnp.zeros((width, matrix_ref.shape[1]), jnp.float32)
    for start in range(0, rows, chunk):
        span = slice(start, start + chunk)
        parts = split(matrix_ref[span, :], 3)
        for i, part in enumerate(parts):
            count = 3 - i
            out = dot16(terms_ref[: count * width, span], part, ((1,), (0,)))
            for t in range(count):
                total = total + out[t * width : (t + 1) * width, :]
    out_ref[:width, :] = total
    out_ref[width:, :] = gram_ref[...]


def to_strip(value, strip_ref):
    width = value.shape[0]
    for i in range(width // STRIP):
        strip_ref[:, i * width : (i + 1) * width] = value[i * STRIP : (i + 1) * STRIP, :]


def from_strip(strip, width):
    return jnp.concatenate(
        [strip[:, i * width : (i + 1) * width] for i in range(width // STRIP)], axis=0
    )


def finish_kernel(other_ref, mine_ref, product_ref, gram_ref):
    width = product_ref.shape[0]
    product_ref[...] = mine_ref[:width, :] + other_ref[:width, :]
    gram_ref[...] = from_strip(mine_ref[width:, :] + other_ref[width:, :], width)


def inner_kernel(product_ref, received_ref, held_ref, takes_ref, inner_ref, panel_cols_ref):
    panel_cols = jnp.where(takes_ref[0] != 0, received_ref[...], held_ref[...])
    panel_cols_ref[...] = panel_cols
    inner_ref[...] = dot(panel_cols, product_ref[...], ((1,), (1,)))


def factor_kernel(gram_ref, inverse_ref):
    size = inverse_ref.shape[0]
    batch = 4
    row = lax.broadcasted_iota(jnp.int32, (size, 2 * size), 0)
    lane = lax.broadcasted_iota(jnp.int32, (size, 2 * size), 1)
    eye = jnp.where(row == lane, 1.0, 0.0).astype(jnp.float32)
    table = jnp.concatenate([eye[:, :size], gram_ref[...]], axis=1)
    for first in range(0, size, batch):
        base = first // 8 * 8
        height = size - base
        low = table[base:, :]
        low_row = row[base:, :]
        cols = [
            jnp.broadcast_to(low[:, size + first + t : size + first + t + 1], (height, 2 * size))
            for t in range(batch)
        ]
        rows = [low[first - base + t : first - base + t + 1, :] for t in range(batch)]
        for t in range(batch):
            at = first - base + t
            scale = 1.0 / cols[t][at : at + 1, :]
            factor = jnp.where(low_row > first + t, cols[t] * scale, 0.0)
            for s in range(t + 1, batch):
                cols[s] = cols[s] - factor * cols[s][at : at + 1, :]
                rows[s] = rows[s] - factor[first - base + s : first - base + s + 1, :] * rows[t]
            low = low - factor * rows[t]
        table = low if base == 0 else jnp.concatenate([table[:base, :], low], axis=0)
    diagonal = jnp.sum(jnp.where(lane == row + size, table, 0.0), axis=1, keepdims=True)
    inverse_ref[...] = (table / jnp.sqrt(diagonal))[:, :size]


def stack_left(value):
    high, low = split(value, 2)
    return jnp.concatenate([high, low, high], axis=0)


def stack_right(value):
    high, low = split(value, 2)
    return jnp.concatenate([high, high, low], axis=0)


def basis_kernel(
    matrix_ref, panel_ref, panel_cols_ref, product_cols_ref, inverse_ref,
    begun_ref, basis_ref, kept_ref, right_ref,
):
    inverse = inverse_ref[...]
    basis = dot(inverse, panel_ref[...], ((1,), (0,)))
    image_cols = dot(inverse, product_cols_ref[...], ((1,), (0,)))
    basis_ref[...] = basis
    kept_ref[...] = basis
    right_ref[...] = stack_right(dot(inverse, panel_cols_ref[...], ((1,), (0,))))
    left = stack_left(basis)
    right = stack_right(2.0 * image_cols)
    chunk = 256
    for start in range(0, matrix_ref.shape[0], chunk):
        span = slice(start, start + chunk)
        begun_ref[span, :] = matrix_ref[span, :] - dot16(left[:, span], right, ((0,), (0,)))


def correction_kernel(inner_ref, other_ref, inverse_ref, basis_ref, removed_ref):
    inverse = inverse_ref[...]
    inner = inner_ref[...] + other_ref[...]
    correction = dot(dot(inverse, inner, ((1,), (0,))), inverse, ((1,), (1,)))
    removed_ref[...] = dot(correction, basis_ref[...], ((0,), (0,)))


def update_kernel(ratio, which_ref, begun_ref, removed_ref, right_ref, inverse_ref, *refs):
    halves, (updated_ref, w_ref, buffer_ref, w_buffer_ref, sems) = refs[:ratio], refs[ratio:]
    width = inverse_ref.shape[0]
    which = which_ref[0]
    parts = []
    for j in range(halves[0].shape[1] // width):
        span = slice(j * width, (j + 1) * width)
        for k in range(ratio):
            block = halves[0][:, span]
            for shift in range(1, ratio):
                block = jnp.where((which + shift) % ratio == k, halves[shift][:, span], block)
            parts.append(block)
    image = dot(inverse_ref[...], jnp.concatenate(parts, axis=1), ((1,), (0,)))
    removed = removed_ref[...]
    left = stack_left(2.0 * image - 4.0 * removed)
    right = right_ref[...]
    count = sems.shape[0] - 1
    chunk = begun_ref.shape[0] // count
    w_buffer_ref[...] = 2.0 * (image - removed)
    copies = [pltpu.make_async_copy(w_buffer_ref, w_ref, sems.at[count])]
    copies[-1].start()
    for i in range(count):
        span = slice(i * chunk, (i + 1) * chunk)
        buffer_ref[span, :] = begun_ref[span, :] - dot16(left[:, span], right, ((0,), (0,)))
        copies.append(
            pltpu.make_async_copy(buffer_ref.at[span, :], updated_ref.at[span, :], sems.at[i])
        )
        copies[-1].start()
    for copy in copies:
        copy.wait()


def shape(*dims, dtype=jnp.float32):
    return jax.ShapeDtypeStruct(dims, dtype)


def call(kernel, outs, args, in_specs=None, out_specs=None, scratch=(), flops=0):
    return pl.pallas_call(
        kernel,
        out_shape=outs,
        in_specs=in_specs or [VMEM] * len(args),
        out_specs=out_specs or ((VMEM,) * len(outs) if isinstance(outs, tuple) else VMEM),
        scratch_shapes=scratch,
        compiler_params=PARAMS,
        cost_estimate=pl.CostEstimate(flops=flops, bytes_accessed=1 << 18, transcendentals=0),
    )(*args)


def local(matrix, panel):
    n_row, n_col = lax.axis_size("row"), lax.axis_size("col")
    ratio = n_col // n_row
    rows, width = panel.shape
    cols = matrix.shape[1]
    which = (lax.axis_index("col") // n_row).astype(jnp.int32).reshape(1)
    chunks = 8

    mine, panel_t, terms, gram, kept = call(
        functools.partial(panel_kernel, ratio),
        (
            shape(width, cols),
            shape(width, rows),
            shape(3 * width, rows, dtype=jnp.bfloat16),
            shape(STRIP, cols),
            shape(rows, cols),
        ),
        (
            which,
            pltpu.with_memory_space_constraint(panel.T, pltpu.HBM),
            pltpu.with_memory_space_constraint(matrix, pltpu.HBM),
        ),
        in_specs=[SMEM, HBM, HBM],
        scratch=[pltpu.SemaphoreType.DMA((2 * chunks,))],
        flops=1 << 28,
    )
    message = call(
        product_kernel, shape(width + STRIP, cols), (terms, kept, gram), flops=1 << 30
    )
    step = 1
    while 2 * step < n_row:
        message = message + partner(message, "row", step)
        step *= 2
    last = partner(message, "row", step)
    held, received, takes = spread_rows(mine, message)
    product_cols, gram = call(
        finish_kernel, (shape(width, cols), shape(width, width)), (last, message), flops=1 << 24
    )
    near = transpose_grid(product_cols)
    inner, panel_cols = call(
        inner_kernel,
        (shape(width, width), shape(width, cols)),
        (product_cols, received, held, takes),
        in_specs=[VMEM] * 3 + [SMEM],
        flops=1 << 24,
    )
    col_bits = [1 << i for i in range(n_col.bit_length() - 1)]
    inner = group_sum(inner, "col", col_bits[1:], near)
    inner, gram = lax.optimization_barrier((inner, gram))
    halves = [near] + [other_half(near, shift) for shift in range(1, ratio)]
    inverse = call(factor_kernel, shape(width, width), (gram,), flops=1 << 30)
    begun, basis, basis_kept, right = call(
        basis_kernel,
        (
            shape(rows, cols),
            shape(width, rows),
            shape(width, rows),
            shape(3 * width, cols, dtype=jnp.bfloat16),
        ),
        (kept, panel_t, panel_cols, product_cols, inverse),
        flops=1 << 30,
    )
    removed = call(
        correction_kernel,
        shape(width, rows),
        (inner, partner(inner, "col", 1), inverse, basis_kept),
        flops=1 << 24,
    )
    updated, w_rows = call(
        functools.partial(update_kernel, ratio),
        (shape(rows, cols), shape(width, rows)),
        (which, begun, removed, right, inverse, *halves),
        in_specs=[SMEM] + [VMEM] * (4 + ratio),
        out_specs=(HBM, HBM),
        scratch=[
            pltpu.VMEM((rows, cols), jnp.float32),
            pltpu.VMEM((width, rows), jnp.float32),
            pltpu.SemaphoreType.DMA((chunks + 1,)),
        ],
        flops=1 << 30,
    )
    return (updated, w_rows.T, basis.T)


def solution(mesh):
    return jax.shard_map(
        local,
        mesh=mesh,
        in_specs=(P("row", "col"), P("row", None)),
        out_specs=(P("row", "col"), P("row", None), P("row", None)),
        check_vma=False,
    )
```

```python
import functools

import jax
import jax.numpy as jnp
from jax import lax
from jax.experimental import pallas as pl
from jax.experimental.pallas import tpu as pltpu
from jax.sharding import PartitionSpec as P

HIGH = lax.Precision.HIGHEST
VMEM = pl.BlockSpec(memory_space=pltpu.VMEM)
SMEM = pl.BlockSpec(memory_space=pltpu.SMEM)
HBM = pl.BlockSpec(memory_space=pltpu.HBM)
PARAMS = pltpu.CompilerParams(vmem_limit_bytes=40 * 1024 * 1024)
STRIP = 8


def dot(left, right, contract, precision=HIGH):
    return lax.dot_general(
        left, right, (contract, ((), ())), precision=precision, preferred_element_type=jnp.float32
    )


def dot16(left, right, contract):
    return dot(left, right, contract, lax.Precision.DEFAULT)


def split(value, parts):
    terms = []
    for _ in range(parts):
        terms.append(value.astype(jnp.bfloat16))
        value = value - terms[-1].astype(jnp.float32)
    return terms


def partner(value, axis, step):
    size = lax.axis_size(axis)
    return lax.ppermute(value, axis, [(i, i ^ step) for i in range(size)])


def spread_rows(value, after):
    n_row, n_col = lax.axis_size("row"), lax.axis_size("col")
    apart = lax.axis_index("row") ^ (lax.axis_index("col") % n_row)
    bits = [1] + [1 << i for i in reversed(range(1, n_row.bit_length() - 1))]
    reached = [0]
    for bit in bits:
        pairs = []
        for c in range(n_col):
            for offset in reached:
                source = (c % n_row) ^ offset
                pairs.append((source * n_col + c, (source ^ bit) * n_col + c))
        reached += [offset ^ bit for offset in reached]
        received = lax.ppermute(value, ("row", "col"), pairs)
        takes = apart & bit != 0
        if bit == bits[-1]:
            return value, received, takes.astype(jnp.int32).reshape(1)
        received, _ = lax.optimization_barrier((received, after))
        value = jnp.where(takes, received, value)


def transpose_grid(value):
    n_row, n_col = lax.axis_size("row"), lax.axis_size("col")
    pairs = []
    for r in range(n_row):
        for k in range(n_col // n_row):
            for q in range(n_row):
                source = (q ^ (n_row // 2)) * n_col + k * n_row + r
                pairs.append((source, r * n_col + k * n_row + q))
    return lax.ppermute(value, ("row", "col"), pairs)


def other_half(value, shift):
    n_row, n_col = lax.axis_size("row"), lax.axis_size("col")
    pairs = [((c + shift * n_row) % n_col, c) for c in range(n_col)]
    return lax.ppermute(value, "col", pairs)


def copy_rows(source, target, sems, first, pieces):
    size = source.shape[0] // pieces
    copies = []
    for piece in range(pieces):
        span = slice(piece * size, (piece + 1) * size)
        copies.append(
            pltpu.make_async_copy(source.at[span, :], target.at[span, :], sems.at[first + piece])
        )
        copies[-1].start()
    return copies


def panel_kernel(
    ratio, which_ref, panel_ref, matrix_ref,
    mine_ref, held_ref, terms_ref, gram_ref, kept_ref, sems,
):
    width = panel_ref.shape[0]
    pieces = sems.shape[0] // 2
    panel_copies = copy_rows(panel_ref, held_ref, sems, 0, pieces)
    matrix_copies = copy_rows(matrix_ref, kept_ref, sems, pieces, pieces)
    for copy in panel_copies:
        copy.wait()
    which = which_ref[0]
    for j in range(mine_ref.shape[1] // width):
        start = j * ratio * width
        block = held_ref[:, start : start + width]
        for k in range(1, ratio):
            start += width
            block = jnp.where(which == k, held_ref[:, start : start + width], block)
        mine_ref[:, j * width : (j + 1) * width] = block
    panel = held_ref[...]
    terms_ref[...] = jnp.concatenate(split(panel, 3), axis=0)
    to_strip(dot(panel, panel, ((1,), (1,))), gram_ref)
    for copy in matrix_copies:
        copy.wait()


def product_kernel(terms_ref, matrix_ref, gram_ref, out_ref):
    width = out_ref.shape[0] - STRIP
    rows = matrix_ref.shape[0]
    chunk = 256
    total = jnp.zeros((width, matrix_ref.shape[1]), jnp.float32)
    for start in range(0, rows, chunk):
        span = slice(start, start + chunk)
        parts = split(matrix_ref[span, :], 3)
        for i, part in enumerate(parts):
            count = 3 - i
            out = dot16(terms_ref[: count * width, span], part, ((1,), (0,)))
            for t in range(count):
                total = total + out[t * width : (t + 1) * width, :]
    out_ref[:width, :] = total
    out_ref[width:, :] = gram_ref[...]


def to_strip(value, strip_ref):
    width = value.shape[0]
    for i in range(width // STRIP):
        strip_ref[:, i * width : (i + 1) * width] = value[i * STRIP : (i + 1) * STRIP, :]


def from_strip(strip, width):
    return jnp.concatenate(
        [strip[:, i * width : (i + 1) * width] for i in range(width // STRIP)], axis=0
    )


def finish_kernel(other_ref, mine_ref, product_ref, gram_ref):
    width = product_ref.shape[0]
    product_ref[...] = mine_ref[:width, :] + other_ref[:width, :]
    gram_ref[...] = from_strip(mine_ref[width:, :] + other_ref[width:, :], width)


def inner_kernel(product_ref, received_ref, held_ref, takes_ref, inners_ref, panel_cols_ref):
    panel_cols = jnp.where(takes_ref[0] != 0, received_ref[...], held_ref[...])
    panel_cols_ref[...] = panel_cols
    inner = dot(panel_cols, product_ref[...], ((1,), (1,)))
    for row in range(0, inners_ref.shape[0], STRIP):
        to_strip(inner, inners_ref.at[row : row + STRIP, :])


def factor_kernel(gram_ref, inverse_ref):
    size = inverse_ref.shape[0]
    batch = 4
    row = lax.broadcasted_iota(jnp.int32, (size, 2 * size), 0)
    lane = lax.broadcasted_iota(jnp.int32, (size, 2 * size), 1)
    eye = jnp.where(row == lane, 1.0, 0.0).astype(jnp.float32)
    table = jnp.concatenate([eye[:, :size], gram_ref[...]], axis=1)
    for first in range(0, size, batch):
        base = first // 8 * 8
        height = size - base
        low = table[base:, :]
        low_row = row[base:, :]
        cols = [
            jnp.broadcast_to(low[:, size + first + t : size + first + t + 1], (height, 2 * size))
            for t in range(batch)
        ]
        rows = [low[first - base + t : first - base + t + 1, :] for t in range(batch)]
        for t in range(batch):
            at = first - base + t
            scale = 1.0 / cols[t][at : at + 1, :]
            factor = jnp.where(low_row > first + t, cols[t] * scale, 0.0)
            for s in range(t + 1, batch):
                cols[s] = cols[s] - factor * cols[s][at : at + 1, :]
                rows[s] = rows[s] - factor[first - base + s : first - base + s + 1, :] * rows[t]
            low = low - factor * rows[t]
        table = low if base == 0 else jnp.concatenate([table[:base, :], low], axis=0)
    diagonal = jnp.sum(jnp.where(lane == row + size, table, 0.0), axis=1, keepdims=True)
    inverse_ref[...] = (table / jnp.sqrt(diagonal))[:, :size]


def stack_left(value):
    high, low = split(value, 2)
    return jnp.concatenate([high, low, high], axis=0)


def stack_right(value):
    high, low = split(value, 2)
    return jnp.concatenate([high, high, low], axis=0)


def basis_kernel(
    matrix_ref, panel_ref, panel_cols_ref, product_cols_ref, inverse_ref,
    begun_ref, basis_ref, kept_ref, right_ref,
):
    inverse = inverse_ref[...]
    basis = dot(inverse, panel_ref[...], ((1,), (0,)))
    image_cols = dot(inverse, product_cols_ref[...], ((1,), (0,)))
    basis_ref[...] = basis
    kept_ref[...] = basis
    right_ref[...] = stack_right(dot(inverse, panel_cols_ref[...], ((1,), (0,))))
    left = stack_left(basis)
    right = stack_right(2.0 * image_cols)
    chunk = 256
    for start in range(0, matrix_ref.shape[0], chunk):
        span = slice(start, start + chunk)
        begun_ref[span, :] = matrix_ref[span, :] - dot16(left[:, span], right, ((0,), (0,)))


def correction_kernel(inners_ref, inverse_ref, basis_ref, removed_ref):
    inverse = inverse_ref[...]
    strip = inners_ref[:STRIP, :]
    for row in range(STRIP, inners_ref.shape[0], STRIP):
        strip = strip + inners_ref[row : row + STRIP, :]
    inner = from_strip(strip, inverse.shape[0])
    correction = dot(dot(inverse, inner, ((1,), (0,))), inverse, ((1,), (1,)))
    removed_ref[...] = dot(correction, basis_ref[...], ((0,), (0,)))


def update_kernel(ratio, which_ref, begun_ref, removed_ref, right_ref, inverse_ref, *refs):
    halves, (updated_ref, w_ref, buffer_ref, w_buffer_ref, sems) = refs[:ratio], refs[ratio:]
    width = inverse_ref.shape[0]
    which = which_ref[0]
    parts = []
    for j in range(halves[0].shape[1] // width):
        span = slice(j * width, (j + 1) * width)
        for k in range(ratio):
            block = halves[0][:, span]
            for shift in range(1, ratio):
                block = jnp.where((which + shift) % ratio == k, halves[shift][:, span], block)
            parts.append(block)
    image = dot(inverse_ref[...], jnp.concatenate(parts, axis=1), ((1,), (0,)))
    removed = removed_ref[...]
    left = stack_left(2.0 * image - 4.0 * removed)
    right = right_ref[...]
    count = sems.shape[0] - 1
    chunk = begun_ref.shape[0] // count
    w_buffer_ref[...] = 2.0 * (image - removed)
    copies = [pltpu.make_async_copy(w_buffer_ref, w_ref, sems.at[count])]
    copies[-1].start()
    for i in range(count):
        span = slice(i * chunk, (i + 1) * chunk)
        buffer_ref[span, :] = begun_ref[span, :] - dot16(left[:, span], right, ((0,), (0,)))
        copies.append(
            pltpu.make_async_copy(buffer_ref.at[span, :], updated_ref.at[span, :], sems.at[i])
        )
        copies[-1].start()
    for copy in copies:
        copy.wait()


def shape(*dims, dtype=jnp.float32):
    return jax.ShapeDtypeStruct(dims, dtype)


def call(kernel, outs, args, in_specs=None, out_specs=None, scratch=(), flops=0):
    return pl.pallas_call(
        kernel,
        out_shape=outs,
        in_specs=in_specs or [VMEM] * len(args),
        out_specs=out_specs or ((VMEM,) * len(outs) if isinstance(outs, tuple) else VMEM),
        scratch_shapes=scratch,
        compiler_params=PARAMS,
        cost_estimate=pl.CostEstimate(flops=flops, bytes_accessed=1 << 18, transcendentals=0),
    )(*args)


def local(matrix, panel):
    n_row, n_col = lax.axis_size("row"), lax.axis_size("col")
    ratio = n_col // n_row
    rows, width = panel.shape
    cols = matrix.shape[1]
    which = (lax.axis_index("col") // n_row).astype(jnp.int32).reshape(1)
    chunks = 8

    mine, panel_t, terms, gram, kept = call(
        functools.partial(panel_kernel, ratio),
        (
            shape(width, cols),
            shape(width, rows),
            shape(3 * width, rows, dtype=jnp.bfloat16),
            shape(STRIP, cols),
            shape(rows, cols),
        ),
        (
            which,
            pltpu.with_memory_space_constraint(panel.T, pltpu.HBM),
            pltpu.with_memory_space_constraint(matrix, pltpu.HBM),
        ),
        in_specs=[SMEM, HBM, HBM],
        scratch=[pltpu.SemaphoreType.DMA((2 * chunks,))],
        flops=1 << 28,
    )
    message = call(
        product_kernel, shape(width + STRIP, cols), (terms, kept, gram), flops=1 << 30
    )
    step = 1
    while 2 * step < n_row:
        message = message + partner(message, "row", step)
        step *= 2
    last = partner(message, "row", step)
    held, received, takes = spread_rows(mine, message)
    product_cols, gram = call(
        finish_kernel, (shape(width, cols), shape(width, width)), (last, message), flops=1 << 24
    )
    near = transpose_grid(product_cols)
    inners, panel_cols = call(
        inner_kernel,
        (shape(n_col * STRIP, cols), shape(width, cols)),
        (product_cols, received, held, takes),
        in_specs=[VMEM] * 3 + [SMEM],
        flops=1 << 24,
    )
    inners = lax.all_to_all(inners, "col", 0, 0, tiled=True)
    halves = [near] + [other_half(near, shift) for shift in range(1, ratio)]
    inverse = call(factor_kernel, shape(width, width), (gram,), flops=1 << 30)
    begun, basis, basis_kept, right = call(
        basis_kernel,
        (
            shape(rows, cols),
            shape(width, rows),
            shape(width, rows),
            shape(3 * width, cols, dtype=jnp.bfloat16),
        ),
        (kept, panel_t, panel_cols, product_cols, inverse),
        flops=1 << 30,
    )
    removed = call(
        correction_kernel,
        shape(width, rows),
        (inners, inverse, basis_kept),
        flops=1 << 24,
    )
    updated, w_rows = call(
        functools.partial(update_kernel, ratio),
        (shape(rows, cols), shape(width, rows)),
        (which, begun, removed, right, inverse, *halves),
        in_specs=[SMEM] + [VMEM] * (4 + ratio),
        out_specs=(HBM, HBM),
        scratch=[
            pltpu.VMEM((rows, cols), jnp.float32),
            pltpu.VMEM((width, rows), jnp.float32),
            pltpu.SemaphoreType.DMA((chunks + 1,)),
        ],
        flops=1 << 30,
    )
    return (updated, w_rows.T, basis.T)


def solution(mesh):
    return jax.shard_map(
        local,
        mesh=mesh,
        in_specs=(P("row", "col"), P("row", None)),
        out_specs=(P("row", "col"), P("row", None), P("row", None)),
        check_vma=False,
    )
```

```python
import functools

import jax
import jax.numpy as jnp
from jax import lax
from jax.experimental import pallas as pl
from jax.experimental.pallas import tpu as pltpu
from jax.sharding import PartitionSpec as P

HIGH = lax.Precision.HIGHEST
VMEM = pl.BlockSpec(memory_space=pltpu.VMEM)
SMEM = pl.BlockSpec(memory_space=pltpu.SMEM)
HBM = pl.BlockSpec(memory_space=pltpu.HBM)
PARAMS = pltpu.CompilerParams(vmem_limit_bytes=40 * 1024 * 1024)
STRIP = 8


def dot(left, right, contract, precision=HIGH):
    return lax.dot_general(
        left, right, (contract, ((), ())), precision=precision, preferred_element_type=jnp.float32
    )


def dot16(left, right, contract):
    return dot(left, right, contract, lax.Precision.DEFAULT)


def split(value, parts):
    terms = []
    for _ in range(parts):
        terms.append(value.astype(jnp.bfloat16))
        value = value - terms[-1].astype(jnp.float32)
    return terms


def partner(value, axis, step):
    size = lax.axis_size(axis)
    return lax.ppermute(value, axis, [(i, i ^ step) for i in range(size)])


def tree_sum(parts):
    while len(parts) > 1:
        parts = [parts[i] + parts[i + 1] for i in range(0, len(parts), 2)]
    return parts[0]


def group_parts(value, axis, low, high):
    parts = [value]
    while low < high:
        value = tree_sum(parts)
        parts = [value, partner(value, axis, low)]
        low *= 2
    return parts


def spread_rows(value, after):
    n_row, n_col = lax.axis_size("row"), lax.axis_size("col")
    apart = lax.axis_index("row") ^ (lax.axis_index("col") % n_row)
    bits = [1] + [1 << i for i in reversed(range(1, n_row.bit_length() - 1))]
    reached = [0]
    for bit in bits:
        pairs = []
        for c in range(n_col):
            for offset in reached:
                source = (c % n_row) ^ offset
                pairs.append((source * n_col + c, (source ^ bit) * n_col + c))
        reached += [offset ^ bit for offset in reached]
        received = lax.ppermute(value, ("row", "col"), pairs)
        takes = apart & bit != 0
        if bit == bits[-1]:
            return value, received, takes.astype(jnp.int32).reshape(1)
        received, _ = lax.optimization_barrier((received, after))
        value = jnp.where(takes, received, value)


def transpose_grid(value):
    n_row, n_col = lax.axis_size("row"), lax.axis_size("col")
    pairs = []
    for r in range(n_row):
        for k in range(n_col // n_row):
            for q in range(n_row):
                source = (q ^ (n_row // 2)) * n_col + k * n_row + r
                pairs.append((source, r * n_col + k * n_row + q))
    return lax.ppermute(value, ("row", "col"), pairs)


def other_half(value, shift):
    n_row, n_col = lax.axis_size("row"), lax.axis_size("col")
    pairs = [((c + shift * n_row) % n_col, c) for c in range(n_col)]
    return lax.ppermute(value, "col", pairs)


def copy_rows(source, target, sems, first, pieces):
    size = source.shape[0] // pieces
    copies = []
    for piece in range(pieces):
        span = slice(piece * size, (piece + 1) * size)
        copies.append(
            pltpu.make_async_copy(source.at[span, :], target.at[span, :], sems.at[first + piece])
        )
        copies[-1].start()
    return copies


def panel_kernel(
    ratio, which_ref, panel_ref, matrix_ref,
    mine_ref, held_ref, terms_ref, gram_ref, kept_ref, sems,
):
    width = panel_ref.shape[0]
    pieces = panel_ref.shape[0] // STRIP
    panel_copies = copy_rows(panel_ref, held_ref, sems, 0, pieces)
    matrix_copies = copy_rows(matrix_ref, kept_ref, sems, pieces, sems.shape[0] - pieces)
    for copy in panel_copies:
        copy.wait()
    which = which_ref[0]
    for j in range(mine_ref.shape[1] // width):
        start = j * ratio * width
        block = held_ref[:, start : start + width]
        for k in range(1, ratio):
            start += width
            block = jnp.where(which == k, held_ref[:, start : start + width], block)
        mine_ref[:, j * width : (j + 1) * width] = block
    panel = held_ref[...]
    terms_ref[...] = jnp.concatenate(split(panel, 3), axis=0)
    to_strip(dot(panel, panel, ((1,), (1,))), gram_ref)
    for copy in matrix_copies:
        copy.wait()


def product_kernel(terms_ref, matrix_ref, gram_ref, out_ref):
    width = out_ref.shape[0] - STRIP
    rows = matrix_ref.shape[0]
    chunk = 256
    total = jnp.zeros((width, matrix_ref.shape[1]), jnp.float32)
    for start in range(0, rows, chunk):
        span = slice(start, start + chunk)
        parts = split(matrix_ref[span, :], 3)
        for i, part in enumerate(parts):
            count = 3 - i
            out = dot16(terms_ref[: count * width, span], part, ((1,), (0,)))
            for t in range(count):
                total = total + out[t * width : (t + 1) * width, :]
    out_ref[:width, :] = total
    out_ref[width:, :] = gram_ref[...]


def to_strip(value, strip_ref):
    width = value.shape[0]
    for i in range(width // STRIP):
        strip_ref[:, i * width : (i + 1) * width] = value[i * STRIP : (i + 1) * STRIP, :]


def from_strip(strip, width):
    return jnp.concatenate(
        [strip[:, i * width : (i + 1) * width] for i in range(width // STRIP)], axis=0
    )


def finish_kernel(other_ref, mine_ref, product_ref, gram_ref):
    width = product_ref.shape[0]
    product_ref[...] = mine_ref[:width, :] + other_ref[:width, :]
    gram_ref[...] = from_strip(mine_ref[width:, :] + other_ref[width:, :], width)


def inner_kernel(product_ref, received_ref, held_ref, takes_ref, inner_ref, panel_cols_ref):
    panel_cols = jnp.where(takes_ref[0] != 0, received_ref[...], held_ref[...])
    panel_cols_ref[...] = panel_cols
    inner_ref[...] = dot(panel_cols, product_ref[...], ((1,), (1,)))


def pack_kernel(near_ref, *refs):
    parts, sent_ref = refs[:-1], refs[-1]
    width = near_ref.shape[0]
    sent_ref[:width, :] = near_ref[...]
    to_strip(tree_sum([part[...] for part in parts]), sent_ref.at[width:, :])


def factor_kernel(gram_ref, inverse_ref):
    size = inverse_ref.shape[0]
    batch = 4
    row = lax.broadcasted_iota(jnp.int32, (size, 2 * size), 0)
    lane = lax.broadcasted_iota(jnp.int32, (size, 2 * size), 1)
    eye = jnp.where(row == lane, 1.0, 0.0).astype(jnp.float32)
    table = jnp.concatenate([eye[:, :size], gram_ref[...]], axis=1)
    for first in range(0, size, batch):
        base = first // 8 * 8
        height = size - base
        low = table[base:, :]
        low_row = row[base:, :]
        cols = [
            jnp.broadcast_to(low[:, size + first + t : size + first + t + 1], (height, 2 * size))
            for t in range(batch)
        ]
        rows = [low[first - base + t : first - base + t + 1, :] for t in range(batch)]
        for t in range(batch):
            at = first - base + t
            scale = 1.0 / cols[t][at : at + 1, :]
            factor = jnp.where(low_row > first + t, cols[t] * scale, 0.0)
            for s in range(t + 1, batch):
                cols[s] = cols[s] - factor * cols[s][at : at + 1, :]
                rows[s] = rows[s] - factor[first - base + s : first - base + s + 1, :] * rows[t]
            low = low - factor * rows[t]
        table = low if base == 0 else jnp.concatenate([table[:base, :], low], axis=0)
    diagonal = jnp.sum(jnp.where(lane == row + size, table, 0.0), axis=1, keepdims=True)
    inverse_ref[...] = (table / jnp.sqrt(diagonal))[:, :size]


def stack_left(value):
    high, low = split(value, 2)
    return jnp.concatenate([high, low, high], axis=0)


def stack_right(value):
    high, low = split(value, 2)
    return jnp.concatenate([high, high, low], axis=0)


def basis_kernel(
    matrix_ref, panel_ref, panel_cols_ref, product_cols_ref, inverse_ref,
    begun_ref, basis_ref, kept_ref, right_ref,
):
    inverse = inverse_ref[...]
    basis = dot(inverse, panel_ref[...], ((1,), (0,)))
    image_cols = dot(inverse, product_cols_ref[...], ((1,), (0,)))
    basis_ref[...] = basis
    kept_ref[...] = basis
    right_ref[...] = stack_right(dot(inverse, panel_cols_ref[...], ((1,), (0,))))
    left = stack_left(basis)
    right = stack_right(2.0 * image_cols)
    chunk = 256
    for start in range(0, matrix_ref.shape[0], chunk):
        span = slice(start, start + chunk)
        begun_ref[span, :] = matrix_ref[span, :] - dot16(left[:, span], right, ((0,), (0,)))


def update_kernel(
    ratio, which_ref, begun_ref, basis_ref, right_ref, inverse_ref, *refs
):
    halves, (updated_ref, w_ref, buffer_ref, w_buffer_ref, sems) = refs[:ratio], refs[ratio:]
    inverse = inverse_ref[...]
    width = inverse.shape[0]
    strip = halves[0][width:, :]
    for half in halves[1:]:
        strip = strip + half[width:, :]
    correction = dot(
        dot(inverse, from_strip(strip, width), ((1,), (0,))), inverse, ((1,), (1,))
    )
    removed = dot(correction, basis_ref[...], ((0,), (0,)))
    which = which_ref[0]
    parts = []
    for j in range(halves[0].shape[1] // width):
        span = slice(j * width, (j + 1) * width)
        for k in range(ratio):
            block = halves[0][:width, span]
            for shift in range(1, ratio):
                block = jnp.where(
                    (which + shift) % ratio == k, halves[shift][:width, span], block
                )
            parts.append(block)
    image = dot(inverse, jnp.concatenate(parts, axis=1), ((1,), (0,)))
    left = stack_left(2.0 * image - 4.0 * removed)
    right = right_ref[...]
    count = sems.shape[0] - 1
    chunk = 2 * begun_ref.shape[0] // count
    w_buffer_ref[...] = 2.0 * (image - removed)
    copies = [pltpu.make_async_copy(w_buffer_ref, w_ref, sems.at[count])]
    copies[-1].start()
    for i in range(0, count, 2):
        span = slice(i // 2 * chunk, (i // 2 + 1) * chunk)
        buffer_ref[span, :] = begun_ref[span, :] - dot16(left[:, span], right, ((0,), (0,)))
        for part in (i, i + 1):
            span = slice(part * chunk // 2, (part + 1) * chunk // 2)
            copies.append(
                pltpu.make_async_copy(
                    buffer_ref.at[span, :], updated_ref.at[span, :], sems.at[part]
                )
            )
            copies[-1].start()
    for copy in copies:
        copy.wait()


def shape(*dims, dtype=jnp.float32):
    return jax.ShapeDtypeStruct(dims, dtype)


def call(kernel, outs, args, in_specs=None, out_specs=None, scratch=(), flops=0):
    return pl.pallas_call(
        kernel,
        out_shape=outs,
        in_specs=in_specs or [VMEM] * len(args),
        out_specs=out_specs or ((VMEM,) * len(outs) if isinstance(outs, tuple) else VMEM),
        scratch_shapes=scratch,
        compiler_params=PARAMS,
        cost_estimate=pl.CostEstimate(flops=flops, bytes_accessed=1 << 18, transcendentals=0),
    )(*args)


def local(matrix, panel):
    n_row, n_col = lax.axis_size("row"), lax.axis_size("col")
    ratio = n_col // n_row
    rows, width = panel.shape
    cols = matrix.shape[1]
    which = (lax.axis_index("col") // n_row).astype(jnp.int32).reshape(1)
    chunks = 16

    mine, panel_t, terms, gram, kept = call(
        functools.partial(panel_kernel, ratio),
        (
            shape(width, cols),
            shape(width, rows),
            shape(3 * width, rows, dtype=jnp.bfloat16),
            shape(STRIP, cols),
            shape(rows, cols),
        ),
        (
            which,
            pltpu.with_memory_space_constraint(panel.T, pltpu.HBM),
            pltpu.with_memory_space_constraint(matrix, pltpu.HBM),
        ),
        in_specs=[SMEM, HBM, HBM],
        scratch=[pltpu.SemaphoreType.DMA((width // STRIP + chunks,))],
        flops=1 << 28,
    )
    message = call(
        product_kernel, shape(width + STRIP, cols), (terms, kept, gram), flops=1 << 30
    )
    step = 1
    while 2 * step < n_row:
        message = message + partner(message, "row", step)
        step *= 2
    last = partner(message, "row", step)
    held, received, takes = spread_rows(mine, message)
    product_cols, gram = call(
        finish_kernel, (shape(width, cols), shape(width, width)), (last, message), flops=1 << 24
    )
    near = transpose_grid(product_cols)
    inner, panel_cols = call(
        inner_kernel,
        (shape(width, width), shape(width, cols)),
        (product_cols, received, held, takes),
        in_specs=[VMEM] * 3 + [SMEM],
        flops=1 << 24,
    )
    parts = group_parts(inner, "col", 1, n_row)
    sent = call(pack_kernel, shape(width + STRIP, cols), (near, *parts), flops=1 << 18)
    halves = [sent] + [other_half(sent, shift) for shift in range(1, ratio)]
    inverse = call(factor_kernel, shape(width, width), (gram,), flops=1 << 30)
    begun, basis, basis_kept, right = call(
        basis_kernel,
        (
            shape(rows, cols),
            shape(width, rows),
            shape(width, rows),
            shape(3 * width, cols, dtype=jnp.bfloat16),
        ),
        (kept, panel_t, panel_cols, product_cols, inverse),
        flops=1 << 30,
    )
    updated, w_rows = call(
        functools.partial(update_kernel, ratio),
        (shape(rows, cols), shape(width, rows)),
        (which, begun, basis_kept, right, inverse, *halves),
        in_specs=[SMEM] + [VMEM] * (4 + ratio),
        out_specs=(HBM, HBM),
        scratch=[
            pltpu.VMEM((rows, cols), jnp.float32),
            pltpu.VMEM((width, rows), jnp.float32),
            pltpu.SemaphoreType.DMA((chunks + 1,)),
        ],
        flops=1 << 30,
    )
    return (updated, w_rows.T, basis.T)


def solution(mesh):
    return jax.shard_map(
        local,
        mesh=mesh,
        in_specs=(P("row", "col"), P("row", None)),
        out_specs=(P("row", "col"), P("row", None), P("row", None)),
        check_vma=False,
    )
```

```python
import functools

import jax
import jax.numpy as jnp
from jax import lax
from jax.experimental import pallas as pl
from jax.experimental.pallas import tpu as pltpu
from jax.sharding import PartitionSpec as P

HIGH = lax.Precision.HIGHEST
VMEM = pl.BlockSpec(memory_space=pltpu.VMEM)
SMEM = pl.BlockSpec(memory_space=pltpu.SMEM)
HBM = pl.BlockSpec(memory_space=pltpu.HBM)
PARAMS = pltpu.CompilerParams(vmem_limit_bytes=40 * 1024 * 1024)
STRIP = 8


def dot(left, right, contract, precision=HIGH):
    return lax.dot_general(
        left, right, (contract, ((), ())), precision=precision, preferred_element_type=jnp.float32
    )


def dot16(left, right, contract):
    return dot(left, right, contract, lax.Precision.DEFAULT)


def split(value, parts):
    terms = []
    for _ in range(parts):
        terms.append(value.astype(jnp.bfloat16))
        value = value - terms[-1].astype(jnp.float32)
    return terms


def partner(value, axis, step):
    size = lax.axis_size(axis)
    return lax.ppermute(value, axis, [(i, i ^ step) for i in range(size)])


def spread_rows(value, after):
    n_row, n_col = lax.axis_size("row"), lax.axis_size("col")
    apart = lax.axis_index("row") ^ (lax.axis_index("col") % n_row)
    bits = [1] + [1 << i for i in reversed(range(1, n_row.bit_length() - 1))]
    reached = [0]
    for bit in bits:
        pairs = []
        for c in range(n_col):
            for offset in reached:
                source = (c % n_row) ^ offset
                pairs.append((source * n_col + c, (source ^ bit) * n_col + c))
        reached += [offset ^ bit for offset in reached]
        received = lax.ppermute(value, ("row", "col"), pairs)
        takes = apart & bit != 0
        if bit == bits[-1]:
            return value, received, takes.astype(jnp.int32).reshape(1)
        received, _ = lax.optimization_barrier((received, after))
        value = jnp.where(takes, received, value)


def transpose_grid(value, shift):
    n_row, n_col = lax.axis_size("row"), lax.axis_size("col")
    ratio = n_col // n_row
    pairs = []
    for r in range(n_row):
        for k in range(ratio):
            for q in range(n_row):
                column = (k + shift) % ratio * n_row + r
                pairs.append(((q ^ (n_row // 2)) * n_col + column, r * n_col + k * n_row + q))
    return lax.ppermute(value, ("row", "col"), pairs)


def copy_rows(source, target, sems, first, pieces):
    size = source.shape[0] // pieces
    copies = []
    for piece in range(pieces):
        span = slice(piece * size, (piece + 1) * size)
        copies.append(
            pltpu.make_async_copy(source.at[span, :], target.at[span, :], sems.at[first + piece])
        )
        copies[-1].start()
    return copies


def panel_kernel(
    ratio, which_ref, panel_ref, matrix_ref,
    mine_ref, held_ref, terms_ref, gram_ref, kept_ref, sems,
):
    width = panel_ref.shape[0]
    pieces = sems.shape[0] // 2
    panel_copies = copy_rows(panel_ref, held_ref, sems, 0, pieces)
    matrix_copies = copy_rows(matrix_ref, kept_ref, sems, pieces, pieces)
    for copy in panel_copies:
        copy.wait()
    which = which_ref[0]
    for j in range(mine_ref.shape[1] // width):
        start = j * ratio * width
        block = held_ref[:, start : start + width]
        for k in range(1, ratio):
            start += width
            block = jnp.where(which == k, held_ref[:, start : start + width], block)
        mine_ref[:, j * width : (j + 1) * width] = block
    panel = held_ref[...]
    terms_ref[...] = jnp.concatenate(split(panel, 3), axis=0)
    to_strip(dot(panel, panel, ((1,), (1,))), gram_ref)
    for copy in matrix_copies:
        copy.wait()


def product_kernel(terms_ref, matrix_ref, gram_ref, out_ref):
    width = out_ref.shape[0] - STRIP
    rows = matrix_ref.shape[0]
    chunk = 256
    total = jnp.zeros((width, matrix_ref.shape[1]), jnp.float32)
    for start in range(0, rows, chunk):
        span = slice(start, start + chunk)
        parts = split(matrix_ref[span, :], 3)
        for i, part in enumerate(parts):
            count = 3 - i
            out = dot16(terms_ref[: count * width, span], part, ((1,), (0,)))
            for t in range(count):
                total = total + out[t * width : (t + 1) * width, :]
    out_ref[:width, :] = total
    out_ref[width:, :] = gram_ref[...]


def to_strip(value, strip_ref):
    width = value.shape[0]
    for i in range(width // STRIP):
        strip_ref[:, i * width : (i + 1) * width] = value[i * STRIP : (i + 1) * STRIP, :]


def from_strip(strip, width):
    return jnp.concatenate(
        [strip[:, i * width : (i + 1) * width] for i in range(width // STRIP)], axis=0
    )


def finish_kernel(other_ref, mine_ref, product_ref, gram_ref):
    width = product_ref.shape[0]
    product_ref[...] = mine_ref[:width, :] + other_ref[:width, :]
    gram_ref[...] = from_strip(mine_ref[width:, :] + other_ref[width:, :], width)


def factor_kernel(gram_ref, inverse_ref):
    size = inverse_ref.shape[0]
    batch = 4
    row = lax.broadcasted_iota(jnp.int32, (size, 2 * size), 0)
    lane = lax.broadcasted_iota(jnp.int32, (size, 2 * size), 1)
    eye = jnp.where(row == lane, 1.0, 0.0).astype(jnp.float32)
    table = jnp.concatenate([eye[:, :size], gram_ref[...]], axis=1)
    for first in range(0, size, batch):
        base = first // 8 * 8
        height = size - base
        low = table[base:, :]
        low_row = row[base:, :]
        cols = [
            jnp.broadcast_to(low[:, size + first + t : size + first + t + 1], (height, 2 * size))
            for t in range(batch)
        ]
        rows = [low[first - base + t : first - base + t + 1, :] for t in range(batch)]
        for t in range(batch):
            at = first - base + t
            scale = 1.0 / cols[t][at : at + 1, :]
            factor = jnp.where(low_row > first + t, cols[t] * scale, 0.0)
            for s in range(t + 1, batch):
                cols[s] = cols[s] - factor * cols[s][at : at + 1, :]
                rows[s] = rows[s] - factor[first - base + s : first - base + s + 1, :] * rows[t]
            low = low - factor * rows[t]
        table = low if base == 0 else jnp.concatenate([table[:base, :], low], axis=0)
    diagonal = jnp.sum(jnp.where(lane == row + size, table, 0.0), axis=1, keepdims=True)
    inverse_ref[...] = (table / jnp.sqrt(diagonal))[:, :size]


def stack_left(value):
    high, low = split(value, 2)
    return jnp.concatenate([high, low, high], axis=0)


def stack_right(value):
    high, low = split(value, 2)
    return jnp.concatenate([high, high, low], axis=0)


def basis_kernel(
    matrix_ref, panel_ref, product_cols_ref, inverse_ref, received_ref, held_ref, takes_ref,
    begun_ref, basis_ref, kept_ref, cols_ref,
):
    inverse = inverse_ref[...]
    basis = dot(inverse, panel_ref[...], ((1,), (0,)))
    image_cols = dot(inverse, product_cols_ref[...], ((1,), (0,)))
    basis_ref[...] = basis
    kept_ref[...] = basis
    panel_cols = jnp.where(takes_ref[0] != 0, received_ref[...], held_ref[...])
    cols_ref[...] = dot(inverse, panel_cols, ((1,), (0,)))
    left = stack_left(basis)
    right = stack_right(2.0 * image_cols)
    chunk = 256
    for start in range(0, matrix_ref.shape[0], chunk):
        span = slice(start, start + chunk)
        begun_ref[span, :] = matrix_ref[span, :] - dot16(left[:, span], right, ((0,), (0,)))


def inner_kernel(ratio, which_ref, panel_ref, *refs):
    halves, (rows_ref, inner_ref) = refs[:ratio], refs[ratio:]
    width = inner_ref.shape[0]
    which = which_ref[0]
    parts = []
    for j in range(halves[0].shape[1] // width):
        span = slice(j * width, (j + 1) * width)
        for k in range(ratio):
            block = halves[0][:, span]
            for shift in range(1, ratio):
                block = jnp.where((which + shift) % ratio == k, halves[shift][:, span], block)
            parts.append(block)
    product_rows = jnp.concatenate(parts, axis=1)
    rows_ref[...] = product_rows
    inner_ref[...] = dot(panel_ref[...], product_rows, ((1,), (1,)))


def image_kernel(begun_ref, rows_ref, cols_ref, inverse_ref, further_ref, image_ref):
    image = dot(inverse_ref[...], rows_ref[...], ((1,), (0,)))
    image_ref[...] = image
    left = stack_left(2.0 * image)
    right = stack_right(cols_ref[...])
    chunk = 256
    for start in range(0, begun_ref.shape[0], chunk):
        span = slice(start, start + chunk)
        further_ref[span, :] = begun_ref[span, :] - dot16(left[:, span], right, ((0,), (0,)))


def update_kernel(
    further_ref, image_ref, basis_ref, cols_ref, inverse_ref, inner_ref, other_ref,
    updated_ref, w_ref, buffer_ref, w_buffer_ref, sems,
):
    inverse = inverse_ref[...]
    basis = basis_ref[...]
    inner = inner_ref[...] + other_ref[...]
    correction = dot(dot(inverse, inner, ((1,), (0,))), inverse, ((1,), (1,)))
    right = stack_right(4.0 * dot(correction, cols_ref[...], ((1,), (0,))))
    left = stack_left(basis)
    count = sems.shape[0] - 1
    chunk = further_ref.shape[0] // count
    copies = []
    for i in range(count):
        span = slice(i * chunk, (i + 1) * chunk)
        buffer_ref[span, :] = further_ref[span, :] + dot16(left[:, span], right, ((0,), (0,)))
        copies.append(
            pltpu.make_async_copy(buffer_ref.at[span, :], updated_ref.at[span, :], sems.at[i])
        )
        copies[-1].start()
    w_buffer_ref[...] = 2.0 * (image_ref[...] - dot(correction, basis, ((0,), (0,))))
    copies.append(pltpu.make_async_copy(w_buffer_ref, w_ref, sems.at[count]))
    copies[-1].start()
    for copy in copies:
        copy.wait()


def shape(*dims, dtype=jnp.float32):
    return jax.ShapeDtypeStruct(dims, dtype)


def call(kernel, outs, args, in_specs=None, out_specs=None, scratch=(), flops=0):
    return pl.pallas_call(
        kernel,
        out_shape=outs,
        in_specs=in_specs or [VMEM] * len(args),
        out_specs=out_specs or ((VMEM,) * len(outs) if isinstance(outs, tuple) else VMEM),
        scratch_shapes=scratch,
        compiler_params=PARAMS,
        cost_estimate=pl.CostEstimate(flops=flops, bytes_accessed=1 << 18, transcendentals=0),
    )(*args)


def local(matrix, panel):
    n_row, n_col = lax.axis_size("row"), lax.axis_size("col")
    ratio = n_col // n_row
    rows, width = panel.shape
    cols = matrix.shape[1]
    which = (lax.axis_index("col") // n_row).astype(jnp.int32).reshape(1)
    chunks = 8

    mine, panel_t, terms, gram, kept = call(
        functools.partial(panel_kernel, ratio),
        (
            shape(width, cols),
            shape(width, rows),
            shape(3 * width, rows, dtype=jnp.bfloat16),
            shape(STRIP, cols),
            shape(rows, cols),
        ),
        (
            which,
            pltpu.with_memory_space_constraint(panel.T, pltpu.HBM),
            pltpu.with_memory_space_constraint(matrix, pltpu.HBM),
        ),
        in_specs=[SMEM, HBM, HBM],
        scratch=[pltpu.SemaphoreType.DMA((2 * chunks,))],
        flops=1 << 28,
    )
    message = call(
        product_kernel, shape(width + STRIP, cols), (terms, kept, gram), flops=1 << 30
    )
    step = 1
    while 2 * step < n_row:
        message = message + partner(message, "row", step)
        step *= 2
    last = partner(message, "row", step)
    held, received, takes = spread_rows(mine, message)
    product_cols, gram = call(
        finish_kernel, (shape(width, cols), shape(width, width)), (last, message), flops=1 << 24
    )
    halves = [transpose_grid(product_cols, shift) for shift in range(ratio)]
    inverse = call(factor_kernel, shape(width, width), (gram,), flops=1 << 30)
    begun, basis, basis_kept, basis_cols = call(
        basis_kernel,
        (shape(rows, cols), shape(width, rows), shape(width, rows), shape(width, cols)),
        (kept, panel_t, product_cols, inverse, received, held, takes),
        in_specs=[VMEM] * 6 + [SMEM],
        flops=1 << 30,
    )
    halves, begun = lax.optimization_barrier((halves, begun))
    product_rows, inner = call(
        functools.partial(inner_kernel, ratio),
        (shape(width, rows), shape(width, width)),
        (which, panel_t, *halves),
        in_specs=[SMEM] + [VMEM] * (1 + ratio),
        flops=1 << 24,
    )
    further, image = call(
        image_kernel,
        (shape(rows, cols), shape(width, rows)),
        (begun, product_rows, basis_cols, inverse),
        flops=1 << 30,
    )
    step = 1
    while 2 * step < n_row:
        inner = inner + partner(inner, "row", step)
        step *= 2
    updated, w_rows = call(
        update_kernel,
        (shape(rows, cols), shape(width, rows)),
        (further, image, basis_kept, basis_cols, inverse, inner, partner(inner, "row", step)),
        out_specs=(HBM, HBM),
        scratch=[
            pltpu.VMEM((rows, cols), jnp.float32),
            pltpu.VMEM((width, rows), jnp.float32),
            pltpu.SemaphoreType.DMA((chunks + 1,)),
        ],
        flops=1 << 30,
    )
    return (updated, w_rows.T, basis.T)


def solution(mesh):
    return jax.shard_map(
        local,
        mesh=mesh,
        in_specs=(P("row", "col"), P("row", None)),
        out_specs=(P("row", "col"), P("row", None), P("row", None)),
        check_vma=False,
    )
```

```python
import functools

import jax
import jax.numpy as jnp
from jax import lax
from jax.experimental import pallas as pl
from jax.experimental.pallas import tpu as pltpu
from jax.sharding import PartitionSpec as P

HIGH = lax.Precision.HIGHEST
VMEM = pl.BlockSpec(memory_space=pltpu.VMEM)
SMEM = pl.BlockSpec(memory_space=pltpu.SMEM)
HBM = pl.BlockSpec(memory_space=pltpu.HBM)
PARAMS = pltpu.CompilerParams(vmem_limit_bytes=40 * 1024 * 1024)
STRIP = 8


def dot(left, right, contract, precision=HIGH):
    return lax.dot_general(
        left, right, (contract, ((), ())), precision=precision, preferred_element_type=jnp.float32
    )


def dot16(left, right, contract):
    return dot(left, right, contract, lax.Precision.DEFAULT)


def split(value, parts):
    terms = []
    for _ in range(parts):
        terms.append(value.astype(jnp.bfloat16))
        value = value - terms[-1].astype(jnp.float32)
    return terms


def partner(value, axis, step):
    size = lax.axis_size(axis)
    return lax.ppermute(value, axis, [(i, i ^ step) for i in range(size)])


def tree_sum(parts):
    while len(parts) > 1:
        parts = [parts[i] + parts[i + 1] for i in range(0, len(parts), 2)]
    return parts[0]


def group_parts(value, axis, low, high):
    parts = [value]
    while low < high:
        value = tree_sum(parts)
        radix = min(4, high // low)
        parts = [value] + [partner(value, axis, i * low) for i in range(1, radix)]
        low *= radix
    return parts


def spread_rows(value, after):
    n_row, n_col = lax.axis_size("row"), lax.axis_size("col")
    apart = lax.axis_index("row") ^ (lax.axis_index("col") % n_row)
    bits = [1] + [1 << i for i in reversed(range(1, n_row.bit_length() - 1))]
    reached = [0]
    for bit in bits:
        pairs = []
        for c in range(n_col):
            for offset in reached:
                source = (c % n_row) ^ offset
                pairs.append((source * n_col + c, (source ^ bit) * n_col + c))
        reached += [offset ^ bit for offset in reached]
        received = lax.ppermute(value, ("row", "col"), pairs)
        takes = apart & bit != 0
        if bit == bits[-1]:
            return value, received, takes.astype(jnp.int32).reshape(1)
        received, _ = lax.optimization_barrier((received, after))
        value = jnp.where(takes, received, value)


def transpose_grid(value, shift):
    n_row, n_col = lax.axis_size("row"), lax.axis_size("col")
    ratio = n_col // n_row
    pairs = []
    for r in range(n_row):
        for k in range(ratio):
            for q in range(n_row):
                column = (k + shift) % ratio * n_row + r
                row = q ^ (n_row // 2) if shift % 2 else q
                pairs.append((row * n_col + column, r * n_col + k * n_row + q))
    return lax.ppermute(value, ("row", "col"), pairs)


def copy_rows(source, target, sems, first, pieces):
    size = source.shape[0] // pieces
    copies = []
    for piece in range(pieces):
        span = slice(piece * size, (piece + 1) * size)
        copies.append(
            pltpu.make_async_copy(source.at[span, :], target.at[span, :], sems.at[first + piece])
        )
        copies[-1].start()
    return copies


def panel_kernel(
    ratio, which_ref, panel_ref, matrix_ref,
    mine_ref, held_ref, terms_ref, gram_ref, kept_ref, sems,
):
    width = panel_ref.shape[0]
    pieces = sems.shape[0] // 2
    panel_copies = copy_rows(panel_ref, held_ref, sems, 0, pieces)
    matrix_copies = copy_rows(matrix_ref, kept_ref, sems, pieces, pieces)
    for copy in panel_copies:
        copy.wait()
    which = which_ref[0]
    for j in range(mine_ref.shape[1] // width):
        start = j * ratio * width
        block = held_ref[:, start : start + width]
        for k in range(1, ratio):
            start += width
            block = jnp.where(which == k, held_ref[:, start : start + width], block)
        mine_ref[:, j * width : (j + 1) * width] = block
    panel = held_ref[...]
    terms_ref[...] = jnp.concatenate(split(panel, 3), axis=0)
    to_strip(dot(panel, panel, ((1,), (1,))), gram_ref)
    for copy in matrix_copies:
        copy.wait()


def product_kernel(terms_ref, matrix_ref, gram_ref, out_ref):
    width = out_ref.shape[0] - STRIP
    rows = matrix_ref.shape[0]
    chunk = 256
    total = jnp.zeros((width, matrix_ref.shape[1]), jnp.float32)
    for start in range(0, rows, chunk):
        span = slice(start, start + chunk)
        parts = split(matrix_ref[span, :], 3)
        for i, part in enumerate(parts):
            count = 3 - i
            out = dot16(terms_ref[: count * width, span], part, ((1,), (0,)))
            for t in range(count):
                total = total + out[t * width : (t + 1) * width, :]
    out_ref[:width, :] = total
    out_ref[width:, :] = gram_ref[...]


def to_strip(value, strip_ref):
    width = value.shape[0]
    for i in range(width // STRIP):
        strip_ref[:, i * width : (i + 1) * width] = value[i * STRIP : (i + 1) * STRIP, :]


def from_strip(strip, width):
    return jnp.concatenate(
        [strip[:, i * width : (i + 1) * width] for i in range(width // STRIP)], axis=0
    )


def finish_kernel(other_ref, mine_ref, product_ref, gram_ref):
    width = product_ref.shape[0]
    product_ref[...] = mine_ref[:width, :] + other_ref[:width, :]
    gram_ref[...] = from_strip(mine_ref[width:, :] + other_ref[width:, :], width)


def factor_kernel(gram_ref, inverse_ref):
    size = inverse_ref.shape[0]
    batch = 4
    row = lax.broadcasted_iota(jnp.int32, (size, 2 * size), 0)
    lane = lax.broadcasted_iota(jnp.int32, (size, 2 * size), 1)
    eye = jnp.where(row == lane, 1.0, 0.0).astype(jnp.float32)
    table = jnp.concatenate([eye[:, :size], gram_ref[...]], axis=1)
    for first in range(0, size, batch):
        base = first // 8 * 8
        height = size - base
        low = table[base:, :]
        low_row = row[base:, :]
        cols = [
            jnp.broadcast_to(low[:, size + first + t : size + first + t + 1], (height, 2 * size))
            for t in range(batch)
        ]
        rows = [low[first - base + t : first - base + t + 1, :] for t in range(batch)]
        for t in range(batch):
            at = first - base + t
            scale = 1.0 / cols[t][at : at + 1, :]
            factor = jnp.where(low_row > first + t, cols[t] * scale, 0.0)
            for s in range(t + 1, batch):
                cols[s] = cols[s] - factor * cols[s][at : at + 1, :]
                rows[s] = rows[s] - factor[first - base + s : first - base + s + 1, :] * rows[t]
            low = low - factor * rows[t]
        table = low if base == 0 else jnp.concatenate([table[:base, :], low], axis=0)
    diagonal = jnp.sum(jnp.where(lane == row + size, table, 0.0), axis=1, keepdims=True)
    inverse_ref[...] = (table / jnp.sqrt(diagonal))[:, :size]


def stack_left(value):
    high, low = split(value, 2)
    return jnp.concatenate([high, low, high], axis=0)


def stack_right(value):
    high, low = split(value, 2)
    return jnp.concatenate([high, high, low], axis=0)


def basis_kernel(
    matrix_ref, panel_ref, product_cols_ref, inverse_ref, received_ref, held_ref, takes_ref,
    begun_ref, basis_ref, kept_ref, cols_ref,
):
    inverse = inverse_ref[...]
    basis = dot(inverse, panel_ref[...], ((1,), (0,)))
    image_cols = dot(inverse, product_cols_ref[...], ((1,), (0,)))
    basis_ref[...] = basis
    kept_ref[...] = basis
    panel_cols = jnp.where(takes_ref[0] != 0, received_ref[...], held_ref[...])
    cols_ref[...] = dot(inverse, panel_cols, ((1,), (0,)))
    left = stack_left(basis)
    right = stack_right(2.0 * image_cols)
    chunk = 256
    for start in range(0, matrix_ref.shape[0], chunk):
        span = slice(start, start + chunk)
        begun_ref[span, :] = matrix_ref[span, :] - dot16(left[:, span], right, ((0,), (0,)))


def inner_kernel(ratio, which_ref, panel_ref, *refs):
    halves, (rows_ref, inner_ref) = refs[:ratio], refs[ratio:]
    width = inner_ref.shape[0]
    which = which_ref[0]
    parts = []
    for j in range(halves[0].shape[1] // width):
        span = slice(j * width, (j + 1) * width)
        for k in range(ratio):
            block = halves[0][:, span]
            for shift in range(1, ratio):
                block = jnp.where((which + shift) % ratio == k, halves[shift][:, span], block)
            parts.append(block)
    product_rows = jnp.concatenate(parts, axis=1)
    rows_ref[...] = product_rows
    inner_ref[...] = dot(panel_ref[...], product_rows, ((1,), (1,)))


def image_kernel(begun_ref, rows_ref, cols_ref, inverse_ref, further_ref, image_ref):
    image = dot(inverse_ref[...], rows_ref[...], ((1,), (0,)))
    image_ref[...] = image
    left = stack_left(2.0 * image)
    right = stack_right(cols_ref[...])
    chunk = 256
    for start in range(0, begun_ref.shape[0], chunk):
        span = slice(start, start + chunk)
        further_ref[span, :] = begun_ref[span, :] - dot16(left[:, span], right, ((0,), (0,)))


def update_kernel(further_ref, image_ref, basis_ref, cols_ref, inverse_ref, *refs):
    inners, (updated_ref, w_ref, buffer_ref, w_buffer_ref, sems) = refs[:-5], refs[-5:]
    inverse = inverse_ref[...]
    basis = basis_ref[...]
    inner = tree_sum([part[...] for part in inners])
    correction = dot(dot(inverse, inner, ((1,), (0,))), inverse, ((1,), (1,)))
    right = stack_right(4.0 * dot(correction, cols_ref[...], ((1,), (0,))))
    left = stack_left(basis)
    count = sems.shape[0] - 1
    chunk = further_ref.shape[0] // count
    copies = []
    for i in range(count):
        span = slice(i * chunk, (i + 1) * chunk)
        buffer_ref[span, :] = further_ref[span, :] + dot16(left[:, span], right, ((0,), (0,)))
        copies.append(
            pltpu.make_async_copy(buffer_ref.at[span, :], updated_ref.at[span, :], sems.at[i])
        )
        copies[-1].start()
    w_buffer_ref[...] = 2.0 * (image_ref[...] - dot(correction, basis, ((0,), (0,))))
    copies.append(pltpu.make_async_copy(w_buffer_ref, w_ref, sems.at[count]))
    copies[-1].start()
    for copy in copies:
        copy.wait()


def shape(*dims, dtype=jnp.float32):
    return jax.ShapeDtypeStruct(dims, dtype)


def call(kernel, outs, args, in_specs=None, out_specs=None, scratch=(), flops=0):
    return pl.pallas_call(
        kernel,
        out_shape=outs,
        in_specs=in_specs or [VMEM] * len(args),
        out_specs=out_specs or ((VMEM,) * len(outs) if isinstance(outs, tuple) else VMEM),
        scratch_shapes=scratch,
        compiler_params=PARAMS,
        cost_estimate=pl.CostEstimate(flops=flops, bytes_accessed=1 << 18, transcendentals=0),
    )(*args)


def local(matrix, panel):
    n_row, n_col = lax.axis_size("row"), lax.axis_size("col")
    ratio = n_col // n_row
    rows, width = panel.shape
    cols = matrix.shape[1]
    which = (lax.axis_index("col") // n_row).astype(jnp.int32).reshape(1)
    chunks = 8

    mine, panel_t, terms, gram, kept = call(
        functools.partial(panel_kernel, ratio),
        (
            shape(width, cols),
            shape(width, rows),
            shape(3 * width, rows, dtype=jnp.bfloat16),
            shape(STRIP, cols),
            shape(rows, cols),
        ),
        (
            which,
            pltpu.with_memory_space_constraint(panel.T, pltpu.HBM),
            pltpu.with_memory_space_constraint(matrix, pltpu.HBM),
        ),
        in_specs=[SMEM, HBM, HBM],
        scratch=[pltpu.SemaphoreType.DMA((2 * chunks,))],
        flops=1 << 28,
    )
    message = call(
        product_kernel, shape(width + STRIP, cols), (terms, kept, gram), flops=1 << 30
    )
    step = 1
    while 2 * step < n_row:
        message = message + partner(message, "row", step)
        step *= 2
    last = partner(message, "row", step)
    held, received, takes = spread_rows(mine, message)
    product_cols, gram = call(
        finish_kernel, (shape(width, cols), shape(width, width)), (last, message), flops=1 << 24
    )
    halves = [transpose_grid(product_cols, shift) for shift in range(ratio)]
    inverse = call(factor_kernel, shape(width, width), (gram,), flops=1 << 30)
    begun, basis, basis_kept, basis_cols = call(
        basis_kernel,
        (shape(rows, cols), shape(width, rows), shape(width, rows), shape(width, cols)),
        (kept, panel_t, product_cols, inverse, received, held, takes),
        in_specs=[VMEM] * 6 + [SMEM],
        flops=1 << 30,
    )
    halves, begun = lax.optimization_barrier((halves, begun))
    product_rows, inner = call(
        functools.partial(inner_kernel, ratio),
        (shape(width, rows), shape(width, width)),
        (which, panel_t, *halves),
        in_specs=[SMEM] + [VMEM] * (1 + ratio),
        flops=1 << 24,
    )
    further, image = call(
        image_kernel,
        (shape(rows, cols), shape(width, rows)),
        (begun, product_rows, basis_cols, inverse),
        flops=1 << 30,
    )
    inners = group_parts(inner, "row", 1, n_row)[::-1]
    updated, w_rows = call(
        update_kernel,
        (shape(rows, cols), shape(width, rows)),
        (further, image, basis_kept, basis_cols, inverse, *inners),
        out_specs=(HBM, HBM),
        scratch=[
            pltpu.VMEM((rows, cols), jnp.float32),
            pltpu.VMEM((width, rows), jnp.float32),
            pltpu.SemaphoreType.DMA((chunks + 1,)),
        ],
        flops=1 << 30,
    )
    return (updated, w_rows.T, basis.T)


def solution(mesh):
    return jax.shard_map(
        local,
        mesh=mesh,
        in_specs=(P("row", "col"), P("row", None)),
        out_specs=(P("row", "col"), P("row", None), P("row", None)),
        check_vma=False,
    )
```

```python
import functools

import jax
import jax.numpy as jnp
from jax import lax
from jax.experimental import pallas as pl
from jax.experimental.pallas import tpu as pltpu
from jax.sharding import PartitionSpec as P

HIGH = lax.Precision.HIGHEST
VMEM = pl.BlockSpec(memory_space=pltpu.VMEM)
SMEM = pl.BlockSpec(memory_space=pltpu.SMEM)
HBM = pl.BlockSpec(memory_space=pltpu.HBM)
PARAMS = pltpu.CompilerParams(vmem_limit_bytes=40 * 1024 * 1024)
STRIP = 8


def dot(left, right, contract, precision=HIGH):
    return lax.dot_general(
        left, right, (contract, ((), ())), precision=precision, preferred_element_type=jnp.float32
    )


def dot16(left, right, contract):
    return dot(left, right, contract, lax.Precision.DEFAULT)


def split(value, parts):
    terms = []
    for _ in range(parts):
        terms.append(value.astype(jnp.bfloat16))
        value = value - terms[-1].astype(jnp.float32)
    return terms


def partner(value, axis, step):
    size = lax.axis_size(axis)
    return lax.ppermute(value, axis, [(i, i ^ step) for i in range(size)])


def spread_rows(value, after):
    n_row, n_col = lax.axis_size("row"), lax.axis_size("col")
    apart = lax.axis_index("row") ^ (lax.axis_index("col") % n_row)
    bits = [1] + [1 << i for i in reversed(range(1, n_row.bit_length() - 1))]
    reached = [0]
    for bit in bits:
        pairs = []
        for c in range(n_col):
            for offset in reached:
                source = (c % n_row) ^ offset
                pairs.append((source * n_col + c, (source ^ bit) * n_col + c))
        reached += [offset ^ bit for offset in reached]
        received = lax.ppermute(value, ("row", "col"), pairs)
        takes = apart & bit != 0
        if bit == bits[-1]:
            return value, received, takes.astype(jnp.int32).reshape(1)
        received, _ = lax.optimization_barrier((received, after))
        value = jnp.where(takes, received, value)


def transpose_grid(value, shift):
    n_row, n_col = lax.axis_size("row"), lax.axis_size("col")
    ratio = n_col // n_row
    pairs = []
    for r in range(n_row):
        for k in range(ratio):
            for q in range(n_row):
                column = (k + shift) % ratio * n_row + r
                row = q if shift % 2 else q ^ (n_row // 2)
                pairs.append((row * n_col + column, r * n_col + k * n_row + q))
    return lax.ppermute(value, ("row", "col"), pairs)


def copy_rows(source, target, sems, first, pieces):
    size = source.shape[0] // pieces
    copies = []
    for piece in range(pieces):
        span = slice(piece * size, (piece + 1) * size)
        copies.append(
            pltpu.make_async_copy(source.at[span, :], target.at[span, :], sems.at[first + piece])
        )
        copies[-1].start()
    return copies


def panel_kernel(
    ratio, which_ref, panel_ref, matrix_ref,
    mine_ref, held_ref, terms_ref, gram_ref, kept_ref, sems,
):
    width = panel_ref.shape[0]
    pieces = sems.shape[0] // 2
    panel_copies = copy_rows(panel_ref, held_ref, sems, 0, pieces)
    matrix_copies = copy_rows(matrix_ref, kept_ref, sems, pieces, pieces)
    for copy in panel_copies:
        copy.wait()
    which = which_ref[0]
    for j in range(mine_ref.shape[1] // width):
        start = j * ratio * width
        block = held_ref[:, start : start + width]
        for k in range(1, ratio):
            start += width
            block = jnp.where(which == k, held_ref[:, start : start + width], block)
        mine_ref[:, j * width : (j + 1) * width] = block
    panel = held_ref[...]
    terms_ref[...] = jnp.concatenate(split(panel, 3), axis=0)
    to_strip(dot(panel, panel, ((1,), (1,))), gram_ref)
    for copy in matrix_copies:
        copy.wait()


def product_kernel(terms_ref, matrix_ref, gram_ref, out_ref):
    width = out_ref.shape[0] - STRIP
    rows = matrix_ref.shape[0]
    chunk = 256
    total = jnp.zeros((width, matrix_ref.shape[1]), jnp.float32)
    for start in range(0, rows, chunk):
        span = slice(start, start + chunk)
        parts = split(matrix_ref[span, :], 3)
        for i, part in enumerate(parts):
            count = 3 - i
            out = dot16(terms_ref[: count * width, span], part, ((1,), (0,)))
            for t in range(count):
                total = total + out[t * width : (t + 1) * width, :]
    out_ref[:width, :] = total
    out_ref[width:, :] = gram_ref[...]


def to_strip(value, strip_ref):
    width = value.shape[0]
    for i in range(width // STRIP):
        strip_ref[:, i * width : (i + 1) * width] = value[i * STRIP : (i + 1) * STRIP, :]


def from_strip(strip, width):
    return jnp.concatenate(
        [strip[:, i * width : (i + 1) * width] for i in range(width // STRIP)], axis=0
    )


def finish_kernel(other_ref, mine_ref, product_ref, gram_ref):
    width = product_ref.shape[0]
    product_ref[...] = mine_ref[:width, :] + other_ref[:width, :]
    gram_ref[...] = from_strip(mine_ref[width:, :] + other_ref[width:, :], width)


def factor_kernel(gram_ref, inverse_ref):
    size = inverse_ref.shape[0]
    batch = 4
    row = lax.broadcasted_iota(jnp.int32, (size, 2 * size), 0)
    lane = lax.broadcasted_iota(jnp.int32, (size, 2 * size), 1)
    eye = jnp.where(row == lane, 1.0, 0.0).astype(jnp.float32)
    table = jnp.concatenate([eye[:, :size], gram_ref[...]], axis=1)
    for first in range(0, size, batch):
        base = first // 8 * 8
        height = size - base
        low = table[base:, :]
        low_row = row[base:, :]
        cols = [
            jnp.broadcast_to(low[:, size + first + t : size + first + t + 1], (height, 2 * size))
            for t in range(batch)
        ]
        rows = [low[first - base + t : first - base + t + 1, :] for t in range(batch)]
        for t in range(batch):
            at = first - base + t
            scale = 1.0 / cols[t][at : at + 1, :]
            factor = jnp.where(low_row > first + t, cols[t] * scale, 0.0)
            for s in range(t + 1, batch):
                cols[s] = cols[s] - factor * cols[s][at : at + 1, :]
                rows[s] = rows[s] - factor[first - base + s : first - base + s + 1, :] * rows[t]
            low = low - factor * rows[t]
        table = low if base == 0 else jnp.concatenate([table[:base, :], low], axis=0)
    diagonal = jnp.sum(jnp.where(lane == row + size, table, 0.0), axis=1, keepdims=True)
    inverse_ref[...] = (table / jnp.sqrt(diagonal))[:, :size]


def stack_left(value):
    high, low = split(value, 2)
    return jnp.concatenate([high, low, high], axis=0)


def stack_right(value):
    high, low = split(value, 2)
    return jnp.concatenate([high, high, low], axis=0)


def basis_kernel(
    matrix_ref, panel_ref, product_cols_ref, inverse_ref, received_ref, held_ref, takes_ref,
    begun_ref, basis_ref, kept_ref, cols_ref,
):
    inverse = inverse_ref[...]
    basis = dot(inverse, panel_ref[...], ((1,), (0,)))
    image_cols = dot(inverse, product_cols_ref[...], ((1,), (0,)))
    basis_ref[...] = basis
    kept_ref[...] = basis
    panel_cols = jnp.where(takes_ref[0] != 0, received_ref[...], held_ref[...])
    cols_ref[...] = dot(inverse, panel_cols, ((1,), (0,)))
    left = stack_left(basis)
    right = stack_right(2.0 * image_cols)
    chunk = 256
    for start in range(0, matrix_ref.shape[0], chunk):
        span = slice(start, start + chunk)
        begun_ref[span, :] = matrix_ref[span, :] - dot16(left[:, span], right, ((0,), (0,)))


def inner_kernel(ratio, which_ref, panel_ref, *refs):
    halves, (rows_ref, inner_ref) = refs[:ratio][::-1], refs[ratio:]
    width = inner_ref.shape[0]
    which = which_ref[0]
    parts = []
    for j in range(halves[0].shape[1] // width):
        span = slice(j * width, (j + 1) * width)
        for k in range(ratio):
            block = halves[0][:, span]
            for shift in range(1, ratio):
                block = jnp.where((which + shift) % ratio == k, halves[shift][:, span], block)
            parts.append(block)
    product_rows = jnp.concatenate(parts, axis=1)
    rows_ref[...] = product_rows
    inner_ref[...] = dot(panel_ref[...], product_rows, ((1,), (1,)))


def image_kernel(begun_ref, rows_ref, cols_ref, inverse_ref, further_ref, image_ref):
    image = dot(inverse_ref[...], rows_ref[...], ((1,), (0,)))
    image_ref[...] = image
    left = stack_left(2.0 * image)
    right = stack_right(cols_ref[...])
    chunk = 256
    for start in range(0, begun_ref.shape[0], chunk):
        span = slice(start, start + chunk)
        further_ref[span, :] = begun_ref[span, :] - dot16(left[:, span], right, ((0,), (0,)))


def update_kernel(
    further_ref, image_ref, basis_ref, cols_ref, inverse_ref, inner_ref, other_ref,
    updated_ref, w_ref, buffer_ref, w_buffer_ref, sems,
):
    inverse = inverse_ref[...]
    basis = basis_ref[...]
    inner = inner_ref[...] + other_ref[...]
    correction = dot(dot(inverse, inner, ((1,), (0,))), inverse, ((1,), (1,)))
    right = stack_right(4.0 * dot(correction, cols_ref[...], ((1,), (0,))))
    left = stack_left(basis)
    count = sems.shape[0] - 1
    chunk = further_ref.shape[0] // count
    copies = []
    for i in range(count):
        span = slice(i * chunk, (i + 1) * chunk)
        buffer_ref[span, :] = further_ref[span, :] + dot16(left[:, span], right, ((0,), (0,)))
        copies.append(
            pltpu.make_async_copy(buffer_ref.at[span, :], updated_ref.at[span, :], sems.at[i])
        )
        copies[-1].start()
    w_buffer_ref[...] = 2.0 * (image_ref[...] - dot(correction, basis, ((0,), (0,))))
    copies.append(pltpu.make_async_copy(w_buffer_ref, w_ref, sems.at[count]))
    copies[-1].start()
    for copy in copies:
        copy.wait()


def shape(*dims, dtype=jnp.float32):
    return jax.ShapeDtypeStruct(dims, dtype)


def call(kernel, outs, args, in_specs=None, out_specs=None, scratch=(), flops=0):
    return pl.pallas_call(
        kernel,
        out_shape=outs,
        in_specs=in_specs or [VMEM] * len(args),
        out_specs=out_specs or ((VMEM,) * len(outs) if isinstance(outs, tuple) else VMEM),
        scratch_shapes=scratch,
        compiler_params=PARAMS,
        cost_estimate=pl.CostEstimate(flops=flops, bytes_accessed=1 << 18, transcendentals=0),
    )(*args)


def local(matrix, panel):
    n_row, n_col = lax.axis_size("row"), lax.axis_size("col")
    ratio = n_col // n_row
    rows, width = panel.shape
    cols = matrix.shape[1]
    which = (lax.axis_index("col") // n_row).astype(jnp.int32).reshape(1)
    chunks = 8

    mine, panel_t, terms, gram, kept = call(
        functools.partial(panel_kernel, ratio),
        (
            shape(width, cols),
            shape(width, rows),
            shape(3 * width, rows, dtype=jnp.bfloat16),
            shape(STRIP, cols),
            shape(rows, cols),
        ),
        (
            which,
            pltpu.with_memory_space_constraint(panel.T, pltpu.HBM),
            pltpu.with_memory_space_constraint(matrix, pltpu.HBM),
        ),
        in_specs=[SMEM, HBM, HBM],
        scratch=[pltpu.SemaphoreType.DMA((2 * chunks,))],
        flops=1 << 28,
    )
    message = call(
        product_kernel, shape(width + STRIP, cols), (terms, kept, gram), flops=1 << 30
    )
    step = 1
    while 2 * step < n_row:
        message = message + partner(message, "row", step)
        step *= 2
    last = partner(message, "row", step)
    held, received, takes = spread_rows(mine, message)
    product_cols, gram = call(
        finish_kernel, (shape(width, cols), shape(width, width)), (last, message), flops=1 << 24
    )
    halves = [transpose_grid(product_cols, shift) for shift in reversed(range(ratio))]
    inverse = call(factor_kernel, shape(width, width), (gram,), flops=1 << 30)
    begun, basis, basis_kept, basis_cols = call(
        basis_kernel,
        (shape(rows, cols), shape(width, rows), shape(width, rows), shape(width, cols)),
        (kept, panel_t, product_cols, inverse, received, held, takes),
        in_specs=[VMEM] * 6 + [SMEM],
        flops=1 << 30,
    )
    halves, begun = lax.optimization_barrier((halves, begun))
    product_rows, inner = call(
        functools.partial(inner_kernel, ratio),
        (shape(width, rows), shape(width, width)),
        (which, panel_t, *halves),
        in_specs=[SMEM] + [VMEM] * (1 + ratio),
        flops=1 << 24,
    )
    further, image = call(
        image_kernel,
        (shape(rows, cols), shape(width, rows)),
        (begun, product_rows, basis_cols, inverse),
        flops=1 << 30,
    )
    step = 1
    while 2 * step < n_row:
        inner = inner + partner(inner, "row", step)
        step *= 2
    updated, w_rows = call(
        update_kernel,
        (shape(rows, cols), shape(width, rows)),
        (further, image, basis_kept, basis_cols, inverse, inner, partner(inner, "row", step)),
        out_specs=(HBM, HBM),
        scratch=[
            pltpu.VMEM((rows, cols), jnp.float32),
            pltpu.VMEM((width, rows), jnp.float32),
            pltpu.SemaphoreType.DMA((chunks + 1,)),
        ],
        flops=1 << 30,
    )
    return (updated, w_rows.T, basis.T)


def solution(mesh):
    return jax.shard_map(
        local,
        mesh=mesh,
        in_specs=(P("row", "col"), P("row", None)),
        out_specs=(P("row", "col"), P("row", None), P("row", None)),
        check_vma=False,
    )
```

```python
import functools

import jax
import jax.numpy as jnp
from jax import lax
from jax.experimental import pallas as pl
from jax.experimental.pallas import tpu as pltpu
from jax.sharding import PartitionSpec as P

HIGH = lax.Precision.HIGHEST
VMEM = pl.BlockSpec(memory_space=pltpu.VMEM)
SMEM = pl.BlockSpec(memory_space=pltpu.SMEM)
HBM = pl.BlockSpec(memory_space=pltpu.HBM)
PARAMS = pltpu.CompilerParams(vmem_limit_bytes=40 * 1024 * 1024)
STRIP = 8


def dot(left, right, contract, precision=HIGH):
    return lax.dot_general(
        left, right, (contract, ((), ())), precision=precision, preferred_element_type=jnp.float32
    )


def dot16(left, right, contract):
    return dot(left, right, contract, lax.Precision.DEFAULT)


def split(value, parts):
    terms = []
    for _ in range(parts):
        terms.append(value.astype(jnp.bfloat16))
        value = value - terms[-1].astype(jnp.float32)
    return terms


def partner(value, axis, step):
    size = lax.axis_size(axis)
    return lax.ppermute(value, axis, [(i, i ^ step) for i in range(size)])


def spread_rows(value, after):
    n_row, n_col = lax.axis_size("row"), lax.axis_size("col")
    apart = lax.axis_index("row") ^ (lax.axis_index("col") % n_row)
    bits = [1] + [1 << i for i in reversed(range(1, n_row.bit_length() - 1))]
    reached = [0]
    for bit in bits:
        pairs = []
        for c in range(n_col):
            for offset in reached:
                source = (c % n_row) ^ offset
                pairs.append((source * n_col + c, (source ^ bit) * n_col + c))
        reached += [offset ^ bit for offset in reached]
        received = lax.ppermute(value, ("row", "col"), pairs)
        takes = apart & bit != 0
        if bit == bits[-1]:
            return value, received, takes.astype(jnp.int32).reshape(1)
        received, _ = lax.optimization_barrier((received, after))
        value = jnp.where(takes, received, value)


def transpose_grid(value, shift):
    n_row, n_col = lax.axis_size("row"), lax.axis_size("col")
    ratio = n_col // n_row
    pairs = []
    for r in range(n_row):
        for k in range(ratio):
            for q in range(n_row):
                column = (k + shift) % ratio * n_row + r
                row = q if shift % 2 else q ^ (n_row // 2)
                pairs.append((row * n_col + column, r * n_col + k * n_row + q))
    return lax.ppermute(value, ("row", "col"), pairs)


def copy_rows(source, target, sems, first, pieces):
    size = source.shape[0] // pieces
    copies = []
    for piece in range(pieces):
        span = slice(piece * size, (piece + 1) * size)
        copies.append(
            pltpu.make_async_copy(source.at[span, :], target.at[span, :], sems.at[first + piece])
        )
        copies[-1].start()
    return copies


def panel_kernel(ratio, which_ref, panel_ref, matrix_ref, *refs):
    mine_refs, (held_ref, terms_ref, gram_ref, kept_ref, sems) = refs[:ratio], refs[ratio:]
    width = panel_ref.shape[0]
    pieces = sems.shape[0] // 2
    panel_copies = copy_rows(panel_ref, held_ref, sems, 0, pieces)
    matrix_copies = copy_rows(matrix_ref, kept_ref, sems, pieces, pieces)
    for copy in panel_copies:
        copy.wait()
    which = which_ref[0]
    for j in range(mine_refs[0].shape[1] // width):
        start = j * ratio * width
        blocks = [held_ref[:, start + k * width : start + (k + 1) * width] for k in range(ratio)]
        for shift, mine_ref in enumerate(mine_refs):
            block = blocks[shift]
            for k in range(1, ratio):
                block = jnp.where(which == k, blocks[(k + shift) % ratio], block)
            mine_ref[:, j * width : (j + 1) * width] = block
    panel = held_ref[...]
    terms_ref[...] = jnp.concatenate(split(panel, 3), axis=0)
    to_strip(dot(panel, panel, ((1,), (1,))), gram_ref)
    for copy in matrix_copies:
        copy.wait()


def product_kernel(terms_ref, matrix_ref, gram_ref, out_ref):
    width = out_ref.shape[0] - STRIP
    rows = matrix_ref.shape[0]
    chunk = 256
    total = jnp.zeros((width, matrix_ref.shape[1]), jnp.float32)
    for start in range(0, rows, chunk):
        span = slice(start, start + chunk)
        parts = split(matrix_ref[span, :], 3)
        for i, part in enumerate(parts):
            count = 3 - i
            out = dot16(terms_ref[: count * width, span], part, ((1,), (0,)))
            for t in range(count):
                total = total + out[t * width : (t + 1) * width, :]
    out_ref[:width, :] = total
    out_ref[width:, :] = gram_ref[...]


def to_strip(value, strip_ref):
    width = value.shape[0]
    for i in range(width // STRIP):
        strip_ref[:, i * width : (i + 1) * width] = value[i * STRIP : (i + 1) * STRIP, :]


def from_strip(strip, width):
    return jnp.concatenate(
        [strip[:, i * width : (i + 1) * width] for i in range(width // STRIP)], axis=0
    )


def finish_kernel(other_ref, mine_ref, product_ref, gram_ref):
    width = product_ref.shape[0]
    product_ref[...] = mine_ref[:width, :] + other_ref[:width, :]
    gram_ref[...] = from_strip(mine_ref[width:, :] + other_ref[width:, :], width)


def factor_kernel(gram_ref, inverse_ref):
    size = inverse_ref.shape[0]
    batch = 4
    row = lax.broadcasted_iota(jnp.int32, (size, 2 * size), 0)
    lane = lax.broadcasted_iota(jnp.int32, (size, 2 * size), 1)
    eye = jnp.where(row == lane, 1.0, 0.0).astype(jnp.float32)
    table = jnp.concatenate([eye[:, :size], gram_ref[...]], axis=1)
    for first in range(0, size, batch):
        base = first // 8 * 8
        height = size - base
        low = table[base:, :]
        low_row = row[base:, :]
        cols = [
            jnp.broadcast_to(low[:, size + first + t : size + first + t + 1], (height, 2 * size))
            for t in range(batch)
        ]
        rows = [low[first - base + t : first - base + t + 1, :] for t in range(batch)]
        for t in range(batch):
            at = first - base + t
            scale = 1.0 / cols[t][at : at + 1, :]
            factor = jnp.where(low_row > first + t, cols[t] * scale, 0.0)
            for s in range(t + 1, batch):
                cols[s] = cols[s] - factor * cols[s][at : at + 1, :]
                rows[s] = rows[s] - factor[first - base + s : first - base + s + 1, :] * rows[t]
            low = low - factor * rows[t]
        table = low if base == 0 else jnp.concatenate([table[:base, :], low], axis=0)
    diagonal = jnp.sum(jnp.where(lane == row + size, table, 0.0), axis=1, keepdims=True)
    inverse_ref[...] = (table / jnp.sqrt(diagonal))[:, :size]


def stack_left(value):
    high, low = split(value, 2)
    return jnp.concatenate([high, low, high], axis=0)


def stack_right(value):
    high, low = split(value, 2)
    return jnp.concatenate([high, high, low], axis=0)


def basis_kernel(
    matrix_ref, panel_ref, product_cols_ref, inverse_ref, received_ref, held_ref, takes_ref,
    begun_ref, basis_ref, left_ref, coeffs_ref, cols_ref, coeffs_cols_ref,
):
    inverse = inverse_ref[...]
    basis = dot(inverse, panel_ref[...], ((1,), (0,)))
    image_cols = dot(inverse, product_cols_ref[...], ((1,), (0,)))
    basis_ref[...] = basis
    coeffs_ref[...] = dot(inverse, basis, ((0,), (0,)))
    panel_cols = jnp.where(takes_ref[0] != 0, received_ref[...], held_ref[...])
    cols = dot(inverse, panel_cols, ((1,), (0,)))
    cols_ref[...] = cols
    coeffs_cols_ref[...] = dot(inverse, cols, ((0,), (0,)))
    left = stack_left(basis)
    left_ref[...] = left
    right = stack_right(2.0 * image_cols)
    chunk = 256
    for start in range(0, matrix_ref.shape[0], chunk):
        span = slice(start, start + chunk)
        begun_ref[span, :] = matrix_ref[span, :] - dot16(left[:, span], right, ((0,), (0,)))


def inner_kernel(*refs):
    count = len(refs) // 2
    inner_ref = refs[-1]
    inner_ref[...] = sum(
        dot(refs[count + i][...], refs[i][...], ((1,), (1,))) for i in range(count)
    )


def image_kernel(ratio, which_ref, begun_ref, cols_ref, inverse_ref, *refs):
    halves, (further_ref, image_ref) = refs[:ratio][::-1], refs[ratio:]
    width = inverse_ref.shape[0]
    which = which_ref[0]
    parts = []
    for j in range(halves[0].shape[1] // width):
        span = slice(j * width, (j + 1) * width)
        for k in range(ratio):
            block = halves[0][:, span]
            for shift in range(1, ratio):
                block = jnp.where((which + shift) % ratio == k, halves[shift][:, span], block)
            parts.append(block)
    image = dot(inverse_ref[...], jnp.concatenate(parts, axis=1), ((1,), (0,)))
    image_ref[...] = image
    left = stack_left(2.0 * image)
    right = stack_right(cols_ref[...])
    chunk = 256
    for start in range(0, begun_ref.shape[0], chunk):
        span = slice(start, start + chunk)
        further_ref[span, :] = begun_ref[span, :] - dot16(left[:, span], right, ((0,), (0,)))


def update_kernel(
    further_ref, image_ref, left_ref, coeffs_ref, coeffs_cols_ref, inverse_ref,
    inner_ref, other_ref, updated_ref, w_ref, buffer_ref, w_buffer_ref, sems,
):
    inverse = inverse_ref[...]
    inner = inner_ref[...] + other_ref[...]
    right = dot(inverse, dot(inner, coeffs_cols_ref[...], ((1,), (0,))), ((1,), (0,)))
    right = stack_right(4.0 * right)
    count = sems.shape[0] - 1
    chunk = further_ref.shape[0] // count
    copies = []
    for i in range(count):
        span = slice(i * chunk, (i + 1) * chunk)
        buffer_ref[span, :] = further_ref[span, :] + dot16(left_ref[:, span], right, ((0,), (0,)))
        copies.append(
            pltpu.make_async_copy(buffer_ref.at[span, :], updated_ref.at[span, :], sems.at[i])
        )
        copies[-1].start()
    removed = dot(inverse, dot(inner, coeffs_ref[...], ((0,), (0,))), ((1,), (0,)))
    w_buffer_ref[...] = 2.0 * (image_ref[...] - removed)
    copies.append(pltpu.make_async_copy(w_buffer_ref, w_ref, sems.at[count]))
    copies[-1].start()
    for copy in copies:
        copy.wait()


def shape(*dims, dtype=jnp.float32):
    return jax.ShapeDtypeStruct(dims, dtype)


def call(kernel, outs, args, in_specs=None, out_specs=None, scratch=(), flops=0):
    return pl.pallas_call(
        kernel,
        out_shape=outs,
        in_specs=in_specs or [VMEM] * len(args),
        out_specs=out_specs or ((VMEM,) * len(outs) if isinstance(outs, tuple) else VMEM),
        scratch_shapes=scratch,
        compiler_params=PARAMS,
        cost_estimate=pl.CostEstimate(flops=flops, bytes_accessed=1 << 18, transcendentals=0),
    )(*args)


def local(matrix, panel):
    n_row, n_col = lax.axis_size("row"), lax.axis_size("col")
    ratio = n_col // n_row
    rows, width = panel.shape
    cols = matrix.shape[1]
    which = (lax.axis_index("col") // n_row).astype(jnp.int32).reshape(1)
    chunks = 8

    *mines, panel_t, terms, gram, kept = call(
        functools.partial(panel_kernel, ratio),
        (
            *[shape(width, cols)] * ratio,
            shape(width, rows),
            shape(3 * width, rows, dtype=jnp.bfloat16),
            shape(STRIP, cols),
            shape(rows, cols),
        ),
        (
            which,
            pltpu.with_memory_space_constraint(panel.T, pltpu.HBM),
            pltpu.with_memory_space_constraint(matrix, pltpu.HBM),
        ),
        in_specs=[SMEM, HBM, HBM],
        scratch=[pltpu.SemaphoreType.DMA((2 * chunks,))],
        flops=1 << 28,
    )
    message = call(
        product_kernel, shape(width + STRIP, cols), (terms, kept, gram), flops=1 << 30
    )
    step = 1
    while 2 * step < n_row:
        message = message + partner(message, "row", step)
        step *= 2
    last = partner(message, "row", step)
    held, received, takes = spread_rows(mines[0], message)
    product_cols, gram = call(
        finish_kernel, (shape(width, cols), shape(width, width)), (last, message), flops=1 << 24
    )
    halves = [transpose_grid(product_cols, shift) for shift in reversed(range(ratio))]
    inverse = call(factor_kernel, shape(width, width), (gram,), flops=1 << 30)
    begun, basis, left, coeffs, basis_cols, coeffs_cols = call(
        basis_kernel,
        (
            shape(rows, cols),
            shape(width, rows),
            shape(3 * width, rows, dtype=jnp.bfloat16),
            shape(width, rows),
            shape(width, cols),
            shape(width, cols),
        ),
        (kept, panel_t, product_cols, inverse, received, held, takes),
        in_specs=[VMEM] * 6 + [SMEM],
        flops=1 << 30,
    )
    halves, begun = lax.optimization_barrier((halves, begun))
    inner = call(inner_kernel, shape(width, width), (*halves, *mines[::-1]), flops=1 << 24)
    further, image = call(
        functools.partial(image_kernel, ratio),
        (shape(rows, cols), shape(width, rows)),
        (which, begun, basis_cols, inverse, *halves),
        in_specs=[SMEM] + [VMEM] * (3 + ratio),
        flops=1 << 30,
    )
    step = 1
    while 2 * step < n_row:
        inner = inner + partner(inner, "row", step)
        step *= 2
    updated, w_rows = call(
        update_kernel,
        (shape(rows, cols), shape(width, rows)),
        (
            further, image, left, coeffs, coeffs_cols, inverse,
            inner, partner(inner, "row", step),
        ),
        out_specs=(HBM, HBM),
        scratch=[
            pltpu.VMEM((rows, cols), jnp.float32),
            pltpu.VMEM((width, rows), jnp.float32),
            pltpu.SemaphoreType.DMA((chunks + 1,)),
        ],
        flops=1 << 30,
    )
    return (updated, w_rows.T, basis.T)


def solution(mesh):
    return jax.shard_map(
        local,
        mesh=mesh,
        in_specs=(P("row", "col"), P("row", None)),
        out_specs=(P("row", "col"), P("row", None), P("row", None)),
        check_vma=False,
    )
```

```python
import functools

import jax
import jax.numpy as jnp
from jax import lax
from jax.experimental import pallas as pl
from jax.experimental.pallas import tpu as pltpu
from jax.sharding import PartitionSpec as P

HIGH = lax.Precision.HIGHEST
VMEM = pl.BlockSpec(memory_space=pltpu.VMEM)
SMEM = pl.BlockSpec(memory_space=pltpu.SMEM)
HBM = pl.BlockSpec(memory_space=pltpu.HBM)
PARAMS = pltpu.CompilerParams(vmem_limit_bytes=40 * 1024 * 1024)
STRIP = 8


def dot(left, right, contract, precision=HIGH):
    return lax.dot_general(
        left, right, (contract, ((), ())), precision=precision, preferred_element_type=jnp.float32
    )


def dot16(left, right, contract):
    return dot(left, right, contract, lax.Precision.DEFAULT)


def split(value, parts):
    terms = []
    for _ in range(parts):
        terms.append(value.astype(jnp.bfloat16))
        value = value - terms[-1].astype(jnp.float32)
    return terms


def partner(value, axis, step):
    size = lax.axis_size(axis)
    return lax.ppermute(value, axis, [(i, i ^ step) for i in range(size)])


def tree_sum(parts):
    while len(parts) > 1:
        parts = [parts[i] + parts[i + 1] for i in range(0, len(parts), 2)]
    return parts[0]


def group_parts(value, axis, low, high):
    parts = [value]
    while low < high:
        value = tree_sum(parts)
        radix = min(4, high // low)
        parts = [value] + [partner(value, axis, i * low) for i in range(1, radix)]
        low *= radix
    return parts


def spread_rows(value, after):
    n_row, n_col = lax.axis_size("row"), lax.axis_size("col")
    apart = lax.axis_index("row") ^ (lax.axis_index("col") % n_row)
    bits = [1] + [1 << i for i in reversed(range(1, n_row.bit_length() - 1))]
    reached = [0]
    for bit in bits:
        pairs = []
        for c in range(n_col):
            for offset in reached:
                source = (c % n_row) ^ offset
                pairs.append((source * n_col + c, (source ^ bit) * n_col + c))
        reached += [offset ^ bit for offset in reached]
        received = lax.ppermute(value, ("row", "col"), pairs)
        takes = apart & bit != 0
        if bit == bits[-1]:
            return value, received, takes.astype(jnp.int32).reshape(1)
        received, _ = lax.optimization_barrier((received, after))
        value = jnp.where(takes, received, value)


def transpose_grid(value, shift):
    n_row, n_col = lax.axis_size("row"), lax.axis_size("col")
    ratio = n_col // n_row
    pairs = []
    for r in range(n_row):
        for k in range(ratio):
            for q in range(n_row):
                column = (k + shift) % ratio * n_row + r
                row = q if shift % 2 else q ^ (n_row // 2)
                pairs.append((row * n_col + column, r * n_col + k * n_row + q))
    return lax.ppermute(value, ("row", "col"), pairs)


def copy_rows(source, target, sems, first, pieces):
    size = source.shape[0] // pieces
    copies = []
    for piece in range(pieces):
        span = slice(piece * size, (piece + 1) * size)
        copies.append(
            pltpu.make_async_copy(source.at[span, :], target.at[span, :], sems.at[first + piece])
        )
        copies[-1].start()
    return copies


def product_kernel(ratio, which_ref, panel_ref, matrix_ref, *refs):
    mine_refs, (out_ref, held_ref, kept_ref, sems) = refs[:ratio], refs[ratio:]
    width, rows = panel_ref.shape
    pieces = width // STRIP
    panel_copies = copy_rows(panel_ref, held_ref, sems, 0, pieces)
    matrix_copies = copy_rows(matrix_ref, kept_ref, sems, pieces, sems.shape[0] - pieces)
    for copy in panel_copies:
        copy.wait()
    which = which_ref[0]
    for j in range(mine_refs[0].shape[1] // width):
        start = j * ratio * width
        blocks = [held_ref[:, start + k * width : start + (k + 1) * width] for k in range(ratio)]
        for shift, mine_ref in enumerate(mine_refs):
            block = blocks[shift]
            for k in range(1, ratio):
                block = jnp.where(which == k, blocks[(k + shift) % ratio], block)
            mine_ref[:, j * width : (j + 1) * width] = block
    panel = held_ref[...]
    to_strip(dot(panel, panel, ((1,), (1,))), out_ref.at[width:, :])
    chunk = 256
    each = len(matrix_copies) * chunk // rows
    total = jnp.zeros((width, matrix_ref.shape[1]), jnp.float32)
    for start in range(0, rows, chunk):
        for copy in matrix_copies[start // chunk * each : (start // chunk + 1) * each]:
            copy.wait()
        span = slice(start, start + chunk)
        terms = jnp.concatenate(split(held_ref[:, span], 3), axis=0)
        for i, part in enumerate(split(kept_ref[span, :], 3)):
            count = 3 - i
            out = dot16(terms[: count * width, :], part, ((1,), (0,)))
            for t in range(count):
                total = total + out[t * width : (t + 1) * width, :]
    out_ref[:width, :] = total


def to_strip(value, strip_ref):
    width = value.shape[0]
    for i in range(width // STRIP):
        strip_ref[:, i * width : (i + 1) * width] = value[i * STRIP : (i + 1) * STRIP, :]


def from_strip(strip, width):
    return jnp.concatenate(
        [strip[:, i * width : (i + 1) * width] for i in range(width // STRIP)], axis=0
    )


def finish_kernel(other_ref, mine_ref, product_ref, gram_ref):
    width = product_ref.shape[0]
    product_ref[...] = mine_ref[:width, :] + other_ref[:width, :]
    gram_ref[...] = from_strip(mine_ref[width:, :] + other_ref[width:, :], width)


def factor_kernel(gram_ref, inverse_ref):
    size = inverse_ref.shape[0]
    batch = 4
    row = lax.broadcasted_iota(jnp.int32, (size, 2 * size), 0)
    lane = lax.broadcasted_iota(jnp.int32, (size, 2 * size), 1)
    eye = jnp.where(row == lane, 1.0, 0.0).astype(jnp.float32)
    table = jnp.concatenate([eye[:, :size], gram_ref[...]], axis=1)
    for first in range(0, size, batch):
        base = first // 8 * 8
        height = size - base
        low = table[base:, :]
        low_row = row[base:, :]
        cols = [
            jnp.broadcast_to(low[:, size + first + t : size + first + t + 1], (height, 2 * size))
            for t in range(batch)
        ]
        rows = [low[first - base + t : first - base + t + 1, :] for t in range(batch)]
        for t in range(batch):
            at = first - base + t
            scale = 1.0 / cols[t][at : at + 1, :]
            factor = jnp.where(low_row > first + t, cols[t] * scale, 0.0)
            for s in range(t + 1, batch):
                cols[s] = cols[s] - factor * cols[s][at : at + 1, :]
                rows[s] = rows[s] - factor[first - base + s : first - base + s + 1, :] * rows[t]
            low = low - factor * rows[t]
        table = low if base == 0 else jnp.concatenate([table[:base, :], low], axis=0)
    diagonal = jnp.sum(jnp.where(lane == row + size, table, 0.0), axis=1, keepdims=True)
    inverse_ref[...] = (table / jnp.sqrt(diagonal))[:, :size]


def stack_left(value):
    high, low = split(value, 2)
    return jnp.concatenate([high, low, high], axis=0)


def stack_right(value):
    high, low = split(value, 2)
    return jnp.concatenate([high, high, low], axis=0)


def basis_kernel(
    matrix_ref, panel_ref, product_cols_ref, inverse_ref, received_ref, held_ref, takes_ref,
    begun_ref, basis_ref, left_ref, coeffs_ref, cols_ref, coeffs_cols_ref,
):
    inverse = inverse_ref[...]
    basis = dot(inverse, panel_ref[...], ((1,), (0,)))
    image_cols = dot(inverse, product_cols_ref[...], ((1,), (0,)))
    basis_ref[...] = basis
    coeffs_ref[...] = dot(inverse, basis, ((0,), (0,)))
    panel_cols = jnp.where(takes_ref[0] != 0, received_ref[...], held_ref[...])
    cols = dot(inverse, panel_cols, ((1,), (0,)))
    cols_ref[...] = cols
    coeffs_cols_ref[...] = dot(inverse, cols, ((0,), (0,)))
    left = stack_left(basis)
    left_ref[...] = left
    right = stack_right(2.0 * image_cols)
    chunk = 256
    for start in range(0, matrix_ref.shape[0], chunk):
        span = slice(start, start + chunk)
        begun_ref[span, :] = matrix_ref[span, :] - dot16(left[:, span], right, ((0,), (0,)))


def inner_kernel(*refs):
    count = len(refs) // 2
    inner_ref = refs[-1]
    inner_ref[...] = sum(
        dot(refs[count + i][...], refs[i][...], ((1,), (1,))) for i in range(count)
    )


def image_kernel(ratio, which_ref, begun_ref, cols_ref, inverse_ref, *refs):
    halves, (further_ref, image_ref) = refs[:ratio][::-1], refs[ratio:]
    width = inverse_ref.shape[0]
    which = which_ref[0]
    parts = []
    for j in range(halves[0].shape[1] // width):
        span = slice(j * width, (j + 1) * width)
        for k in range(ratio):
            block = halves[0][:, span]
            for shift in range(1, ratio):
                block = jnp.where((which + shift) % ratio == k, halves[shift][:, span], block)
            parts.append(block)
    image = dot(inverse_ref[...], jnp.concatenate(parts, axis=1), ((1,), (0,)))
    image_ref[...] = image
    left = stack_left(2.0 * image)
    right = stack_right(cols_ref[...])
    chunk = 256
    for start in range(0, begun_ref.shape[0], chunk):
        span = slice(start, start + chunk)
        further_ref[span, :] = begun_ref[span, :] - dot16(left[:, span], right, ((0,), (0,)))


def update_kernel(
    further_ref, image_ref, left_ref, coeffs_ref, coeffs_cols_ref, inverse_ref, *refs
):
    inners, (updated_ref, w_ref, buffer_ref, w_buffer_ref, sems) = refs[:-5], refs[-5:]
    inverse = inverse_ref[...]
    inner = tree_sum([part[...] for part in inners])
    right = dot(inverse, dot(inner, coeffs_cols_ref[...], ((1,), (0,))), ((1,), (0,)))
    right = stack_right(4.0 * right)
    count = sems.shape[0] - 1
    chunk = further_ref.shape[0] // count
    copies = []
    for i in range(count):
        span = slice(i * chunk, (i + 1) * chunk)
        buffer_ref[span, :] = further_ref[span, :] + dot16(left_ref[:, span], right, ((0,), (0,)))
        copies.append(
            pltpu.make_async_copy(buffer_ref.at[span, :], updated_ref.at[span, :], sems.at[i])
        )
        copies[-1].start()
    removed = dot(inverse, dot(inner, coeffs_ref[...], ((0,), (0,))), ((1,), (0,)))
    w_buffer_ref[...] = 2.0 * (image_ref[...] - removed)
    copies.append(pltpu.make_async_copy(w_buffer_ref, w_ref, sems.at[count]))
    copies[-1].start()
    for copy in copies:
        copy.wait()


def shape(*dims, dtype=jnp.float32):
    return jax.ShapeDtypeStruct(dims, dtype)


def call(kernel, outs, args, in_specs=None, out_specs=None, scratch=(), flops=0):
    return pl.pallas_call(
        kernel,
        out_shape=outs,
        in_specs=in_specs or [VMEM] * len(args),
        out_specs=out_specs or ((VMEM,) * len(outs) if isinstance(outs, tuple) else VMEM),
        scratch_shapes=scratch,
        compiler_params=PARAMS,
        cost_estimate=pl.CostEstimate(flops=flops, bytes_accessed=1 << 18, transcendentals=0),
    )(*args)


def local(matrix, panel):
    n_row, n_col = lax.axis_size("row"), lax.axis_size("col")
    ratio = n_col // n_row
    rows, width = panel.shape
    cols = matrix.shape[1]
    which = (lax.axis_index("col") // n_row).astype(jnp.int32).reshape(1)
    chunks = 8

    *mines, message, panel_t, kept = call(
        functools.partial(product_kernel, ratio),
        (
            *[shape(width, cols)] * ratio,
            shape(width + STRIP, cols),
            shape(width, rows),
            shape(rows, cols),
        ),
        (
            which,
            pltpu.with_memory_space_constraint(panel.T, pltpu.HBM),
            pltpu.with_memory_space_constraint(matrix, pltpu.HBM),
        ),
        in_specs=[SMEM, HBM, HBM],
        scratch=[pltpu.SemaphoreType.DMA((width // STRIP + 2 * chunks,))],
        flops=1 << 30,
    )
    step = 1
    while 2 * step < n_row:
        message = message + partner(message, "row", step)
        step *= 2
    last = partner(message, "row", step)
    held, received, takes = spread_rows(mines[0], message)
    product_cols, gram = call(
        finish_kernel, (shape(width, cols), shape(width, width)), (last, message), flops=1 << 24
    )
    halves = [transpose_grid(product_cols, shift) for shift in reversed(range(ratio))]
    inverse = call(factor_kernel, shape(width, width), (gram,), flops=1 << 30)
    begun, basis, left, coeffs, basis_cols, coeffs_cols = call(
        basis_kernel,
        (
            shape(rows, cols),
            shape(width, rows),
            shape(3 * width, rows, dtype=jnp.bfloat16),
            shape(width, rows),
            shape(width, cols),
            shape(width, cols),
        ),
        (kept, panel_t, product_cols, inverse, received, held, takes),
        in_specs=[VMEM] * 6 + [SMEM],
        flops=1 << 30,
    )
    halves, begun = lax.optimization_barrier((halves, begun))
    inner = call(inner_kernel, shape(width, width), (*halves, *mines[::-1]), flops=1 << 24)
    further, image = call(
        functools.partial(image_kernel, ratio),
        (shape(rows, cols), shape(width, rows)),
        (which, begun, basis_cols, inverse, *halves),
        in_specs=[SMEM] + [VMEM] * (3 + ratio),
        flops=1 << 30,
    )
    inners = group_parts(inner, "row", 1, n_row)[::-1]
    updated, w_rows = call(
        update_kernel,
        (shape(rows, cols), shape(width, rows)),
        (further, image, left, coeffs, coeffs_cols, inverse, *inners),
        out_specs=(HBM, HBM),
        scratch=[
            pltpu.VMEM((rows, cols), jnp.float32),
            pltpu.VMEM((width, rows), jnp.float32),
            pltpu.SemaphoreType.DMA((chunks + 1,)),
        ],
        flops=1 << 30,
    )
    return (updated, w_rows.T, basis.T)


def solution(mesh):
    return jax.shard_map(
        local,
        mesh=mesh,
        in_specs=(P("row", "col"), P("row", None)),
        out_specs=(P("row", "col"), P("row", None), P("row", None)),
        check_vma=False,
    )
```

```python
import functools

import jax
import jax.numpy as jnp
from jax import lax
from jax.experimental import pallas as pl
from jax.experimental.pallas import tpu as pltpu
from jax.sharding import PartitionSpec as P

HIGH = lax.Precision.HIGHEST
VMEM = pl.BlockSpec(memory_space=pltpu.VMEM)
SMEM = pl.BlockSpec(memory_space=pltpu.SMEM)
HBM = pl.BlockSpec(memory_space=pltpu.HBM)
PARAMS = pltpu.CompilerParams(vmem_limit_bytes=40 * 1024 * 1024)
STRIP = 8


def dot(left, right, contract, precision=HIGH):
    return lax.dot_general(
        left, right, (contract, ((), ())), precision=precision, preferred_element_type=jnp.float32
    )


def dot16(left, right, contract):
    return dot(left, right, contract, lax.Precision.DEFAULT)


def split(value, parts):
    terms = []
    for _ in range(parts):
        terms.append(value.astype(jnp.bfloat16))
        value = value - terms[-1].astype(jnp.float32)
    return terms


def partner(value, axis, step):
    size = lax.axis_size(axis)
    return lax.ppermute(value, axis, [(i, i ^ step) for i in range(size)])


def tree_sum(parts):
    while len(parts) > 1:
        parts = [parts[i] + parts[i + 1] for i in range(0, len(parts), 2)]
    return parts[0]


def group_parts(value, axis, low, high):
    parts = [value]
    while low < high:
        value = tree_sum(parts)
        radix = min(4, high // low)
        parts = [value] + [partner(value, axis, i * low) for i in range(1, radix)]
        low *= radix
    return parts


def spread_rows(value, after):
    n_row, n_col = lax.axis_size("row"), lax.axis_size("col")
    apart = lax.axis_index("row") ^ (lax.axis_index("col") % n_row)
    bits = [1] + [1 << i for i in reversed(range(1, n_row.bit_length() - 1))]
    reached = [0]
    for bit in bits:
        pairs = []
        for c in range(n_col):
            for offset in reached:
                source = (c % n_row) ^ offset
                pairs.append((source * n_col + c, (source ^ bit) * n_col + c))
        reached += [offset ^ bit for offset in reached]
        received = lax.ppermute(value, ("row", "col"), pairs)
        takes = apart & bit != 0
        if bit == bits[-1]:
            return value, received, takes.astype(jnp.int32).reshape(1)
        received, _ = lax.optimization_barrier((received, after))
        value = jnp.where(takes, received, value)


def transpose_grid(value, shift):
    n_row, n_col = lax.axis_size("row"), lax.axis_size("col")
    ratio = n_col // n_row
    pairs = []
    for r in range(n_row):
        for k in range(ratio):
            for q in range(n_row):
                column = (k + shift) % ratio * n_row + r
                row = q if shift % 2 else q ^ (n_row // 2)
                pairs.append((row * n_col + column, r * n_col + k * n_row + q))
    return lax.ppermute(value, ("row", "col"), pairs)


def copy_rows(source, target, sems, first, pieces):
    size = source.shape[0] // pieces
    copies = []
    for piece in range(pieces):
        span = slice(piece * size, (piece + 1) * size)
        copies.append(
            pltpu.make_async_copy(source.at[span, :], target.at[span, :], sems.at[first + piece])
        )
        copies[-1].start()
    return copies


def panel_kernel(ratio, which_ref, panel_ref, matrix_ref, *refs):
    block_refs, refs = refs[:ratio], refs[ratio:]
    mine_ref, held_ref, terms_ref, gram_ref, kept_ref, sems = refs
    width = panel_ref.shape[0]
    pieces = sems.shape[0] // 2
    panel_copies = copy_rows(panel_ref, held_ref, sems, 0, pieces)
    matrix_copies = copy_rows(matrix_ref, kept_ref, sems, pieces, pieces)
    for copy in panel_copies:
        copy.wait()
    which = which_ref[0]
    halves = [[] for _ in range(ratio)]
    for j in range(mine_ref.shape[1] // width):
        start = j * ratio * width
        blocks = [held_ref[:, start + k * width : start + (k + 1) * width] for k in range(ratio)]
        for shift in range(ratio):
            block = blocks[shift]
            for k in range(1, ratio):
                block = jnp.where(which == k, blocks[(k + shift) % ratio], block)
            halves[shift].append(block)
    halves = [jnp.concatenate(half, axis=1) for half in halves]
    mine_ref[...] = halves[0]
    for half, block_ref in zip(halves, block_refs):
        block_ref[...] = jnp.concatenate(split(half, 3), axis=0)
    panel = held_ref[...]
    terms_ref[...] = jnp.concatenate(split(panel, 3), axis=0)
    to_strip(dot(panel, panel, ((1,), (1,))), gram_ref)
    for copy in matrix_copies:
        copy.wait()


def exact_product(terms, value, contract):
    width = terms.shape[0] // 3
    total = 0.0
    for i, part in enumerate(split(value, 3)):
        out = dot16(terms[: (3 - i) * width, :], part, contract)
        for t in range(3 - i):
            total = total + out[t * width : (t + 1) * width, :]
    return total


def product_kernel(terms_ref, matrix_ref, gram_ref, out_ref):
    width = out_ref.shape[0] - STRIP
    rows = matrix_ref.shape[0]
    chunk = 256
    total = jnp.zeros((width, matrix_ref.shape[1]), jnp.float32)
    for start in range(0, rows, chunk):
        span = slice(start, start + chunk)
        total = total + exact_product(terms_ref[:, span], matrix_ref[span, :], ((1,), (0,)))
    out_ref[:width, :] = total
    out_ref[width:, :] = gram_ref[...]


def to_strip(value, strip_ref):
    width = value.shape[0]
    for i in range(width // STRIP):
        strip_ref[:, i * width : (i + 1) * width] = value[i * STRIP : (i + 1) * STRIP, :]


def from_strip(strip, width):
    return jnp.concatenate(
        [strip[:, i * width : (i + 1) * width] for i in range(width // STRIP)], axis=0
    )


def finish_kernel(other_ref, mine_ref, product_ref, gram_ref):
    width = product_ref.shape[0]
    product_ref[...] = mine_ref[:width, :] + other_ref[:width, :]
    gram_ref[...] = from_strip(mine_ref[width:, :] + other_ref[width:, :], width)


def factor_kernel(gram_ref, inverse_ref):
    size = inverse_ref.shape[0]
    batch = 4
    row = lax.broadcasted_iota(jnp.int32, (size, 2 * size), 0)
    lane = lax.broadcasted_iota(jnp.int32, (size, 2 * size), 1)
    eye = jnp.where(row == lane, 1.0, 0.0).astype(jnp.float32)
    table = jnp.concatenate([eye[:, :size], gram_ref[...]], axis=1)
    for first in range(0, size, batch):
        base = first // 8 * 8
        height = size - base
        low = table[base:, :]
        low_row = row[base:, :]
        cols = [
            jnp.broadcast_to(low[:, size + first + t : size + first + t + 1], (height, 2 * size))
            for t in range(batch)
        ]
        rows = [low[first - base + t : first - base + t + 1, :] for t in range(batch)]
        for t in range(batch):
            at = first - base + t
            scale = 1.0 / cols[t][at : at + 1, :]
            factor = jnp.where(low_row > first + t, cols[t] * scale, 0.0)
            for s in range(t + 1, batch):
                cols[s] = cols[s] - factor * cols[s][at : at + 1, :]
                rows[s] = rows[s] - factor[first - base + s : first - base + s + 1, :] * rows[t]
            low = low - factor * rows[t]
        table = low if base == 0 else jnp.concatenate([table[:base, :], low], axis=0)
    diagonal = jnp.sum(jnp.where(lane == row + size, table, 0.0), axis=1, keepdims=True)
    inverse_ref[...] = (table / jnp.sqrt(diagonal))[:, :size]


def stack_left(value):
    high, low = split(value, 2)
    return jnp.concatenate([high, low, high], axis=0)


def stack_right(value):
    high, low = split(value, 2)
    return jnp.concatenate([high, high, low], axis=0)


def basis_kernel(
    matrix_ref, panel_ref, product_cols_ref, inverse_ref, received_ref, held_ref, takes_ref,
    begun_ref, basis_ref, left_ref, coeffs_ref, cols_ref, coeffs_cols_ref,
):
    inverse = inverse_ref[...]
    basis = dot(inverse, panel_ref[...], ((1,), (0,)))
    image_cols = dot(inverse, product_cols_ref[...], ((1,), (0,)))
    basis_ref[...] = basis
    coeffs_ref[...] = dot(inverse, basis, ((0,), (0,)))
    panel_cols = jnp.where(takes_ref[0] != 0, received_ref[...], held_ref[...])
    cols = dot(inverse, panel_cols, ((1,), (0,)))
    cols_ref[...] = cols
    coeffs_cols_ref[...] = dot(inverse, cols, ((0,), (0,)))
    left = stack_left(basis)
    left_ref[...] = left
    right = stack_right(2.0 * image_cols)
    chunk = 256
    for start in range(0, matrix_ref.shape[0], chunk):
        span = slice(start, start + chunk)
        begun_ref[span, :] = matrix_ref[span, :] - dot16(left[:, span], right, ((0,), (0,)))


def inner_kernel(*refs):
    count = len(refs) // 2
    total = 0.0
    for half_ref, block_ref in zip(refs[:count], refs[count:-1]):
        total = total + exact_product(block_ref[...], half_ref[...], ((1,), (1,)))
    refs[-1][...] = total


def image_kernel(ratio, which_ref, begun_ref, cols_ref, inverse_ref, *refs):
    halves, (further_ref, image_ref) = refs[:ratio][::-1], refs[ratio:]
    width = inverse_ref.shape[0]
    which = which_ref[0]
    parts = []
    for j in range(halves[0].shape[1] // width):
        span = slice(j * width, (j + 1) * width)
        for k in range(ratio):
            block = halves[0][:, span]
            for shift in range(1, ratio):
                block = jnp.where((which + shift) % ratio == k, halves[shift][:, span], block)
            parts.append(block)
    image = dot(inverse_ref[...], jnp.concatenate(parts, axis=1), ((1,), (0,)))
    image_ref[...] = image
    left = stack_left(2.0 * image)
    right = stack_right(cols_ref[...])
    chunk = 256
    for start in range(0, begun_ref.shape[0], chunk):
        span = slice(start, start + chunk)
        further_ref[span, :] = begun_ref[span, :] - dot16(left[:, span], right, ((0,), (0,)))


def update_kernel(
    further_ref, image_ref, left_ref, coeffs_ref, coeffs_cols_ref, inverse_ref, *refs
):
    inners, (updated_ref, w_ref, buffer_ref, w_buffer_ref, sems) = refs[:-5], refs[-5:]
    inverse = inverse_ref[...]
    inner = tree_sum([part[...] for part in inners])
    right = dot(inverse, dot(inner, coeffs_cols_ref[...], ((1,), (0,))), ((1,), (0,)))
    right = stack_right(4.0 * right)
    count = sems.shape[0] - 1
    chunk = further_ref.shape[0] // count
    copies = []
    for i in range(count):
        span = slice(i * chunk, (i + 1) * chunk)
        buffer_ref[span, :] = further_ref[span, :] + dot16(left_ref[:, span], right, ((0,), (0,)))
        copies.append(
            pltpu.make_async_copy(buffer_ref.at[span, :], updated_ref.at[span, :], sems.at[i])
        )
        copies[-1].start()
    removed = dot(inverse, dot(inner, coeffs_ref[...], ((0,), (0,))), ((1,), (0,)))
    w_buffer_ref[...] = 2.0 * (image_ref[...] - removed)
    copies.append(pltpu.make_async_copy(w_buffer_ref, w_ref, sems.at[count]))
    copies[-1].start()
    for copy in copies:
        copy.wait()


def shape(*dims, dtype=jnp.float32):
    return jax.ShapeDtypeStruct(dims, dtype)


def call(kernel, outs, args, in_specs=None, out_specs=None, scratch=(), flops=0):
    return pl.pallas_call(
        kernel,
        out_shape=outs,
        in_specs=in_specs or [VMEM] * len(args),
        out_specs=out_specs or ((VMEM,) * len(outs) if isinstance(outs, tuple) else VMEM),
        scratch_shapes=scratch,
        compiler_params=PARAMS,
        cost_estimate=pl.CostEstimate(flops=flops, bytes_accessed=1 << 18, transcendentals=0),
    )(*args)


def local(matrix, panel):
    n_row, n_col = lax.axis_size("row"), lax.axis_size("col")
    ratio = n_col // n_row
    rows, width = panel.shape
    cols = matrix.shape[1]
    which = (lax.axis_index("col") // n_row).astype(jnp.int32).reshape(1)
    chunks = 8

    *blocks, mine, panel_t, terms, gram, kept = call(
        functools.partial(panel_kernel, ratio),
        (
            *[shape(3 * width, cols, dtype=jnp.bfloat16)] * ratio,
            shape(width, cols),
            shape(width, rows),
            shape(3 * width, rows, dtype=jnp.bfloat16),
            shape(STRIP, cols),
            shape(rows, cols),
        ),
        (
            which,
            pltpu.with_memory_space_constraint(panel.T, pltpu.HBM),
            pltpu.with_memory_space_constraint(matrix, pltpu.HBM),
        ),
        in_specs=[SMEM, HBM, HBM],
        scratch=[pltpu.SemaphoreType.DMA((2 * chunks,))],
        flops=1 << 28,
    )
    message = call(
        product_kernel, shape(width + STRIP, cols), (terms, kept, gram), flops=1 << 30
    )
    step = 1
    while 2 * step < n_row:
        message = message + partner(message, "row", step)
        step *= 2
    last = partner(message, "row", step)
    held, received, takes = spread_rows(mine, message)
    product_cols, gram = call(
        finish_kernel, (shape(width, cols), shape(width, width)), (last, message), flops=1 << 24
    )
    halves = [transpose_grid(product_cols, shift) for shift in reversed(range(ratio))]
    inverse = call(factor_kernel, shape(width, width), (gram,), flops=1 << 30)
    begun, basis, left, coeffs, basis_cols, coeffs_cols = call(
        basis_kernel,
        (
            shape(rows, cols),
            shape(width, rows),
            shape(3 * width, rows, dtype=jnp.bfloat16),
            shape(width, rows),
            shape(width, cols),
            shape(width, cols),
        ),
        (kept, panel_t, product_cols, inverse, received, held, takes),
        in_specs=[VMEM] * 6 + [SMEM],
        flops=1 << 30,
    )
    halves, begun = lax.optimization_barrier((halves, begun))
    inner = call(inner_kernel, shape(width, width), (*halves, *blocks[::-1]), flops=1 << 24)
    further, image = call(
        functools.partial(image_kernel, ratio),
        (shape(rows, cols), shape(width, rows)),
        (which, begun, basis_cols, inverse, *halves),
        in_specs=[SMEM] + [VMEM] * (3 + ratio),
        flops=1 << 30,
    )
    inners = group_parts(inner, "row", 1, n_row)[::-1]
    updated, w_rows = call(
        update_kernel,
        (shape(rows, cols), shape(width, rows)),
        (further, image, left, coeffs, coeffs_cols, inverse, *inners),
        out_specs=(HBM, HBM),
        scratch=[
            pltpu.VMEM((rows, cols), jnp.float32),
            pltpu.VMEM((width, rows), jnp.float32),
            pltpu.SemaphoreType.DMA((chunks + 1,)),
        ],
        flops=1 << 30,
    )
    return (updated, w_rows.T, basis.T)


def solution(mesh):
    return jax.shard_map(
        local,
        mesh=mesh,
        in_specs=(P("row", "col"), P("row", None)),
        out_specs=(P("row", "col"), P("row", None), P("row", None)),
        check_vma=False,
    )
```

```python
import functools

import jax
import jax.numpy as jnp
from jax import lax
from jax.experimental import pallas as pl
from jax.experimental.pallas import tpu as pltpu
from jax.sharding import PartitionSpec as P

HIGH = lax.Precision.HIGHEST
VMEM = pl.BlockSpec(memory_space=pltpu.VMEM)
SMEM = pl.BlockSpec(memory_space=pltpu.SMEM)
HBM = pl.BlockSpec(memory_space=pltpu.HBM)
PARAMS = pltpu.CompilerParams(vmem_limit_bytes=20 * 1024 * 1024)
STRIP = 8


def dot(left, right, contract, precision=HIGH):
    return lax.dot_general(
        left, right, (contract, ((), ())), precision=precision, preferred_element_type=jnp.float32
    )


def dot16(left, right, contract):
    return dot(left, right, contract, lax.Precision.DEFAULT)


def split(value, parts):
    terms = []
    for _ in range(parts):
        terms.append(value.astype(jnp.bfloat16))
        value = value - terms[-1].astype(jnp.float32)
    return terms


def partner(value, axis, step):
    size = lax.axis_size(axis)
    return lax.ppermute(value, axis, [(i, i ^ step) for i in range(size)])


def tree_sum(parts):
    while len(parts) > 1:
        parts = [parts[i] + parts[i + 1] for i in range(0, len(parts), 2)]
    return parts[0]


def group_parts(value, axis, low, high):
    parts = [value]
    while low < high:
        value = tree_sum(parts)
        radix = min(4, high // low)
        parts = [value] + [partner(value, axis, i * low) for i in range(1, radix)]
        low *= radix
    return parts


def spread_rows(value, after):
    n_row, n_col = lax.axis_size("row"), lax.axis_size("col")
    apart = lax.axis_index("row") ^ (lax.axis_index("col") % n_row)
    bits = [1] + [1 << i for i in reversed(range(1, n_row.bit_length() - 1))]
    reached = [0]
    for bit in bits:
        pairs = []
        for c in range(n_col):
            for offset in reached:
                source = (c % n_row) ^ offset
                pairs.append((source * n_col + c, (source ^ bit) * n_col + c))
        reached += [offset ^ bit for offset in reached]
        received = lax.ppermute(value, ("row", "col"), pairs)
        takes = apart & bit != 0
        if bit == bits[-1]:
            return value, received, takes.astype(jnp.int32).reshape(1)
        received, _ = lax.optimization_barrier((received, after))
        value = jnp.where(takes, received, value)


def transpose_grid(value, shift):
    n_row, n_col = lax.axis_size("row"), lax.axis_size("col")
    ratio = n_col // n_row
    pairs = []
    for r in range(n_row):
        for k in range(ratio):
            for q in range(n_row):
                column = (k + shift) % ratio * n_row + r
                row = q ^ (n_row // 2) if shift % 2 else q
                pairs.append((row * n_col + column, r * n_col + k * n_row + q))
    return lax.ppermute(value, ("row", "col"), pairs)


def copy_rows(source, target, sems, first, pieces):
    size = source.shape[0] // pieces
    copies = []
    for piece in range(pieces):
        span = slice(piece * size, (piece + 1) * size)
        copies.append(
            pltpu.make_async_copy(source.at[span, :], target.at[span, :], sems.at[first + piece])
        )
        copies[-1].start()
    return copies


def panel_kernel(ratio, which_ref, panel_ref, matrix_ref, *refs):
    block_refs, refs = refs[:ratio], refs[ratio:]
    mine_ref, held_ref, terms_ref, gram_ref, kept_ref, sems = refs
    width = panel_ref.shape[0]
    pieces = sems.shape[0] // 2
    panel_copies = copy_rows(panel_ref, held_ref, sems, 0, pieces)
    matrix_copies = copy_rows(matrix_ref, kept_ref, sems, pieces, pieces)
    for copy in panel_copies:
        copy.wait()
    which = which_ref[0]
    halves = [[] for _ in range(ratio)]
    for j in range(mine_ref.shape[1] // width):
        start = j * ratio * width
        blocks = [held_ref[:, start + k * width : start + (k + 1) * width] for k in range(ratio)]
        for shift in range(ratio):
            block = blocks[shift]
            for k in range(1, ratio):
                block = jnp.where(which == k, blocks[(k + shift) % ratio], block)
            halves[shift].append(block)
    halves = [jnp.concatenate(half, axis=1) for half in halves]
    mine_ref[...] = halves[0]
    for half, block_ref in zip(halves, block_refs):
        block_ref[...] = jnp.concatenate(split(half, 3), axis=0)
    panel = held_ref[...]
    terms_ref[...] = jnp.concatenate(split(panel, 3), axis=0)
    to_strip(dot(panel, panel, ((1,), (1,))), gram_ref)
    for copy in matrix_copies:
        copy.wait()


def exact_product(terms, value, contract):
    width = terms.shape[0] // 3
    total = 0.0
    for i, part in enumerate(split(value, 3)):
        out = dot16(terms[: (3 - i) * width, :], part, contract)
        for t in range(3 - i):
            total = total + out[t * width : (t + 1) * width, :]
    return total


def product_kernel(terms_ref, matrix_ref, gram_ref, out_ref):
    width = out_ref.shape[0] - STRIP
    rows = matrix_ref.shape[0]
    chunk = 256
    total = jnp.zeros((width, matrix_ref.shape[1]), jnp.float32)
    for start in range(0, rows, chunk):
        span = slice(start, start + chunk)
        total = total + exact_product(terms_ref[:, span], matrix_ref[span, :], ((1,), (0,)))
    out_ref[:width, :] = total
    out_ref[width:, :] = gram_ref[...]


def to_strip(value, strip_ref):
    width = value.shape[0]
    for i in range(width // STRIP):
        strip_ref[:, i * width : (i + 1) * width] = value[i * STRIP : (i + 1) * STRIP, :]


def from_strip(strip, width):
    return jnp.concatenate(
        [strip[:, i * width : (i + 1) * width] for i in range(width // STRIP)], axis=0
    )


def finish_kernel(other_ref, mine_ref, product_ref, gram_ref):
    width = product_ref.shape[0]
    product_ref[...] = mine_ref[:width, :] + other_ref[:width, :]
    gram_ref[...] = from_strip(mine_ref[width:, :] + other_ref[width:, :], width)


def factor_kernel(gram_ref, inverse_ref):
    size = inverse_ref.shape[0]
    batch = 4
    row = lax.broadcasted_iota(jnp.int32, (size, 2 * size), 0)
    lane = lax.broadcasted_iota(jnp.int32, (size, 2 * size), 1)
    eye = jnp.where(row == lane, 1.0, 0.0).astype(jnp.float32)
    table = jnp.concatenate([eye[:, :size], gram_ref[...]], axis=1)
    for first in range(0, size, batch):
        base = first // 8 * 8
        height = size - base
        low = table[base:, :]
        low_row = row[base:, :]
        cols = [
            jnp.broadcast_to(low[:, size + first + t : size + first + t + 1], (height, 2 * size))
            for t in range(batch)
        ]
        rows = [low[first - base + t : first - base + t + 1, :] for t in range(batch)]
        for t in range(batch):
            at = first - base + t
            scale = 1.0 / cols[t][at : at + 1, :]
            factor = jnp.where(low_row > first + t, cols[t] * scale, 0.0)
            for s in range(t + 1, batch):
                cols[s] = cols[s] - factor * cols[s][at : at + 1, :]
                rows[s] = rows[s] - factor[first - base + s : first - base + s + 1, :] * rows[t]
            low = low - factor * rows[t]
        table = low if base == 0 else jnp.concatenate([table[:base, :], low], axis=0)
    diagonal = jnp.sum(jnp.where(lane == row + size, table, 0.0), axis=1, keepdims=True)
    inverse_ref[...] = (table / jnp.sqrt(diagonal))[:, :size]


def stack_left(value):
    high, low = split(value, 2)
    return jnp.concatenate([high, low, high], axis=0)


def stack_right(value):
    high, low = split(value, 2)
    return jnp.concatenate([high, high, low], axis=0)


def basis_kernel(
    matrix_ref, panel_ref, product_cols_ref, inverse_ref, received_ref, held_ref, takes_ref,
    begun_ref, basis_ref, left_ref, coeffs_ref, cols_ref, coeffs_cols_ref,
):
    inverse = inverse_ref[...]
    basis = dot(inverse, panel_ref[...], ((1,), (0,)))
    image_cols = dot(inverse, product_cols_ref[...], ((1,), (0,)))
    basis_ref[...] = basis
    coeffs_ref[...] = dot(inverse, basis, ((0,), (0,)))
    panel_cols = jnp.where(takes_ref[0] != 0, received_ref[...], held_ref[...])
    cols = dot(inverse, panel_cols, ((1,), (0,)))
    cols_ref[...] = cols
    coeffs_cols_ref[...] = dot(inverse, cols, ((0,), (0,)))
    left = stack_left(basis)
    left_ref[...] = left
    right = stack_right(2.0 * image_cols)
    chunk = 256
    for start in range(0, matrix_ref.shape[0], chunk):
        span = slice(start, start + chunk)
        begun_ref[span, :] = matrix_ref[span, :] - dot16(left[:, span], right, ((0,), (0,)))


def inner_kernel(*refs):
    count = len(refs) // 2
    total = 0.0
    for half_ref, block_ref in zip(refs[:count], refs[count:-1]):
        total = total + exact_product(block_ref[...], half_ref[...], ((1,), (1,)))
    refs[-1][...] = total


def image_kernel(ratio, which_ref, begun_ref, cols_ref, inverse_ref, *refs):
    halves, (further_ref, image_ref) = refs[:ratio][::-1], refs[ratio:]
    width = inverse_ref.shape[0]
    which = which_ref[0]
    parts = []
    for j in range(halves[0].shape[1] // width):
        span = slice(j * width, (j + 1) * width)
        for k in range(ratio):
            block = halves[0][:, span]
            for shift in range(1, ratio):
                block = jnp.where((which + shift) % ratio == k, halves[shift][:, span], block)
            parts.append(block)
    image = dot(inverse_ref[...], jnp.concatenate(parts, axis=1), ((1,), (0,)))
    image_ref[...] = image
    left = stack_left(2.0 * image)
    right = stack_right(cols_ref[...])
    chunk = 256
    for start in range(0, begun_ref.shape[0], chunk):
        span = slice(start, start + chunk)
        further_ref[span, :] = begun_ref[span, :] - dot16(left[:, span], right, ((0,), (0,)))


def update_kernel(
    further_ref, image_ref, left_ref, coeffs_ref, coeffs_cols_ref, inverse_ref, *refs
):
    inners, (updated_ref, w_ref, buffer_ref, w_buffer_ref, sems) = refs[:-5], refs[-5:]
    inverse = inverse_ref[...]
    inner = tree_sum([part[...] for part in inners])
    right = dot(inverse, dot(inner, coeffs_cols_ref[...], ((1,), (0,))), ((1,), (0,)))
    right = stack_right(4.0 * right)
    count = sems.shape[0] - 1
    chunk = further_ref.shape[0] // count
    copies = []
    for i in range(count):
        span = slice(i * chunk, (i + 1) * chunk)
        buffer_ref[span, :] = further_ref[span, :] + dot16(left_ref[:, span], right, ((0,), (0,)))
        copies.append(
            pltpu.make_async_copy(buffer_ref.at[span, :], updated_ref.at[span, :], sems.at[i])
        )
        copies[-1].start()
    removed = dot(inverse, dot(inner, coeffs_ref[...], ((0,), (0,))), ((1,), (0,)))
    w_buffer_ref[...] = 2.0 * (image_ref[...] - removed)
    copies.append(pltpu.make_async_copy(w_buffer_ref, w_ref, sems.at[count]))
    copies[-1].start()
    for copy in copies:
        copy.wait()


def shape(*dims, dtype=jnp.float32):
    return jax.ShapeDtypeStruct(dims, dtype)


def call(kernel, outs, args, in_specs=None, out_specs=None, scratch=(), flops=0):
    return pl.pallas_call(
        kernel,
        out_shape=outs,
        in_specs=in_specs or [VMEM] * len(args),
        out_specs=out_specs or ((VMEM,) * len(outs) if isinstance(outs, tuple) else VMEM),
        scratch_shapes=scratch,
        compiler_params=PARAMS,
        cost_estimate=pl.CostEstimate(flops=flops, bytes_accessed=1 << 18, transcendentals=0),
    )(*args)


def local(matrix, panel):
    n_row, n_col = lax.axis_size("row"), lax.axis_size("col")
    ratio = n_col // n_row
    rows, width = panel.shape
    cols = matrix.shape[1]
    which = (lax.axis_index("col") // n_row).astype(jnp.int32).reshape(1)
    chunks = 8

    *blocks, mine, panel_t, terms, gram, kept = call(
        functools.partial(panel_kernel, ratio),
        (
            *[shape(3 * width, cols, dtype=jnp.bfloat16)] * ratio,
            shape(width, cols),
            shape(width, rows),
            shape(3 * width, rows, dtype=jnp.bfloat16),
            shape(STRIP, cols),
            shape(rows, cols),
        ),
        (
            which,
            pltpu.with_memory_space_constraint(panel.T, pltpu.HBM),
            pltpu.with_memory_space_constraint(matrix, pltpu.HBM),
        ),
        in_specs=[SMEM, HBM, HBM],
        scratch=[pltpu.SemaphoreType.DMA((2 * chunks,))],
        flops=1 << 28,
    )
    message = call(
        product_kernel, shape(width + STRIP, cols), (terms, kept, gram), flops=1 << 30
    )
    step = 1
    while 2 * step < n_row:
        message = message + partner(message, "row", step)
        step *= 2
    last = partner(message, "row", step)
    held, received, takes = spread_rows(mine, message)
    product_cols, gram = call(
        finish_kernel, (shape(width, cols), shape(width, width)), (last, message), flops=1 << 24
    )
    halves = [transpose_grid(product_cols, shift) for shift in reversed(range(ratio))]
    inverse = call(factor_kernel, shape(width, width), (gram,), flops=1 << 30)
    begun, basis, left, coeffs, basis_cols, coeffs_cols = call(
        basis_kernel,
        (
            shape(rows, cols),
            shape(width, rows),
            shape(3 * width, rows, dtype=jnp.bfloat16),
            shape(width, rows),
            shape(width, cols),
            shape(width, cols),
        ),
        (kept, panel_t, product_cols, inverse, received, held, takes),
        in_specs=[VMEM] * 6 + [SMEM],
        flops=1 << 30,
    )
    halves, begun = lax.optimization_barrier((halves, begun))
    inner = call(inner_kernel, shape(width, width), (*halves, *blocks[::-1]), flops=1 << 24)
    further, image = call(
        functools.partial(image_kernel, ratio),
        (shape(rows, cols), shape(width, rows)),
        (which, begun, basis_cols, inverse, *halves),
        in_specs=[SMEM] + [VMEM] * (3 + ratio),
        flops=1 << 30,
    )
    inners = group_parts(inner, "row", 1, n_row)[::-1]
    updated, w_rows = call(
        update_kernel,
        (shape(rows, cols), shape(width, rows)),
        (further, image, left, coeffs, coeffs_cols, inverse, *inners),
        out_specs=(HBM, HBM),
        scratch=[
            pltpu.VMEM((rows, cols), jnp.float32),
            pltpu.VMEM((width, rows), jnp.float32),
            pltpu.SemaphoreType.DMA((chunks + 1,)),
        ],
        flops=1 << 30,
    )
    return (updated, w_rows.T, basis.T)


def solution(mesh):
    return jax.shard_map(
        local,
        mesh=mesh,
        in_specs=(P("row", "col"), P("row", None)),
        out_specs=(P("row", "col"), P("row", None), P("row", None)),
        check_vma=False,
    )
```

```python
import functools

import jax
import jax.numpy as jnp
from jax import lax
from jax.experimental import pallas as pl
from jax.experimental.pallas import tpu as pltpu
from jax.sharding import PartitionSpec as P

HIGH = lax.Precision.HIGHEST
VMEM = pl.BlockSpec(memory_space=pltpu.VMEM)
SMEM = pl.BlockSpec(memory_space=pltpu.SMEM)
HBM = pl.BlockSpec(memory_space=pltpu.HBM)
PARAMS = pltpu.CompilerParams(vmem_limit_bytes=40 * 1024 * 1024)
STRIP = 8


def dot(left, right, contract, precision=HIGH):
    return lax.dot_general(
        left, right, (contract, ((), ())), precision=precision, preferred_element_type=jnp.float32
    )


def dot16(left, right, contract):
    return dot(left, right, contract, lax.Precision.DEFAULT)


def split(value, parts):
    terms = []
    for _ in range(parts):
        terms.append(value.astype(jnp.bfloat16))
        value = value - terms[-1].astype(jnp.float32)
    return terms


def partner(value, axis, step):
    size = lax.axis_size(axis)
    return lax.ppermute(value, axis, [(i, i ^ step) for i in range(size)])


def tree_sum(parts):
    while len(parts) > 1:
        parts = [parts[i] + parts[i + 1] for i in range(0, len(parts), 2)]
    return parts[0]


def group_parts(value, axis, low, high):
    parts = [value]
    while low < high:
        value = tree_sum(parts)
        radix = min(4, high // low)
        parts = [value] + [partner(value, axis, i * low) for i in range(1, radix)]
        low *= radix
    return parts


def spread_rows(value, after):
    n_row, n_col = lax.axis_size("row"), lax.axis_size("col")
    apart = lax.axis_index("row") ^ (lax.axis_index("col") % n_row)
    bits = [1] + [1 << i for i in reversed(range(1, n_row.bit_length() - 1))]
    reached = [0]
    for bit in bits:
        pairs = []
        for c in range(n_col):
            for offset in reached:
                source = (c % n_row) ^ offset
                pairs.append((source * n_col + c, (source ^ bit) * n_col + c))
        reached += [offset ^ bit for offset in reached]
        received = lax.ppermute(value, ("row", "col"), pairs)
        takes = apart & bit != 0
        if bit == bits[-1]:
            return value, received, takes.astype(jnp.int32).reshape(1)
        received, _ = lax.optimization_barrier((received, after))
        value = jnp.where(takes, received, value)


def transpose_grid(value, shift):
    n_row, n_col = lax.axis_size("row"), lax.axis_size("col")
    ratio = n_col // n_row
    pairs = []
    for r in range(n_row):
        for k in range(ratio):
            for q in range(n_row):
                column = (k + shift) % ratio * n_row + r
                row = q if shift % 2 else q ^ (n_row // 2)
                pairs.append((row * n_col + column, r * n_col + k * n_row + q))
    return lax.ppermute(value, ("row", "col"), pairs)


def copy_rows(source, target, sems, first, pieces):
    size = source.shape[0] // pieces
    copies = []
    for piece in range(pieces):
        span = slice(piece * size, (piece + 1) * size)
        copies.append(
            pltpu.make_async_copy(source.at[span, :], target.at[span, :], sems.at[first + piece])
        )
        copies[-1].start()
    return copies


def panel_kernel(ratio, which_ref, panel_ref, matrix_ref, *refs):
    mine_refs, (held_ref, terms_ref, gram_ref, kept_ref, sems) = refs[:ratio], refs[ratio:]
    width = panel_ref.shape[0]
    pieces = sems.shape[0] // 2
    panel_copies = copy_rows(panel_ref, held_ref, sems, 0, pieces)
    matrix_copies = copy_rows(matrix_ref, kept_ref, sems, pieces, pieces)
    for copy in panel_copies:
        copy.wait()
    which = which_ref[0]
    for j in range(mine_refs[0].shape[1] // width):
        start = j * ratio * width
        blocks = [held_ref[:, start + k * width : start + (k + 1) * width] for k in range(ratio)]
        for shift, mine_ref in enumerate(mine_refs):
            block = blocks[shift]
            for k in range(1, ratio):
                block = jnp.where(which == k, blocks[(k + shift) % ratio], block)
            mine_ref[:, j * width : (j + 1) * width] = block
    panel = held_ref[...]
    terms_ref[...] = jnp.concatenate(split(panel, 3), axis=0)
    to_strip(dot(panel, panel, ((1,), (1,))), gram_ref)
    for copy in matrix_copies:
        copy.wait()


def product_kernel(terms_ref, matrix_ref, gram_ref, out_ref):
    width = out_ref.shape[0] - STRIP
    rows = matrix_ref.shape[0]
    chunk = 256
    total = jnp.zeros((width, matrix_ref.shape[1]), jnp.float32)
    for start in range(0, rows, chunk):
        span = slice(start, start + chunk)
        parts = split(matrix_ref[span, :], 3)
        for i, part in enumerate(parts):
            count = 3 - i
            out = dot16(terms_ref[: count * width, span], part, ((1,), (0,)))
            for t in range(count):
                total = total + out[t * width : (t + 1) * width, :]
    out_ref[:width, :] = total
    out_ref[width:, :] = gram_ref[...]


def to_strip(value, strip_ref):
    width = value.shape[0]
    for i in range(width // STRIP):
        strip_ref[:, i * width : (i + 1) * width] = value[i * STRIP : (i + 1) * STRIP, :]


def from_strip(strip, width):
    return jnp.concatenate(
        [strip[:, i * width : (i + 1) * width] for i in range(width // STRIP)], axis=0
    )


def finish_kernel(other_ref, mine_ref, product_ref, gram_ref):
    width = product_ref.shape[0]
    product_ref[...] = mine_ref[:width, :] + other_ref[:width, :]
    gram_ref[...] = from_strip(mine_ref[width:, :] + other_ref[width:, :], width)


def factor_kernel(gram_ref, inverse_ref):
    size = inverse_ref.shape[0]
    batch = 4
    row = lax.broadcasted_iota(jnp.int32, (size, 2 * size), 0)
    lane = lax.broadcasted_iota(jnp.int32, (size, 2 * size), 1)
    eye = jnp.where(row == lane, 1.0, 0.0).astype(jnp.float32)
    table = jnp.concatenate([eye[:, :size], gram_ref[...]], axis=1)
    for first in range(0, size, batch):
        base = first // 8 * 8
        height = size - base
        low = table[base:, :]
        low_row = row[base:, :]
        cols = [
            jnp.broadcast_to(low[:, size + first + t : size + first + t + 1], (height, 2 * size))
            for t in range(batch)
        ]
        rows = [low[first - base + t : first - base + t + 1, :] for t in range(batch)]
        for t in range(batch):
            at = first - base + t
            scale = 1.0 / cols[t][at : at + 1, :]
            factor = jnp.where(low_row > first + t, cols[t] * scale, 0.0)
            for s in range(t + 1, batch):
                cols[s] = cols[s] - factor * cols[s][at : at + 1, :]
                rows[s] = rows[s] - factor[first - base + s : first - base + s + 1, :] * rows[t]
            low = low - factor * rows[t]
        table = low if base == 0 else jnp.concatenate([table[:base, :], low], axis=0)
    diagonal = jnp.sum(jnp.where(lane == row + size, table, 0.0), axis=1, keepdims=True)
    inverse_ref[...] = (table / jnp.sqrt(diagonal))[:, :size]


def stack_left(value):
    high, low = split(value, 2)
    return jnp.concatenate([high, low, high], axis=0)


def stack_right(value):
    high, low = split(value, 2)
    return jnp.concatenate([high, high, low], axis=0)


def basis_kernel(
    matrix_ref, panel_ref, product_cols_ref, inverse_ref,
    begun_ref, basis_ref, left_ref, coeffs_ref,
):
    inverse = inverse_ref[...]
    basis = dot(inverse, panel_ref[...], ((1,), (0,)))
    image_cols = dot(inverse, product_cols_ref[...], ((1,), (0,)))
    basis_ref[...] = basis
    coeffs_ref[...] = dot(inverse, basis, ((0,), (0,)))
    left = stack_left(basis)
    left_ref[...] = left
    right = stack_right(2.0 * image_cols)
    chunk = 256
    for start in range(0, matrix_ref.shape[0], chunk):
        span = slice(start, start + chunk)
        begun_ref[span, :] = matrix_ref[span, :] - dot16(left[:, span], right, ((0,), (0,)))


def columns_kernel(inverse_ref, received_ref, held_ref, takes_ref, cols_ref, coeffs_cols_ref):
    inverse = inverse_ref[...]
    panel_cols = jnp.where(takes_ref[0] != 0, received_ref[...], held_ref[...])
    cols = dot(inverse, panel_cols, ((1,), (0,)))
    cols_ref[...] = cols
    coeffs_cols_ref[...] = dot(inverse, cols, ((0,), (0,)))


def inner_kernel(*refs):
    count = len(refs) // 2
    inner_ref = refs[-1]
    inner_ref[...] = sum(
        dot(refs[count + i][...], refs[i][...], ((1,), (1,))) for i in range(count)
    )


def image_kernel(ratio, which_ref, begun_ref, cols_ref, inverse_ref, *refs):
    halves, (further_ref, image_ref) = refs[:ratio][::-1], refs[ratio:]
    width = inverse_ref.shape[0]
    which = which_ref[0]
    parts = []
    for j in range(halves[0].shape[1] // width):
        span = slice(j * width, (j + 1) * width)
        for k in range(ratio):
            block = halves[0][:, span]
            for shift in range(1, ratio):
                block = jnp.where((which + shift) % ratio == k, halves[shift][:, span], block)
            parts.append(block)
    image = dot(inverse_ref[...], jnp.concatenate(parts, axis=1), ((1,), (0,)))
    image_ref[...] = image
    left = stack_left(2.0 * image)
    right = stack_right(cols_ref[...])
    chunk = 256
    for start in range(0, begun_ref.shape[0], chunk):
        span = slice(start, start + chunk)
        further_ref[span, :] = begun_ref[span, :] - dot16(left[:, span], right, ((0,), (0,)))


def update_kernel(
    further_ref, image_ref, left_ref, coeffs_ref, coeffs_cols_ref, inverse_ref, *refs
):
    inners, (updated_ref, w_ref, buffer_ref, w_buffer_ref, sems) = refs[:-5], refs[-5:]
    inverse = inverse_ref[...]
    inner = tree_sum([part[...] for part in inners])
    right = dot(inverse, dot(inner, coeffs_cols_ref[...], ((1,), (0,))), ((1,), (0,)))
    right = stack_right(4.0 * right)
    count = sems.shape[0] - 1
    chunk = further_ref.shape[0] // count
    copies = []
    for i in range(count):
        span = slice(i * chunk, (i + 1) * chunk)
        buffer_ref[span, :] = further_ref[span, :] + dot16(left_ref[:, span], right, ((0,), (0,)))
        copies.append(
            pltpu.make_async_copy(buffer_ref.at[span, :], updated_ref.at[span, :], sems.at[i])
        )
        copies[-1].start()
    removed = dot(inverse, dot(inner, coeffs_ref[...], ((0,), (0,))), ((1,), (0,)))
    w_buffer_ref[...] = 2.0 * (image_ref[...] - removed)
    copies.append(pltpu.make_async_copy(w_buffer_ref, w_ref, sems.at[count]))
    copies[-1].start()
    for copy in copies:
        copy.wait()


def shape(*dims, dtype=jnp.float32):
    return jax.ShapeDtypeStruct(dims, dtype)


def call(kernel, outs, args, in_specs=None, out_specs=None, scratch=(), flops=0):
    return pl.pallas_call(
        kernel,
        out_shape=outs,
        in_specs=in_specs or [VMEM] * len(args),
        out_specs=out_specs or ((VMEM,) * len(outs) if isinstance(outs, tuple) else VMEM),
        scratch_shapes=scratch,
        compiler_params=PARAMS,
        cost_estimate=pl.CostEstimate(flops=flops, bytes_accessed=1 << 18, transcendentals=0),
    )(*args)


def local(matrix, panel):
    n_row, n_col = lax.axis_size("row"), lax.axis_size("col")
    ratio = n_col // n_row
    rows, width = panel.shape
    cols = matrix.shape[1]
    which = (lax.axis_index("col") // n_row).astype(jnp.int32).reshape(1)
    chunks = 8

    *mines, panel_t, terms, gram, kept = call(
        functools.partial(panel_kernel, ratio),
        (
            *[shape(width, cols)] * ratio,
            shape(width, rows),
            shape(3 * width, rows, dtype=jnp.bfloat16),
            shape(STRIP, cols),
            shape(rows, cols),
        ),
        (
            which,
            pltpu.with_memory_space_constraint(panel.T, pltpu.HBM),
            pltpu.with_memory_space_constraint(matrix, pltpu.HBM),
        ),
        in_specs=[SMEM, HBM, HBM],
        scratch=[pltpu.SemaphoreType.DMA((2 * chunks,))],
        flops=1 << 28,
    )
    message = call(
        product_kernel, shape(width + STRIP, cols), (terms, kept, gram), flops=1 << 30
    )
    step = 1
    while 2 * step < n_row:
        message = message + partner(message, "row", step)
        step *= 2
    last = partner(message, "row", step)
    product_cols, gram = call(
        finish_kernel, (shape(width, cols), shape(width, width)), (last, message), flops=1 << 24
    )
    halves = [transpose_grid(product_cols, shift) for shift in reversed(range(ratio))]
    held, received, takes = spread_rows(mines[0], product_cols)
    inverse = call(factor_kernel, shape(width, width), (gram,), flops=1 << 30)
    begun, basis, left, coeffs = call(
        basis_kernel,
        (
            shape(rows, cols),
            shape(width, rows),
            shape(3 * width, rows, dtype=jnp.bfloat16),
            shape(width, rows),
        ),
        (kept, panel_t, product_cols, inverse),
        flops=1 << 30,
    )
    halves, begun = lax.optimization_barrier((halves, begun))
    inner = call(inner_kernel, shape(width, width), (*halves, *mines[::-1]), flops=1 << 24)
    received, _ = lax.optimization_barrier((received, inner))
    basis_cols, coeffs_cols = call(
        columns_kernel,
        (shape(width, cols), shape(width, cols)),
        (inverse, received, held, takes),
        in_specs=[VMEM] * 3 + [SMEM],
        flops=1 << 24,
    )
    further, image = call(
        functools.partial(image_kernel, ratio),
        (shape(rows, cols), shape(width, rows)),
        (which, begun, basis_cols, inverse, *halves),
        in_specs=[SMEM] + [VMEM] * (3 + ratio),
        flops=1 << 30,
    )
    inners = group_parts(inner, "row", 1, n_row)[::-1]
    updated, w_rows = call(
        update_kernel,
        (shape(rows, cols), shape(width, rows)),
        (further, image, left, coeffs, coeffs_cols, inverse, *inners),
        out_specs=(HBM, HBM),
        scratch=[
            pltpu.VMEM((rows, cols), jnp.float32),
            pltpu.VMEM((width, rows), jnp.float32),
            pltpu.SemaphoreType.DMA((chunks + 1,)),
        ],
        flops=1 << 30,
    )
    return (updated, w_rows.T, basis.T)


def solution(mesh):
    return jax.shard_map(
        local,
        mesh=mesh,
        in_specs=(P("row", "col"), P("row", None)),
        out_specs=(P("row", "col"), P("row", None), P("row", None)),
        check_vma=False,
    )
```

```python
import functools

import jax
import jax.numpy as jnp
from jax import lax
from jax.experimental import pallas as pl
from jax.experimental.pallas import tpu as pltpu
from jax.sharding import PartitionSpec as P

HIGH = lax.Precision.HIGHEST
VMEM = pl.BlockSpec(memory_space=pltpu.VMEM)
SMEM = pl.BlockSpec(memory_space=pltpu.SMEM)
HBM = pl.BlockSpec(memory_space=pltpu.HBM)
PARAMS = pltpu.CompilerParams(vmem_limit_bytes=40 * 1024 * 1024)
STRIP = 8


def dot(left, right, contract, precision=HIGH):
    return lax.dot_general(
        left, right, (contract, ((), ())), precision=precision, preferred_element_type=jnp.float32
    )


def dot16(left, right, contract):
    return dot(left, right, contract, lax.Precision.DEFAULT)


def split(value, parts):
    terms = []
    for _ in range(parts):
        terms.append(value.astype(jnp.bfloat16))
        value = value - terms[-1].astype(jnp.float32)
    return terms


def partner(value, axis, step):
    size = lax.axis_size(axis)
    return lax.ppermute(value, axis, [(i, i ^ step) for i in range(size)])


def tree_sum(parts):
    while len(parts) > 1:
        parts = [parts[i] + parts[i + 1] for i in range(0, len(parts), 2)]
    return parts[0]


def group_parts(value, axis, low, high):
    parts = [value]
    while low < high:
        value = tree_sum(parts)
        radix = min(4, high // low)
        parts = [value] + [partner(value, axis, i * low) for i in range(1, radix)]
        low *= radix
    return parts


def spread_rows(value, after):
    n_row, n_col = lax.axis_size("row"), lax.axis_size("col")
    apart = lax.axis_index("row") ^ (lax.axis_index("col") % n_row)
    bits = [1] + [1 << i for i in reversed(range(1, n_row.bit_length() - 1))]
    reached = [0]
    for bit in bits:
        pairs = []
        for c in range(n_col):
            for offset in reached:
                source = (c % n_row) ^ offset
                pairs.append((source * n_col + c, (source ^ bit) * n_col + c))
        reached += [offset ^ bit for offset in reached]
        received = lax.ppermute(value, ("row", "col"), pairs)
        takes = apart & bit != 0
        if bit == bits[-1]:
            return value, received, takes.astype(jnp.int32).reshape(1)
        received, _ = lax.optimization_barrier((received, after))
        value = jnp.where(takes, received, value)


def transpose_grid(value, shift):
    n_row, n_col = lax.axis_size("row"), lax.axis_size("col")
    ratio = n_col // n_row
    pairs = []
    for r in range(n_row):
        for k in range(ratio):
            for q in range(n_row):
                column = (k + shift) % ratio * n_row + r
                row = q if shift % 2 else q ^ (n_row // 2)
                pairs.append((row * n_col + column, r * n_col + k * n_row + q))
    return lax.ppermute(value, ("row", "col"), pairs)


def copy_rows(source, target, sems, first, pieces):
    size = source.shape[0] // pieces
    copies = []
    for piece in range(pieces):
        span = slice(piece * size, (piece + 1) * size)
        copies.append(
            pltpu.make_async_copy(source.at[span, :], target.at[span, :], sems.at[first + piece])
        )
        copies[-1].start()
    return copies


def panel_kernel(ratio, which_ref, panel_ref, matrix_ref, *refs):
    mine_refs, (held_ref, terms_ref, gram_ref, kept_ref, sems) = refs[:ratio], refs[ratio:]
    width = panel_ref.shape[0]
    pieces = sems.shape[0] // 2
    panel_copies = copy_rows(panel_ref, held_ref, sems, 0, pieces)
    matrix_copies = copy_rows(matrix_ref, kept_ref, sems, pieces, pieces)
    for copy in panel_copies:
        copy.wait()
    which = which_ref[0]
    for j in range(mine_refs[0].shape[1] // width):
        start = j * ratio * width
        blocks = [held_ref[:, start + k * width : start + (k + 1) * width] for k in range(ratio)]
        for shift, mine_ref in enumerate(mine_refs):
            block = blocks[shift]
            for k in range(1, ratio):
                block = jnp.where(which == k, blocks[(k + shift) % ratio], block)
            mine_ref[:, j * width : (j + 1) * width] = block
    panel = held_ref[...]
    terms_ref[...] = jnp.concatenate(split(panel, 3), axis=0)
    to_strip(dot(panel, panel, ((1,), (1,))), gram_ref)
    for copy in matrix_copies:
        copy.wait()


def product_kernel(terms_ref, matrix_ref, gram_ref, out_ref):
    width = out_ref.shape[0] - STRIP
    rows = matrix_ref.shape[0]
    chunk = 256
    total = jnp.zeros((width, matrix_ref.shape[1]), jnp.float32)
    for start in range(0, rows, chunk):
        span = slice(start, start + chunk)
        parts = split(matrix_ref[span, :], 3)
        for i, part in enumerate(parts):
            count = 3 - i
            out = dot16(terms_ref[: count * width, span], part, ((1,), (0,)))
            for t in range(count):
                total = total + out[t * width : (t + 1) * width, :]
    out_ref[:width, :] = total
    out_ref[width:, :] = gram_ref[...]


def to_strip(value, strip_ref):
    width = value.shape[0]
    for i in range(width // STRIP):
        strip_ref[:, i * width : (i + 1) * width] = value[i * STRIP : (i + 1) * STRIP, :]


def from_strip(strip, width):
    return jnp.concatenate(
        [strip[:, i * width : (i + 1) * width] for i in range(width // STRIP)], axis=0
    )


def finish_kernel(other_ref, mine_ref, product_ref, gram_ref):
    width = product_ref.shape[0]
    product_ref[...] = mine_ref[:width, :] + other_ref[:width, :]
    gram_ref[...] = from_strip(mine_ref[width:, :] + other_ref[width:, :], width)


def factor_kernel(gram_ref, inverse_ref):
    size = inverse_ref.shape[0]
    batch = 4
    row = lax.broadcasted_iota(jnp.int32, (size, 2 * size), 0)
    lane = lax.broadcasted_iota(jnp.int32, (size, 2 * size), 1)
    eye = jnp.where(row == lane, 1.0, 0.0).astype(jnp.float32)
    table = jnp.concatenate([eye[:, :size], gram_ref[...]], axis=1)
    for first in range(0, size, batch):
        base = first // 8 * 8
        height = size - base
        low = table[base:, :]
        low_row = row[base:, :]
        cols = [
            jnp.broadcast_to(low[:, size + first + t : size + first + t + 1], (height, 2 * size))
            for t in range(batch)
        ]
        rows = [low[first - base + t : first - base + t + 1, :] for t in range(batch)]
        for t in range(batch):
            at = first - base + t
            scale = 1.0 / cols[t][at : at + 1, :]
            factor = jnp.where(low_row > first + t, cols[t] * scale, 0.0)
            for s in range(t + 1, batch):
                cols[s] = cols[s] - factor * cols[s][at : at + 1, :]
                rows[s] = rows[s] - factor[first - base + s : first - base + s + 1, :] * rows[t]
            low = low - factor * rows[t]
        table = low if base == 0 else jnp.concatenate([table[:base, :], low], axis=0)
    diagonal = jnp.sum(jnp.where(lane == row + size, table, 0.0), axis=1, keepdims=True)
    inverse_ref[...] = (table / jnp.sqrt(diagonal))[:, :size]


def stack_left(value):
    high, low = split(value, 2)
    return jnp.concatenate([high, low, high], axis=0)


def stack_right(value):
    high, low = split(value, 2)
    return jnp.concatenate([high, high, low], axis=0)


def basis_kernel(
    matrix_ref, panel_ref, product_cols_ref, inverse_ref,
    begun_ref, basis_ref, left_ref, coeffs_ref,
):
    inverse = inverse_ref[...]
    basis = dot(inverse, panel_ref[...], ((1,), (0,)))
    image_cols = dot(inverse, product_cols_ref[...], ((1,), (0,)))
    basis_ref[...] = basis
    coeffs_ref[...] = dot(inverse, basis, ((0,), (0,)))
    left = stack_left(basis)
    left_ref[...] = left
    right = stack_right(2.0 * image_cols)
    chunk = 256
    for start in range(0, matrix_ref.shape[0], chunk):
        span = slice(start, start + chunk)
        begun_ref[span, :] = matrix_ref[span, :] - dot16(left[:, span], right, ((0,), (0,)))


def columns_kernel(inverse_ref, received_ref, held_ref, takes_ref, cols_ref, coeffs_cols_ref):
    inverse = inverse_ref[...]
    panel_cols = jnp.where(takes_ref[0] != 0, received_ref[...], held_ref[...])
    cols = dot(inverse, panel_cols, ((1,), (0,)))
    cols_ref[...] = cols
    coeffs_cols_ref[...] = dot(inverse, cols, ((0,), (0,)))


def inner_kernel(*refs):
    count = len(refs) // 2
    inner_ref = refs[-1]
    inner_ref[...] = sum(
        dot(refs[count + i][...], refs[i][...], ((1,), (1,))) for i in range(count)
    )


def image_kernel(ratio, which_ref, begun_ref, cols_ref, inverse_ref, *refs):
    halves, (further_ref, image_ref) = refs[:ratio][::-1], refs[ratio:]
    width = inverse_ref.shape[0]
    which = which_ref[0]
    parts = []
    for j in range(halves[0].shape[1] // width):
        span = slice(j * width, (j + 1) * width)
        for k in range(ratio):
            block = halves[0][:, span]
            for shift in range(1, ratio):
                block = jnp.where((which + shift) % ratio == k, halves[shift][:, span], block)
            parts.append(block)
    image = dot(inverse_ref[...], jnp.concatenate(parts, axis=1), ((1,), (0,)))
    image_ref[...] = image
    left = stack_left(2.0 * image)
    right = stack_right(cols_ref[...])
    chunk = 256
    for start in range(0, begun_ref.shape[0], chunk):
        span = slice(start, start + chunk)
        further_ref[span, :] = begun_ref[span, :] - dot16(left[:, span], right, ((0,), (0,)))


def update_kernel(
    further_ref, image_ref, left_ref, coeffs_ref, coeffs_cols_ref, inverse_ref, *refs
):
    inners, (updated_ref, w_ref, buffer_ref, w_buffer_ref, sems) = refs[:-5], refs[-5:]
    inverse = inverse_ref[...]
    inner = tree_sum([part[...] for part in inners])
    right = dot(inverse, dot(inner, coeffs_cols_ref[...], ((1,), (0,))), ((1,), (0,)))
    right = stack_right(4.0 * right)
    count = sems.shape[0] - 1
    chunk = further_ref.shape[0] // count
    copies = []
    for i in range(count):
        span = slice(i * chunk, (i + 1) * chunk)
        buffer_ref[span, :] = further_ref[span, :] + dot16(left_ref[:, span], right, ((0,), (0,)))
        copies.append(
            pltpu.make_async_copy(buffer_ref.at[span, :], updated_ref.at[span, :], sems.at[i])
        )
        copies[-1].start()
    removed = dot(inverse, dot(inner, coeffs_ref[...], ((0,), (0,))), ((1,), (0,)))
    w_buffer_ref[...] = 2.0 * (image_ref[...] - removed)
    copies.append(pltpu.make_async_copy(w_buffer_ref, w_ref, sems.at[count]))
    copies[-1].start()
    for copy in copies:
        copy.wait()


def shape(*dims, dtype=jnp.float32):
    return jax.ShapeDtypeStruct(dims, dtype)


def call(kernel, outs, args, in_specs=None, out_specs=None, scratch=(), flops=0):
    return pl.pallas_call(
        kernel,
        out_shape=outs,
        in_specs=in_specs or [VMEM] * len(args),
        out_specs=out_specs or ((VMEM,) * len(outs) if isinstance(outs, tuple) else VMEM),
        scratch_shapes=scratch,
        compiler_params=PARAMS,
        cost_estimate=pl.CostEstimate(flops=flops, bytes_accessed=1 << 18, transcendentals=0),
    )(*args)


def local(matrix, panel):
    n_row, n_col = lax.axis_size("row"), lax.axis_size("col")
    ratio = n_col // n_row
    rows, width = panel.shape
    cols = matrix.shape[1]
    which = (lax.axis_index("col") // n_row).astype(jnp.int32).reshape(1)
    chunks = 8

    *mines, panel_t, terms, gram, kept = call(
        functools.partial(panel_kernel, ratio),
        (
            *[shape(width, cols)] * ratio,
            shape(width, rows),
            shape(3 * width, rows, dtype=jnp.bfloat16),
            shape(STRIP, cols),
            shape(rows, cols),
        ),
        (
            which,
            pltpu.with_memory_space_constraint(panel.T, pltpu.HBM),
            pltpu.with_memory_space_constraint(matrix, pltpu.HBM),
        ),
        in_specs=[SMEM, HBM, HBM],
        scratch=[pltpu.SemaphoreType.DMA((2 * chunks,))],
        flops=1 << 28,
    )
    message = call(
        product_kernel, shape(width + STRIP, cols), (terms, kept, gram), flops=1 << 30
    )
    step = 1
    while 2 * step < n_row:
        message = message + partner(message, "row", step)
        step *= 2
    last = partner(message, "row", step)
    product_cols, gram = call(
        finish_kernel, (shape(width, cols), shape(width, width)), (last, message), flops=1 << 24
    )
    halves = [transpose_grid(product_cols, shift) for shift in reversed(range(ratio))]
    inverse = call(factor_kernel, shape(width, width), (gram,), flops=1 << 30)
    begun, basis, left, coeffs = call(
        basis_kernel,
        (
            shape(rows, cols),
            shape(width, rows),
            shape(3 * width, rows, dtype=jnp.bfloat16),
            shape(width, rows),
        ),
        (kept, panel_t, product_cols, inverse),
        flops=1 << 30,
    )
    held, received, takes = spread_rows(mines[0], begun)
    halves, begun = lax.optimization_barrier((halves, begun))
    inner = call(inner_kernel, shape(width, width), (*halves, *mines[::-1]), flops=1 << 24)
    received, _ = lax.optimization_barrier((received, inner))
    basis_cols, coeffs_cols = call(
        columns_kernel,
        (shape(width, cols), shape(width, cols)),
        (inverse, received, held, takes),
        in_specs=[VMEM] * 3 + [SMEM],
        flops=1 << 24,
    )
    further, image = call(
        functools.partial(image_kernel, ratio),
        (shape(rows, cols), shape(width, rows)),
        (which, begun, basis_cols, inverse, *halves),
        in_specs=[SMEM] + [VMEM] * (3 + ratio),
        flops=1 << 30,
    )
    inners = group_parts(inner, "row", 1, n_row)[::-1]
    updated, w_rows = call(
        update_kernel,
        (shape(rows, cols), shape(width, rows)),
        (further, image, left, coeffs, coeffs_cols, inverse, *inners),
        out_specs=(HBM, HBM),
        scratch=[
            pltpu.VMEM((rows, cols), jnp.float32),
            pltpu.VMEM((width, rows), jnp.float32),
            pltpu.SemaphoreType.DMA((chunks + 1,)),
        ],
        flops=1 << 30,
    )
    return (updated, w_rows.T, basis.T)


def solution(mesh):
    return jax.shard_map(
        local,
        mesh=mesh,
        in_specs=(P("row", "col"), P("row", None)),
        out_specs=(P("row", "col"), P("row", None), P("row", None)),
        check_vma=False,
    )
```

```python
import functools

import jax
import jax.numpy as jnp
from jax import lax
from jax.experimental import pallas as pl
from jax.experimental.pallas import tpu as pltpu
from jax.sharding import PartitionSpec as P

HIGH = lax.Precision.HIGHEST
VMEM = pl.BlockSpec(memory_space=pltpu.VMEM)
SMEM = pl.BlockSpec(memory_space=pltpu.SMEM)
HBM = pl.BlockSpec(memory_space=pltpu.HBM)
PARAMS = pltpu.CompilerParams(vmem_limit_bytes=40 * 1024 * 1024)
STRIP = 8


def dot(left, right, contract, precision=HIGH):
    return lax.dot_general(
        left, right, (contract, ((), ())), precision=precision, preferred_element_type=jnp.float32
    )


def dot16(left, right, contract):
    return dot(left, right, contract, lax.Precision.DEFAULT)


def split(value, parts):
    terms = []
    for _ in range(parts):
        terms.append(value.astype(jnp.bfloat16))
        value = value - terms[-1].astype(jnp.float32)
    return terms


def partner(value, axis, step):
    size = lax.axis_size(axis)
    return lax.ppermute(value, axis, [(i, i ^ step) for i in range(size)])


def tree_sum(parts):
    while len(parts) > 1:
        parts = [parts[i] + parts[i + 1] for i in range(0, len(parts), 2)]
    return parts[0]


def group_parts(value, axis, low, high):
    parts = [value]
    while low < high:
        value = tree_sum(parts)
        radix = min(4, high // low)
        parts = [value] + [partner(value, axis, i * low) for i in range(1, radix)]
        low *= radix
    return parts


def spread_rows(value, after):
    n_row, n_col = lax.axis_size("row"), lax.axis_size("col")
    apart = lax.axis_index("row") ^ (lax.axis_index("col") % n_row)
    bits = [1] + [1 << i for i in reversed(range(1, n_row.bit_length() - 1))]
    reached = [0]
    for bit in bits:
        pairs = []
        for c in range(n_col):
            for offset in reached:
                source = (c % n_row) ^ offset
                pairs.append((source * n_col + c, (source ^ bit) * n_col + c))
        reached += [offset ^ bit for offset in reached]
        received = lax.ppermute(value, ("row", "col"), pairs)
        takes = apart & bit != 0
        if bit == bits[-1]:
            return value, received, takes.astype(jnp.int32).reshape(1)
        received, _ = lax.optimization_barrier((received, after))
        value = jnp.where(takes, received, value)


def transpose_grid(value, shift):
    n_row, n_col = lax.axis_size("row"), lax.axis_size("col")
    ratio = n_col // n_row
    pairs = []
    for r in range(n_row):
        for k in range(ratio):
            for q in range(n_row):
                column = (k + shift) % ratio * n_row + r
                row = q if shift % 2 else q ^ (n_row // 2)
                pairs.append((row * n_col + column, r * n_col + k * n_row + q))
    return lax.ppermute(value, ("row", "col"), pairs)


def copy_rows(source, target, sems, first, pieces):
    size = source.shape[0] // pieces
    copies = []
    for piece in range(pieces):
        span = slice(piece * size, (piece + 1) * size)
        copies.append(
            pltpu.make_async_copy(source.at[span, :], target.at[span, :], sems.at[first + piece])
        )
        copies[-1].start()
    return copies


def panel_kernel(ratio, which_ref, panel_ref, matrix_ref, *refs):
    mine_refs, (held_ref, terms_ref, gram_ref, kept_ref, sems) = refs[:ratio], refs[ratio:]
    width = panel_ref.shape[0]
    pieces = sems.shape[0] // 2
    panel_copies = copy_rows(panel_ref, held_ref, sems, 0, pieces)
    matrix_copies = copy_rows(matrix_ref, kept_ref, sems, pieces, pieces)
    for copy in panel_copies:
        copy.wait()
    which = which_ref[0]
    for j in range(mine_refs[0].shape[1] // width):
        start = j * ratio * width
        blocks = [held_ref[:, start + k * width : start + (k + 1) * width] for k in range(ratio)]
        for shift, mine_ref in enumerate(mine_refs):
            block = blocks[shift]
            for k in range(1, ratio):
                block = jnp.where(which == k, blocks[(k + shift) % ratio], block)
            mine_ref[:, j * width : (j + 1) * width] = block
    panel = held_ref[...]
    terms_ref[...] = jnp.concatenate(split(panel, 3), axis=0)
    to_strip(dot(panel, panel, ((1,), (1,))), gram_ref)
    for copy in matrix_copies:
        copy.wait()


def product_kernel(terms_ref, matrix_ref, gram_ref, out_ref):
    width = out_ref.shape[0] - STRIP
    rows = matrix_ref.shape[0]
    chunk = 256
    total = jnp.zeros((width, matrix_ref.shape[1]), jnp.float32)
    for start in range(0, rows, chunk):
        span = slice(start, start + chunk)
        parts = split(matrix_ref[span, :], 3)
        for i, part in enumerate(parts):
            count = 3 - i
            out = dot16(terms_ref[: count * width, span], part, ((1,), (0,)))
            for t in range(count):
                total = total + out[t * width : (t + 1) * width, :]
    out_ref[:width, :] = total
    out_ref[width:, :] = gram_ref[...]


def to_strip(value, strip_ref):
    width = value.shape[0]
    for i in range(width // STRIP):
        strip_ref[:, i * width : (i + 1) * width] = value[i * STRIP : (i + 1) * STRIP, :]


def from_strip(strip, width):
    return jnp.concatenate(
        [strip[:, i * width : (i + 1) * width] for i in range(width // STRIP)], axis=0
    )


def finish_kernel(other_ref, mine_ref, product_ref, gram_ref):
    width = product_ref.shape[0]
    product_ref[...] = mine_ref[:width, :] + other_ref[:width, :]
    gram_ref[...] = from_strip(mine_ref[width:, :] + other_ref[width:, :], width)


def factor_kernel(gram_ref, inverse_ref):
    size = inverse_ref.shape[0]
    batch = 4
    row = lax.broadcasted_iota(jnp.int32, (size, 2 * size), 0)
    lane = lax.broadcasted_iota(jnp.int32, (size, 2 * size), 1)
    eye = jnp.where(row == lane, 1.0, 0.0).astype(jnp.float32)
    table = jnp.concatenate([eye[:, :size], gram_ref[...]], axis=1)
    for first in range(0, size, batch):
        base = first // 8 * 8
        height = size - base
        low = table[base:, :]
        low_row = row[base:, :]
        cols = [
            jnp.broadcast_to(low[:, size + first + t : size + first + t + 1], (height, 2 * size))
            for t in range(batch)
        ]
        rows = [low[first - base + t : first - base + t + 1, :] for t in range(batch)]
        for t in range(batch):
            at = first - base + t
            scale = 1.0 / cols[t][at : at + 1, :]
            factor = jnp.where(low_row > first + t, cols[t] * scale, 0.0)
            for s in range(t + 1, batch):
                cols[s] = cols[s] - factor * cols[s][at : at + 1, :]
                rows[s] = rows[s] - factor[first - base + s : first - base + s + 1, :] * rows[t]
            low = low - factor * rows[t]
        table = low if base == 0 else jnp.concatenate([table[:base, :], low], axis=0)
    diagonal = jnp.sum(jnp.where(lane == row + size, table, 0.0), axis=1, keepdims=True)
    inverse_ref[...] = (table / jnp.sqrt(diagonal))[:, :size]


def stack_left(value):
    high, low = split(value, 2)
    return jnp.concatenate([high, low, high], axis=0)


def stack_right(value):
    high, low = split(value, 2)
    return jnp.concatenate([high, high, low], axis=0)


def basis_kernel(
    matrix_ref, panel_ref, product_cols_ref, inverse_ref,
    begun_ref, basis_ref, left_ref, coeffs_ref, ready_ref,
):
    inverse = inverse_ref[...]
    basis = dot(inverse, panel_ref[...], ((1,), (0,)))
    image_cols = dot(inverse, product_cols_ref[...], ((1,), (0,)))
    basis_ref[...] = basis
    coeffs_ref[...] = dot(inverse, basis, ((0,), (0,)))
    left = stack_left(basis)
    left_ref[...] = left
    right = stack_right(2.0 * image_cols)
    chunk = 256
    for start in range(0, matrix_ref.shape[0], chunk):
        span = slice(start, start + chunk)
        begun_ref[span, :] = matrix_ref[span, :] - dot16(left[:, span], right, ((0,), (0,)))
    ready_ref[...] = basis[: ready_ref.shape[0], : ready_ref.shape[1]]


def columns_kernel(inverse_ref, received_ref, held_ref, takes_ref, cols_ref, coeffs_cols_ref):
    inverse = inverse_ref[...]
    panel_cols = jnp.where(takes_ref[0] != 0, received_ref[...], held_ref[...])
    cols = dot(inverse, panel_cols, ((1,), (0,)))
    cols_ref[...] = cols
    coeffs_cols_ref[...] = dot(inverse, cols, ((0,), (0,)))


def inner_kernel(*refs):
    count = len(refs) // 2
    inner_ref = refs[-1]
    inner_ref[...] = sum(
        dot(refs[count + i][...], refs[i][...], ((1,), (1,))) for i in range(count)
    )


def image_kernel(ratio, which_ref, begun_ref, cols_ref, inverse_ref, *refs):
    halves, (further_ref, image_ref) = refs[:ratio][::-1], refs[ratio:]
    width = inverse_ref.shape[0]
    which = which_ref[0]
    parts = []
    for j in range(halves[0].shape[1] // width):
        span = slice(j * width, (j + 1) * width)
        for k in range(ratio):
            block = halves[0][:, span]
            for shift in range(1, ratio):
                block = jnp.where((which + shift) % ratio == k, halves[shift][:, span], block)
            parts.append(block)
    image = dot(inverse_ref[...], jnp.concatenate(parts, axis=1), ((1,), (0,)))
    image_ref[...] = image
    left = stack_left(2.0 * image)
    right = stack_right(cols_ref[...])
    chunk = 256
    for start in range(0, begun_ref.shape[0], chunk):
        span = slice(start, start + chunk)
        further_ref[span, :] = begun_ref[span, :] - dot16(left[:, span], right, ((0,), (0,)))


def update_kernel(
    further_ref, image_ref, left_ref, coeffs_ref, coeffs_cols_ref, inverse_ref, *refs
):
    inners, (updated_ref, w_ref, buffer_ref, w_buffer_ref, sems) = refs[:-5], refs[-5:]
    inverse = inverse_ref[...]
    inner = tree_sum([part[...] for part in inners])
    right = dot(inverse, dot(inner, coeffs_cols_ref[...], ((1,), (0,))), ((1,), (0,)))
    right = stack_right(4.0 * right)
    count = sems.shape[0] - 1
    chunk = further_ref.shape[0] // count
    copies = []
    for i in range(count):
        span = slice(i * chunk, (i + 1) * chunk)
        buffer_ref[span, :] = further_ref[span, :] + dot16(left_ref[:, span], right, ((0,), (0,)))
        copies.append(
            pltpu.make_async_copy(buffer_ref.at[span, :], updated_ref.at[span, :], sems.at[i])
        )
        copies[-1].start()
    removed = dot(inverse, dot(inner, coeffs_ref[...], ((0,), (0,))), ((1,), (0,)))
    w_buffer_ref[...] = 2.0 * (image_ref[...] - removed)
    copies.append(pltpu.make_async_copy(w_buffer_ref, w_ref, sems.at[count]))
    copies[-1].start()
    for copy in copies:
        copy.wait()


def shape(*dims, dtype=jnp.float32):
    return jax.ShapeDtypeStruct(dims, dtype)


def call(kernel, outs, args, in_specs=None, out_specs=None, scratch=(), flops=0):
    return pl.pallas_call(
        kernel,
        out_shape=outs,
        in_specs=in_specs or [VMEM] * len(args),
        out_specs=out_specs or ((VMEM,) * len(outs) if isinstance(outs, tuple) else VMEM),
        scratch_shapes=scratch,
        compiler_params=PARAMS,
        cost_estimate=pl.CostEstimate(flops=flops, bytes_accessed=1 << 18, transcendentals=0),
    )(*args)


def local(matrix, panel):
    n_row, n_col = lax.axis_size("row"), lax.axis_size("col")
    ratio = n_col // n_row
    rows, width = panel.shape
    cols = matrix.shape[1]
    which = (lax.axis_index("col") // n_row).astype(jnp.int32).reshape(1)
    chunks = 8

    *mines, panel_t, terms, gram, kept = call(
        functools.partial(panel_kernel, ratio),
        (
            *[shape(width, cols)] * ratio,
            shape(width, rows),
            shape(3 * width, rows, dtype=jnp.bfloat16),
            shape(STRIP, cols),
            shape(rows, cols),
        ),
        (
            which,
            pltpu.with_memory_space_constraint(panel.T, pltpu.HBM),
            pltpu.with_memory_space_constraint(matrix, pltpu.HBM),
        ),
        in_specs=[SMEM, HBM, HBM],
        scratch=[pltpu.SemaphoreType.DMA((2 * chunks,))],
        flops=1 << 28,
    )
    message = call(
        product_kernel, shape(width + STRIP, cols), (terms, kept, gram), flops=1 << 30
    )
    step = 1
    while 2 * step < n_row:
        message = message + partner(message, "row", step)
        step *= 2
    last = partner(message, "row", step)
    product_cols, gram = call(
        finish_kernel, (shape(width, cols), shape(width, width)), (last, message), flops=1 << 24
    )
    halves = [transpose_grid(product_cols, shift) for shift in reversed(range(ratio))]
    inverse = call(factor_kernel, shape(width, width), (gram,), flops=1 << 30)
    begun, basis, left, coeffs, ready = call(
        basis_kernel,
        (
            shape(rows, cols),
            shape(width, rows),
            shape(3 * width, rows, dtype=jnp.bfloat16),
            shape(width, rows),
            shape(8, 128),
        ),
        (kept, panel_t, product_cols, inverse),
        flops=1 << 30,
    )
    held, received, takes = spread_rows(mines[0], ready)
    halves, begun = lax.optimization_barrier((halves, begun))
    inner = call(inner_kernel, shape(width, width), (*halves, *mines[::-1]), flops=1 << 24)
    received, _ = lax.optimization_barrier((received, inner))
    basis_cols, coeffs_cols = call(
        columns_kernel,
        (shape(width, cols), shape(width, cols)),
        (inverse, received, held, takes),
        in_specs=[VMEM] * 3 + [SMEM],
        flops=1 << 24,
    )
    further, image = call(
        functools.partial(image_kernel, ratio),
        (shape(rows, cols), shape(width, rows)),
        (which, begun, basis_cols, inverse, *halves),
        in_specs=[SMEM] + [VMEM] * (3 + ratio),
        flops=1 << 30,
    )
    inners = group_parts(inner, "row", 1, n_row)[::-1]
    updated, w_rows = call(
        update_kernel,
        (shape(rows, cols), shape(width, rows)),
        (further, image, left, coeffs, coeffs_cols, inverse, *inners),
        out_specs=(HBM, HBM),
        scratch=[
            pltpu.VMEM((rows, cols), jnp.float32),
            pltpu.VMEM((width, rows), jnp.float32),
            pltpu.SemaphoreType.DMA((chunks + 1,)),
        ],
        flops=1 << 30,
    )
    return (updated, w_rows.T, basis.T)


def solution(mesh):
    return jax.shard_map(
        local,
        mesh=mesh,
        in_specs=(P("row", "col"), P("row", None)),
        out_specs=(P("row", "col"), P("row", None), P("row", None)),
        check_vma=False,
    )
```

```python
import functools

import jax
import jax.numpy as jnp
from jax import lax
from jax.experimental import pallas as pl
from jax.experimental.pallas import tpu as pltpu
from jax.sharding import PartitionSpec as P

HIGH = lax.Precision.HIGHEST
VMEM = pl.BlockSpec(memory_space=pltpu.VMEM)
SMEM = pl.BlockSpec(memory_space=pltpu.SMEM)
HBM = pl.BlockSpec(memory_space=pltpu.HBM)
PARAMS = pltpu.CompilerParams(vmem_limit_bytes=40 * 1024 * 1024)
STRIP = 8


def dot(left, right, contract, precision=HIGH):
    return lax.dot_general(
        left, right, (contract, ((), ())), precision=precision, preferred_element_type=jnp.float32
    )


def dot16(left, right, contract):
    return dot(left, right, contract, lax.Precision.DEFAULT)


def split(value, parts):
    terms = []
    for _ in range(parts):
        terms.append(value.astype(jnp.bfloat16))
        value = value - terms[-1].astype(jnp.float32)
    return terms


def partner(value, axis, step):
    size = lax.axis_size(axis)
    return lax.ppermute(value, axis, [(i, i ^ step) for i in range(size)])


def tree_sum(parts):
    while len(parts) > 1:
        parts = [parts[i] + parts[i + 1] for i in range(0, len(parts), 2)]
    return parts[0]


def group_parts(value, axis, low, high):
    parts = [value]
    while low < high:
        value = tree_sum(parts)
        radix = min(4, high // low)
        parts = [value] + [partner(value, axis, i * low) for i in range(1, radix)]
        low *= radix
    return parts


def spread_rows(value, after):
    n_row, n_col = lax.axis_size("row"), lax.axis_size("col")
    apart = lax.axis_index("row") ^ (lax.axis_index("col") % n_row)
    bits = [1] + [1 << i for i in reversed(range(1, n_row.bit_length() - 1))]
    reached = [0]
    for bit in bits:
        pairs = []
        for c in range(n_col):
            for offset in reached:
                source = (c % n_row) ^ offset
                pairs.append((source * n_col + c, (source ^ bit) * n_col + c))
        reached += [offset ^ bit for offset in reached]
        received = lax.ppermute(value, ("row", "col"), pairs)
        takes = apart & bit != 0
        if bit == bits[-1]:
            return value, received, takes.astype(jnp.int32).reshape(1)
        received, _ = lax.optimization_barrier((received, after))
        value = jnp.where(takes, received, value)


def transpose_grid(value, shift):
    n_row, n_col = lax.axis_size("row"), lax.axis_size("col")
    ratio = n_col // n_row
    pairs = []
    for r in range(n_row):
        for k in range(ratio):
            for q in range(n_row):
                column = (k + shift) % ratio * n_row + r
                row = q if shift % 2 else q ^ (n_row // 2)
                pairs.append((row * n_col + column, r * n_col + k * n_row + q))
    return lax.ppermute(value, ("row", "col"), pairs)


def copy_rows(source, target, sems, first, pieces):
    size = source.shape[0] // pieces
    copies = []
    for piece in range(pieces):
        span = slice(piece * size, (piece + 1) * size)
        copies.append(
            pltpu.make_async_copy(source.at[span, :], target.at[span, :], sems.at[first + piece])
        )
        copies[-1].start()
    return copies


def panel_kernel(ratio, which_ref, panel_ref, matrix_ref, *refs):
    mine_refs, (held_ref, terms_ref, gram_ref, kept_ref, sems) = refs[:ratio], refs[ratio:]
    width = panel_ref.shape[0]
    pieces = sems.shape[0] // 2
    panel_copies = copy_rows(panel_ref, held_ref, sems, 0, pieces)
    matrix_copies = copy_rows(matrix_ref, kept_ref, sems, pieces, pieces)
    for copy in panel_copies:
        copy.wait()
    which = which_ref[0]
    for j in range(mine_refs[0].shape[1] // width):
        start = j * ratio * width
        blocks = [held_ref[:, start + k * width : start + (k + 1) * width] for k in range(ratio)]
        for shift, mine_ref in enumerate(mine_refs):
            block = blocks[shift]
            for k in range(1, ratio):
                block = jnp.where(which == k, blocks[(k + shift) % ratio], block)
            mine_ref[:, j * width : (j + 1) * width] = block
    panel = held_ref[...]
    terms_ref[...] = jnp.concatenate(split(panel, 3), axis=0)
    to_strip(dot(panel, panel, ((1,), (1,))), gram_ref)
    for copy in matrix_copies:
        copy.wait()


def product_kernel(terms_ref, matrix_ref, gram_ref, out_ref):
    width = out_ref.shape[0] - STRIP
    rows = matrix_ref.shape[0]
    chunk = 256
    total = jnp.zeros((width, matrix_ref.shape[1]), jnp.float32)
    for start in range(0, rows, chunk):
        span = slice(start, start + chunk)
        parts = split(matrix_ref[span, :], 3)
        for i, part in enumerate(parts):
            count = 3 - i
            out = dot16(terms_ref[: count * width, span], part, ((1,), (0,)))
            for t in range(count):
                total = total + out[t * width : (t + 1) * width, :]
    out_ref[:width, :] = total
    out_ref[width:, :] = gram_ref[...]


def to_strip(value, strip_ref):
    width = value.shape[0]
    for i in range(width // STRIP):
        strip_ref[:, i * width : (i + 1) * width] = value[i * STRIP : (i + 1) * STRIP, :]


def from_strip(strip, width):
    return jnp.concatenate(
        [strip[:, i * width : (i + 1) * width] for i in range(width // STRIP)], axis=0
    )


def finish_kernel(other_ref, mine_ref, product_ref, gram_ref):
    width = product_ref.shape[0]
    product_ref[...] = mine_ref[:width, :] + other_ref[:width, :]
    gram_ref[...] = from_strip(mine_ref[width:, :] + other_ref[width:, :], width)


def factor_kernel(gram_ref, inverse_ref):
    size = inverse_ref.shape[0]
    batch = 4
    row = lax.broadcasted_iota(jnp.int32, (size, 2 * size), 0)
    lane = lax.broadcasted_iota(jnp.int32, (size, 2 * size), 1)
    eye = jnp.where(row == lane, 1.0, 0.0).astype(jnp.float32)
    table = jnp.concatenate([eye[:, :size], gram_ref[...]], axis=1)
    for first in range(0, size, batch):
        base = first // 8 * 8
        height = size - base
        low = table[base:, :]
        low_row = row[base:, :]
        cols = [
            jnp.broadcast_to(low[:, size + first + t : size + first + t + 1], (height, 2 * size))
            for t in range(batch)
        ]
        rows = [low[first - base + t : first - base + t + 1, :] for t in range(batch)]
        for t in range(batch):
            at = first - base + t
            scale = 1.0 / cols[t][at : at + 1, :]
            factor = jnp.where(low_row > first + t, cols[t] * scale, 0.0)
            for s in range(t + 1, batch):
                cols[s] = cols[s] - factor * cols[s][at : at + 1, :]
                rows[s] = rows[s] - factor[first - base + s : first - base + s + 1, :] * rows[t]
            low = low - factor * rows[t]
        table = low if base == 0 else jnp.concatenate([table[:base, :], low], axis=0)
    diagonal = jnp.sum(jnp.where(lane == row + size, table, 0.0), axis=1, keepdims=True)
    inverse_ref[...] = (table / jnp.sqrt(diagonal))[:, :size]


def stack_left(value):
    high, low = split(value, 2)
    return jnp.concatenate([high, low, high], axis=0)


def stack_right(value):
    high, low = split(value, 2)
    return jnp.concatenate([high, high, low], axis=0)


def basis_kernel(
    matrix_ref, panel_ref, product_cols_ref, inverse_ref,
    begun_ref, basis_ref, left_ref, coeffs_ref,
):
    inverse = inverse_ref[...]
    basis = dot(inverse, panel_ref[...], ((1,), (0,)))
    image_cols = dot(inverse, product_cols_ref[...], ((1,), (0,)))
    basis_ref[...] = basis
    coeffs_ref[...] = dot(inverse, basis, ((0,), (0,)))
    left = stack_left(basis)
    left_ref[...] = left
    right = stack_right(2.0 * image_cols)
    chunk = 256
    for start in range(0, matrix_ref.shape[0], chunk):
        span = slice(start, start + chunk)
        begun_ref[span, :] = matrix_ref[span, :] - dot16(left[:, span], right, ((0,), (0,)))


def columns_kernel(inverse_ref, received_ref, held_ref, takes_ref, cols_ref, coeffs_cols_ref):
    inverse = inverse_ref[...]
    panel_cols = jnp.where(takes_ref[0] != 0, received_ref[...], held_ref[...])
    cols = dot(inverse, panel_cols, ((1,), (0,)))
    cols_ref[...] = cols
    coeffs_cols_ref[...] = dot(inverse, cols, ((0,), (0,)))


def inner_kernel(*refs):
    count = len(refs) // 2
    inner_ref = refs[-1]
    inner_ref[...] = sum(
        dot(refs[count + i][...], refs[i][...], ((1,), (1,))) for i in range(count)
    )


def image_kernel(ratio, which_ref, begun_ref, cols_ref, inverse_ref, *refs):
    halves, (further_ref, image_ref) = refs[:ratio][::-1], refs[ratio:]
    width = inverse_ref.shape[0]
    which = which_ref[0]
    parts = []
    for j in range(halves[0].shape[1] // width):
        span = slice(j * width, (j + 1) * width)
        for k in range(ratio):
            block = halves[0][:, span]
            for shift in range(1, ratio):
                block = jnp.where((which + shift) % ratio == k, halves[shift][:, span], block)
            parts.append(block)
    image = dot(inverse_ref[...], jnp.concatenate(parts, axis=1), ((1,), (0,)))
    image_ref[...] = image
    left = stack_left(2.0 * image)
    right = stack_right(cols_ref[...])
    chunk = 256
    for start in range(0, begun_ref.shape[0], chunk):
        span = slice(start, start + chunk)
        further_ref[span, :] = begun_ref[span, :] - dot16(left[:, span], right, ((0,), (0,)))


def update_kernel(
    further_ref, image_ref, left_ref, coeffs_ref, coeffs_cols_ref, inverse_ref, *refs
):
    inners, (updated_ref, w_ref, buffer_ref, w_buffer_ref, sems) = refs[:-5], refs[-5:]
    inverse = inverse_ref[...]
    inner = tree_sum([part[...] for part in inners])
    right = dot(inverse, dot(inner, coeffs_cols_ref[...], ((1,), (0,))), ((1,), (0,)))
    right = stack_right(4.0 * right)
    count = sems.shape[0] - 1
    chunk = further_ref.shape[0] // count
    copies = []
    for i in range(count):
        span = slice(i * chunk, (i + 1) * chunk)
        buffer_ref[span, :] = further_ref[span, :] + dot16(left_ref[:, span], right, ((0,), (0,)))
        copies.append(
            pltpu.make_async_copy(buffer_ref.at[span, :], updated_ref.at[span, :], sems.at[i])
        )
        copies[-1].start()
    removed = dot(inverse, dot(inner, coeffs_ref[...], ((0,), (0,))), ((1,), (0,)))
    w_buffer_ref[...] = 2.0 * (image_ref[...] - removed)
    copies.append(pltpu.make_async_copy(w_buffer_ref, w_ref, sems.at[count]))
    copies[-1].start()
    for copy in copies:
        copy.wait()


def shape(*dims, dtype=jnp.float32):
    return jax.ShapeDtypeStruct(dims, dtype)


def call(kernel, outs, args, in_specs=None, out_specs=None, scratch=(), flops=0):
    return pl.pallas_call(
        kernel,
        out_shape=outs,
        in_specs=in_specs or [VMEM] * len(args),
        out_specs=out_specs or ((VMEM,) * len(outs) if isinstance(outs, tuple) else VMEM),
        scratch_shapes=scratch,
        compiler_params=PARAMS,
        cost_estimate=pl.CostEstimate(flops=flops, bytes_accessed=1 << 18, transcendentals=0),
    )(*args)


def local(matrix, panel):
    n_row, n_col = lax.axis_size("row"), lax.axis_size("col")
    ratio = n_col // n_row
    rows, width = panel.shape
    cols = matrix.shape[1]
    which = (lax.axis_index("col") // n_row).astype(jnp.int32).reshape(1)
    chunks = 8

    *mines, panel_t, terms, gram, kept = call(
        functools.partial(panel_kernel, ratio),
        (
            *[shape(width, cols)] * ratio,
            shape(width, rows),
            shape(3 * width, rows, dtype=jnp.bfloat16),
            shape(STRIP, cols),
            shape(rows, cols),
        ),
        (
            which,
            pltpu.with_memory_space_constraint(panel.T, pltpu.HBM),
            pltpu.with_memory_space_constraint(matrix, pltpu.HBM),
        ),
        in_specs=[SMEM, HBM, HBM],
        scratch=[pltpu.SemaphoreType.DMA((2 * chunks,))],
        flops=1 << 28,
    )
    message = call(
        product_kernel, shape(width + STRIP, cols), (terms, kept, gram), flops=1 << 30
    )
    step = 1
    while 2 * step < n_row:
        message = message + partner(message, "row", step)
        step *= 2
    last = partner(message, "row", step)
    product_cols, gram = call(
        finish_kernel, (shape(width, cols), shape(width, width)), (last, message), flops=1 << 24
    )
    halves = [transpose_grid(product_cols, shift) for shift in reversed(range(ratio))]
    inverse = call(factor_kernel, shape(width, width), (gram,), flops=1 << 30)
    held, received, takes = spread_rows(mines[0], inverse)
    begun, basis, left, coeffs = call(
        basis_kernel,
        (
            shape(rows, cols),
            shape(width, rows),
            shape(3 * width, rows, dtype=jnp.bfloat16),
            shape(width, rows),
        ),
        (kept, panel_t, product_cols, inverse),
        flops=1 << 30,
    )
    halves, begun = lax.optimization_barrier((halves, begun))
    inner = call(inner_kernel, shape(width, width), (*halves, *mines[::-1]), flops=1 << 24)
    received, _ = lax.optimization_barrier((received, inner))
    basis_cols, coeffs_cols = call(
        columns_kernel,
        (shape(width, cols), shape(width, cols)),
        (inverse, received, held, takes),
        in_specs=[VMEM] * 3 + [SMEM],
        flops=1 << 24,
    )
    further, image = call(
        functools.partial(image_kernel, ratio),
        (shape(rows, cols), shape(width, rows)),
        (which, begun, basis_cols, inverse, *halves),
        in_specs=[SMEM] + [VMEM] * (3 + ratio),
        flops=1 << 30,
    )
    inners = group_parts(inner, "row", 1, n_row)[::-1]
    updated, w_rows = call(
        update_kernel,
        (shape(rows, cols), shape(width, rows)),
        (further, image, left, coeffs, coeffs_cols, inverse, *inners),
        out_specs=(HBM, HBM),
        scratch=[
            pltpu.VMEM((rows, cols), jnp.float32),
            pltpu.VMEM((width, rows), jnp.float32),
            pltpu.SemaphoreType.DMA((chunks + 1,)),
        ],
        flops=1 << 30,
    )
    return (updated, w_rows.T, basis.T)


def solution(mesh):
    return jax.shard_map(
        local,
        mesh=mesh,
        in_specs=(P("row", "col"), P("row", None)),
        out_specs=(P("row", "col"), P("row", None), P("row", None)),
        check_vma=False,
    )
```

```python
import functools

import jax
import jax.numpy as jnp
from jax import lax
from jax.experimental import pallas as pl
from jax.experimental.pallas import tpu as pltpu
from jax.sharding import PartitionSpec as P

HIGH = lax.Precision.HIGHEST
VMEM = pl.BlockSpec(memory_space=pltpu.VMEM)
SMEM = pl.BlockSpec(memory_space=pltpu.SMEM)
HBM = pl.BlockSpec(memory_space=pltpu.HBM)
PARAMS = pltpu.CompilerParams(vmem_limit_bytes=40 * 1024 * 1024)
STRIP = 8


def dot(left, right, contract, precision=HIGH):
    return lax.dot_general(
        left, right, (contract, ((), ())), precision=precision, preferred_element_type=jnp.float32
    )


def dot16(left, right, contract):
    return dot(left, right, contract, lax.Precision.DEFAULT)


def split(value, parts):
    terms = []
    for _ in range(parts):
        terms.append(value.astype(jnp.bfloat16))
        value = value - terms[-1].astype(jnp.float32)
    return terms


def partner(value, axis, step):
    size = lax.axis_size(axis)
    return lax.ppermute(value, axis, [(i, i ^ step) for i in range(size)])


def tree_sum(parts):
    while len(parts) > 1:
        parts = [parts[i] + parts[i + 1] for i in range(0, len(parts), 2)]
    return parts[0]


def group_parts(value, axis, low, high):
    parts = [value]
    while low < high:
        value = tree_sum(parts)
        radix = min(4, high // low)
        parts = [value] + [partner(value, axis, i * low) for i in range(1, radix)]
        low *= radix
    return parts


def spread_rows(value, after):
    n_row, n_col = lax.axis_size("row"), lax.axis_size("col")
    apart = lax.axis_index("row") ^ (lax.axis_index("col") % n_row)
    bits = [1] + [1 << i for i in reversed(range(1, n_row.bit_length() - 1))]
    reached = [0]
    for bit in bits:
        pairs = []
        for c in range(n_col):
            for offset in reached:
                source = (c % n_row) ^ offset
                pairs.append((source * n_col + c, (source ^ bit) * n_col + c))
        reached += [offset ^ bit for offset in reached]
        received = lax.ppermute(value, ("row", "col"), pairs)
        takes = apart & bit != 0
        if bit == bits[-1]:
            return value, received, takes.astype(jnp.int32).reshape(1)
        received, _ = lax.optimization_barrier((received, after))
        value = jnp.where(takes, received, value)


def transpose_grid(value, shift):
    n_row, n_col = lax.axis_size("row"), lax.axis_size("col")
    ratio = n_col // n_row
    pairs = []
    for r in range(n_row):
        for k in range(ratio):
            for q in range(n_row):
                column = (k + shift) % ratio * n_row + r
                row = q if shift % 2 else q ^ (n_row // 2)
                pairs.append((row * n_col + column, r * n_col + k * n_row + q))
    return lax.ppermute(value, ("row", "col"), pairs)


def copy_rows(source, target, sems, first, pieces):
    size = source.shape[0] // pieces
    copies = []
    for piece in range(pieces):
        span = slice(piece * size, (piece + 1) * size)
        copies.append(
            pltpu.make_async_copy(source.at[span, :], target.at[span, :], sems.at[first + piece])
        )
        copies[-1].start()
    return copies


def panel_kernel(ratio, which_ref, panel_ref, matrix_ref, *refs):
    mine_refs, (held_ref, terms_ref, gram_ref, kept_ref, sems) = refs[:ratio], refs[ratio:]
    width = panel_ref.shape[0]
    pieces = sems.shape[0] // 2
    panel_copies = copy_rows(panel_ref, held_ref, sems, 0, pieces)
    matrix_copies = copy_rows(matrix_ref, kept_ref, sems, pieces, pieces)
    for copy in panel_copies:
        copy.wait()
    which = which_ref[0]
    for j in range(mine_refs[0].shape[1] // width):
        start = j * ratio * width
        blocks = [held_ref[:, start + k * width : start + (k + 1) * width] for k in range(ratio)]
        for shift, mine_ref in enumerate(mine_refs):
            block = blocks[shift]
            for k in range(1, ratio):
                block = jnp.where(which == k, blocks[(k + shift) % ratio], block)
            mine_ref[:, j * width : (j + 1) * width] = block
    panel = held_ref[...]
    terms_ref[...] = jnp.concatenate(split(panel, 3), axis=0)
    to_strip(dot(panel, panel, ((1,), (1,))), gram_ref)
    for copy in matrix_copies:
        copy.wait()


def product_kernel(terms_ref, matrix_ref, gram_ref, out_ref):
    width = out_ref.shape[0] - STRIP
    rows = matrix_ref.shape[0]
    chunk = 256
    total = jnp.zeros((width, matrix_ref.shape[1]), jnp.float32)
    for start in range(0, rows, chunk):
        span = slice(start, start + chunk)
        parts = split(matrix_ref[span, :], 3)
        for i, part in enumerate(parts):
            count = 3 - i
            out = dot16(terms_ref[: count * width, span], part, ((1,), (0,)))
            for t in range(count):
                total = total + out[t * width : (t + 1) * width, :]
    out_ref[:width, :] = total
    out_ref[width:, :] = gram_ref[...]


def to_strip(value, strip_ref):
    width = value.shape[0]
    for i in range(width // STRIP):
        strip_ref[:, i * width : (i + 1) * width] = value[i * STRIP : (i + 1) * STRIP, :]


def from_strip(strip, width):
    return jnp.concatenate(
        [strip[:, i * width : (i + 1) * width] for i in range(width // STRIP)], axis=0
    )


def finish_kernel(other_ref, mine_ref, product_ref, gram_ref):
    width = product_ref.shape[0]
    product_ref[...] = mine_ref[:width, :] + other_ref[:width, :]
    gram_ref[...] = from_strip(mine_ref[width:, :] + other_ref[width:, :], width)


def factor_kernel(gram_ref, inverse_ref):
    size = inverse_ref.shape[0]
    batch = 4
    row = lax.broadcasted_iota(jnp.int32, (size, 2 * size), 0)
    lane = lax.broadcasted_iota(jnp.int32, (size, 2 * size), 1)
    eye = jnp.where(row == lane, 1.0, 0.0).astype(jnp.float32)
    table = jnp.concatenate([eye[:, :size], gram_ref[...]], axis=1)
    for first in range(0, size, batch):
        base = first // 8 * 8
        height = size - base
        low = table[base:, :]
        low_row = row[base:, :]
        cols = [
            jnp.broadcast_to(low[:, size + first + t : size + first + t + 1], (height, 2 * size))
            for t in range(batch)
        ]
        rows = [low[first - base + t : first - base + t + 1, :] for t in range(batch)]
        for t in range(batch):
            at = first - base + t
            scale = 1.0 / cols[t][at : at + 1, :]
            factor = jnp.where(low_row > first + t, cols[t] * scale, 0.0)
            for s in range(t + 1, batch):
                cols[s] = cols[s] - factor * cols[s][at : at + 1, :]
                rows[s] = rows[s] - factor[first - base + s : first - base + s + 1, :] * rows[t]
            low = low - factor * rows[t]
        table = low if base == 0 else jnp.concatenate([table[:base, :], low], axis=0)
    diagonal = jnp.sum(jnp.where(lane == row + size, table, 0.0), axis=1, keepdims=True)
    inverse_ref[...] = (table / jnp.sqrt(diagonal))[:, :size]


def stack_left(value):
    high, low = split(value, 2)
    return jnp.concatenate([high, low, high], axis=0)


def stack_right(value):
    high, low = split(value, 2)
    return jnp.concatenate([high, high, low], axis=0)


def basis_kernel(
    matrix_ref, panel_ref, product_cols_ref, inverse_ref, received_ref, held_ref, takes_ref,
    begun_ref, basis_ref, left_ref, coeffs_ref, cols_ref, coeffs_cols_ref,
):
    inverse = inverse_ref[...]
    basis = dot(inverse, panel_ref[...], ((1,), (0,)))
    image_cols = dot(inverse, product_cols_ref[...], ((1,), (0,)))
    basis_ref[...] = basis
    coeffs_ref[...] = dot(inverse, basis, ((0,), (0,)))
    panel_cols = jnp.where(takes_ref[0] != 0, received_ref[...], held_ref[...])
    cols = dot(inverse, panel_cols, ((1,), (0,)))
    cols_ref[...] = cols
    coeffs_cols_ref[...] = dot(inverse, cols, ((0,), (0,)))
    left = stack_left(basis)
    left_ref[...] = left
    right = stack_right(2.0 * image_cols)
    chunk = 256
    for start in range(0, matrix_ref.shape[0], chunk):
        span = slice(start, start + chunk)
        begun_ref[span, :] = matrix_ref[span, :] - dot16(left[:, span], right, ((0,), (0,)))


def inner_kernel(*refs):
    count = len(refs) // 2
    inner_ref = refs[-1]
    inner_ref[...] = sum(
        dot(refs[count + i][...], refs[i][...], ((1,), (1,))) for i in range(count)
    )


def image_kernel(ratio, which_ref, begun_ref, cols_ref, inverse_ref, *refs):
    halves, (further_ref, image_ref) = refs[:ratio][::-1], refs[ratio:]
    width = inverse_ref.shape[0]
    which = which_ref[0]
    parts = []
    for j in range(halves[0].shape[1] // width):
        span = slice(j * width, (j + 1) * width)
        for k in range(ratio):
            block = halves[0][:, span]
            for shift in range(1, ratio):
                block = jnp.where((which + shift) % ratio == k, halves[shift][:, span], block)
            parts.append(block)
    image = dot(inverse_ref[...], jnp.concatenate(parts, axis=1), ((1,), (0,)))
    image_ref[...] = image
    left = stack_left(2.0 * image)
    right = stack_right(cols_ref[...])
    chunk = 256
    for start in range(0, begun_ref.shape[0], chunk):
        span = slice(start, start + chunk)
        further_ref[span, :] = begun_ref[span, :] - dot16(left[:, span], right, ((0,), (0,)))


def update_kernel(
    further_ref, image_ref, left_ref, coeffs_ref, coeffs_cols_ref, inverse_ref, *refs
):
    inners, (updated_ref, w_ref, buffer_ref, w_buffer_ref, sems) = refs[:-5], refs[-5:]
    inverse = inverse_ref[...]
    inner = tree_sum([part[...] for part in inners])
    right = dot(inverse, dot(inner, coeffs_cols_ref[...], ((1,), (0,))), ((1,), (0,)))
    right = stack_right(4.0 * right)
    count = sems.shape[0] - 1
    rows = further_ref.shape[0] // count
    copies = []
    for i in range(0, count, 2):
        span = slice(i * rows, (i + 2) * rows)
        buffer_ref[span, :] = further_ref[span, :] + dot16(left_ref[:, span], right, ((0,), (0,)))
        for part in (i, i + 1):
            span = slice(part * rows, (part + 1) * rows)
            copies.append(
                pltpu.make_async_copy(
                    buffer_ref.at[span, :], updated_ref.at[span, :], sems.at[part]
                )
            )
            copies[-1].start()
    removed = dot(inverse, dot(inner, coeffs_ref[...], ((0,), (0,))), ((1,), (0,)))
    w_buffer_ref[...] = 2.0 * (image_ref[...] - removed)
    copies.append(pltpu.make_async_copy(w_buffer_ref, w_ref, sems.at[count]))
    copies[-1].start()
    for copy in copies:
        copy.wait()


def shape(*dims, dtype=jnp.float32):
    return jax.ShapeDtypeStruct(dims, dtype)


def call(kernel, outs, args, in_specs=None, out_specs=None, scratch=(), flops=0):
    return pl.pallas_call(
        kernel,
        out_shape=outs,
        in_specs=in_specs or [VMEM] * len(args),
        out_specs=out_specs or ((VMEM,) * len(outs) if isinstance(outs, tuple) else VMEM),
        scratch_shapes=scratch,
        compiler_params=PARAMS,
        cost_estimate=pl.CostEstimate(flops=flops, bytes_accessed=1 << 18, transcendentals=0),
    )(*args)


def local(matrix, panel):
    n_row, n_col = lax.axis_size("row"), lax.axis_size("col")
    ratio = n_col // n_row
    rows, width = panel.shape
    cols = matrix.shape[1]
    which = (lax.axis_index("col") // n_row).astype(jnp.int32).reshape(1)
    chunks = 8

    *mines, panel_t, terms, gram, kept = call(
        functools.partial(panel_kernel, ratio),
        (
            *[shape(width, cols)] * ratio,
            shape(width, rows),
            shape(3 * width, rows, dtype=jnp.bfloat16),
            shape(STRIP, cols),
            shape(rows, cols),
        ),
        (
            which,
            pltpu.with_memory_space_constraint(panel.T, pltpu.HBM),
            pltpu.with_memory_space_constraint(matrix, pltpu.HBM),
        ),
        in_specs=[SMEM, HBM, HBM],
        scratch=[pltpu.SemaphoreType.DMA((2 * chunks,))],
        flops=1 << 28,
    )
    message = call(
        product_kernel, shape(width + STRIP, cols), (terms, kept, gram), flops=1 << 30
    )
    step = 1
    while 2 * step < n_row:
        message = message + partner(message, "row", step)
        step *= 2
    last = partner(message, "row", step)
    held, received, takes = spread_rows(mines[0], message)
    product_cols, gram = call(
        finish_kernel, (shape(width, cols), shape(width, width)), (last, message), flops=1 << 24
    )
    halves = [transpose_grid(product_cols, shift) for shift in reversed(range(ratio))]
    inverse = call(factor_kernel, shape(width, width), (gram,), flops=1 << 30)
    begun, basis, left, coeffs, basis_cols, coeffs_cols = call(
        basis_kernel,
        (
            shape(rows, cols),
            shape(width, rows),
            shape(3 * width, rows, dtype=jnp.bfloat16),
            shape(width, rows),
            shape(width, cols),
            shape(width, cols),
        ),
        (kept, panel_t, product_cols, inverse, received, held, takes),
        in_specs=[VMEM] * 6 + [SMEM],
        flops=1 << 30,
    )
    halves, begun = lax.optimization_barrier((halves, begun))
    inner = call(inner_kernel, shape(width, width), (*halves, *mines[::-1]), flops=1 << 24)
    further, image = call(
        functools.partial(image_kernel, ratio),
        (shape(rows, cols), shape(width, rows)),
        (which, begun, basis_cols, inverse, *halves),
        in_specs=[SMEM] + [VMEM] * (3 + ratio),
        flops=1 << 30,
    )
    inners = group_parts(inner, "row", 1, n_row)[::-1]
    updated, w_rows = call(
        update_kernel,
        (shape(rows, cols), shape(width, rows)),
        (further, image, left, coeffs, coeffs_cols, inverse, *inners),
        out_specs=(HBM, HBM),
        scratch=[
            pltpu.VMEM((rows, cols), jnp.float32),
            pltpu.VMEM((width, rows), jnp.float32),
            pltpu.SemaphoreType.DMA((chunks + 1,)),
        ],
        flops=1 << 30,
    )
    return (updated, w_rows.T, basis.T)


def solution(mesh):
    return jax.shard_map(
        local,
        mesh=mesh,
        in_specs=(P("row", "col"), P("row", None)),
        out_specs=(P("row", "col"), P("row", None), P("row", None)),
        check_vma=False,
    )
```

```python
import functools

import jax
import jax.numpy as jnp
from jax import lax
from jax.experimental import pallas as pl
from jax.experimental.pallas import tpu as pltpu
from jax.sharding import PartitionSpec as P

HIGH = lax.Precision.HIGHEST
VMEM = pl.BlockSpec(memory_space=pltpu.VMEM)
SMEM = pl.BlockSpec(memory_space=pltpu.SMEM)
HBM = pl.BlockSpec(memory_space=pltpu.HBM)
PARAMS = pltpu.CompilerParams(vmem_limit_bytes=40 * 1024 * 1024)
STRIP = 8


def dot(left, right, contract, precision=HIGH):
    return lax.dot_general(
        left, right, (contract, ((), ())), precision=precision, preferred_element_type=jnp.float32
    )


def dot16(left, right, contract):
    return dot(left, right, contract, lax.Precision.DEFAULT)


def split(value, parts):
    terms = []
    for _ in range(parts):
        terms.append(value.astype(jnp.bfloat16))
        value = value - terms[-1].astype(jnp.float32)
    return terms


def partner(value, axis, step):
    size = lax.axis_size(axis)
    return lax.ppermute(value, axis, [(i, i ^ step) for i in range(size)])


def tree_sum(parts):
    while len(parts) > 1:
        parts = [parts[i] + parts[i + 1] for i in range(0, len(parts), 2)]
    return parts[0]


def group_parts(value, axis, low, high):
    parts = [value]
    while low < high:
        value = tree_sum(parts)
        radix = min(4, high // low)
        parts = [value] + [partner(value, axis, i * low) for i in range(1, radix)]
        low *= radix
    return parts


def spread_rows(value, after):
    n_row, n_col = lax.axis_size("row"), lax.axis_size("col")
    apart = lax.axis_index("row") ^ (lax.axis_index("col") % n_row)
    bits = [1] + [1 << i for i in reversed(range(1, n_row.bit_length() - 1))]
    reached = [0]
    for bit in bits:
        pairs = []
        for c in range(n_col):
            for offset in reached:
                source = (c % n_row) ^ offset
                pairs.append((source * n_col + c, (source ^ bit) * n_col + c))
        reached += [offset ^ bit for offset in reached]
        received = lax.ppermute(value, ("row", "col"), pairs)
        takes = apart & bit != 0
        if bit == bits[-1]:
            return value, received, takes.astype(jnp.int32).reshape(1)
        received, _ = lax.optimization_barrier((received, after))
        value = jnp.where(takes, received, value)


def transpose_grid(value, shift):
    n_row, n_col = lax.axis_size("row"), lax.axis_size("col")
    ratio = n_col // n_row
    pairs = []
    for r in range(n_row):
        for k in range(ratio):
            for q in range(n_row):
                column = (k + shift) % ratio * n_row + r
                row = q if shift % 2 else q ^ (n_row // 2)
                pairs.append((row * n_col + column, r * n_col + k * n_row + q))
    return lax.ppermute(value, ("row", "col"), pairs)


def copy_rows(source, target, sems, first, pieces):
    size = source.shape[0] // pieces
    copies = []
    for piece in range(pieces):
        span = slice(piece * size, (piece + 1) * size)
        copies.append(
            pltpu.make_async_copy(source.at[span, :], target.at[span, :], sems.at[first + piece])
        )
        copies[-1].start()
    return copies


def panel_kernel(ratio, which_ref, panel_ref, matrix_ref, *refs):
    mine_refs, (held_ref, terms_ref, gram_ref, kept_ref, sems) = refs[:ratio], refs[ratio:]
    width = panel_ref.shape[0]
    pieces = sems.shape[0] // 2
    panel_copies = copy_rows(panel_ref, held_ref, sems, 0, pieces)
    matrix_copies = copy_rows(matrix_ref, kept_ref, sems, pieces, pieces)
    for copy in panel_copies:
        copy.wait()
    which = which_ref[0]
    for j in range(mine_refs[0].shape[1] // width):
        start = j * ratio * width
        blocks = [held_ref[:, start + k * width : start + (k + 1) * width] for k in range(ratio)]
        for shift, mine_ref in enumerate(mine_refs):
            block = blocks[shift]
            for k in range(1, ratio):
                block = jnp.where(which == k, blocks[(k + shift) % ratio], block)
            mine_ref[:, j * width : (j + 1) * width] = block
    panel = held_ref[...]
    terms_ref[...] = jnp.concatenate(split(panel, 3), axis=0)
    to_strip(dot(panel, panel, ((1,), (1,))), gram_ref)
    for copy in matrix_copies:
        copy.wait()


def product_kernel(terms_ref, matrix_ref, gram_ref, out_ref):
    width = out_ref.shape[0] - STRIP
    rows = matrix_ref.shape[0]
    chunk = 256
    total = jnp.zeros((width, matrix_ref.shape[1]), jnp.float32)
    for start in range(0, rows, chunk):
        span = slice(start, start + chunk)
        parts = split(matrix_ref[span, :], 3)
        for i, part in enumerate(parts):
            count = 3 - i
            out = dot16(terms_ref[: count * width, span], part, ((1,), (0,)))
            for t in range(count):
                total = total + out[t * width : (t + 1) * width, :]
    out_ref[:width, :] = total
    out_ref[width:, :] = gram_ref[...]


def to_strip(value, strip_ref):
    width = value.shape[0]
    for i in range(width // STRIP):
        strip_ref[:, i * width : (i + 1) * width] = value[i * STRIP : (i + 1) * STRIP, :]


def from_strip(strip, width):
    return jnp.concatenate(
        [strip[:, i * width : (i + 1) * width] for i in range(width // STRIP)], axis=0
    )


def finish_kernel(other_ref, mine_ref, product_ref, gram_ref):
    width = product_ref.shape[0]
    product_ref[...] = mine_ref[:width, :] + other_ref[:width, :]
    gram_ref[...] = from_strip(mine_ref[width:, :] + other_ref[width:, :], width)


def factor_kernel(gram_ref, inverse_ref):
    size = inverse_ref.shape[0]
    batch = 4
    row = lax.broadcasted_iota(jnp.int32, (size, 2 * size), 0)
    lane = lax.broadcasted_iota(jnp.int32, (size, 2 * size), 1)
    eye = jnp.where(row == lane, 1.0, 0.0).astype(jnp.float32)
    table = jnp.concatenate([eye[:, :size], gram_ref[...]], axis=1)
    for first in range(0, size, batch):
        base = first // 8 * 8
        height = size - base
        low = table[base:, :]
        low_row = row[base:, :]
        cols = [
            jnp.broadcast_to(low[:, size + first + t : size + first + t + 1], (height, 2 * size))
            for t in range(batch)
        ]
        rows = [low[first - base + t : first - base + t + 1, :] for t in range(batch)]
        for t in range(batch):
            at = first - base + t
            scale = 1.0 / cols[t][at : at + 1, :]
            factor = jnp.where(low_row > first + t, cols[t] * scale, 0.0)
            for s in range(t + 1, batch):
                cols[s] = cols[s] - factor * cols[s][at : at + 1, :]
                rows[s] = rows[s] - factor[first - base + s : first - base + s + 1, :] * rows[t]
            low = low - factor * rows[t]
        table = low if base == 0 else jnp.concatenate([table[:base, :], low], axis=0)
    diagonal = jnp.sum(jnp.where(lane == row + size, table, 0.0), axis=1, keepdims=True)
    inverse_ref[...] = (table / jnp.sqrt(diagonal))[:, :size]


def stack_left(value):
    high, low = split(value, 2)
    return jnp.concatenate([high, low, high], axis=0)


def stack_right(value):
    high, low = split(value, 2)
    return jnp.concatenate([high, high, low], axis=0)


def basis_kernel(
    matrix_ref, panel_ref, product_cols_ref, inverse_ref,
    begun_ref, basis_ref, left_ref, coeffs_ref,
):
    inverse = inverse_ref[...]
    basis = dot(inverse, panel_ref[...], ((1,), (0,)))
    image_cols = dot(inverse, product_cols_ref[...], ((1,), (0,)))
    basis_ref[...] = basis
    coeffs_ref[...] = dot(inverse, basis, ((0,), (0,)))
    left = stack_left(basis)
    left_ref[...] = left
    right = stack_right(2.0 * image_cols)
    chunk = 256
    for start in range(0, matrix_ref.shape[0], chunk):
        span = slice(start, start + chunk)
        begun_ref[span, :] = matrix_ref[span, :] - dot16(left[:, span], right, ((0,), (0,)))


def columns_kernel(inverse_ref, received_ref, held_ref, takes_ref, cols_ref, coeffs_cols_ref):
    inverse = inverse_ref[...]
    panel_cols = jnp.where(takes_ref[0] != 0, received_ref[...], held_ref[...])
    cols = dot(inverse, panel_cols, ((1,), (0,)))
    cols_ref[...] = cols
    coeffs_cols_ref[...] = dot(inverse, cols, ((0,), (0,)))


def inner_kernel(*refs):
    count = len(refs) // 2
    inner_ref = refs[-1]
    inner_ref[...] = sum(
        dot(refs[count + i][...], refs[i][...], ((1,), (1,))) for i in range(count)
    )


def image_kernel(ratio, which_ref, begun_ref, cols_ref, inverse_ref, *refs):
    halves, (further_ref, image_ref) = refs[:ratio][::-1], refs[ratio:]
    width = inverse_ref.shape[0]
    which = which_ref[0]
    parts = []
    for j in range(halves[0].shape[1] // width):
        span = slice(j * width, (j + 1) * width)
        for k in range(ratio):
            block = halves[0][:, span]
            for shift in range(1, ratio):
                block = jnp.where((which + shift) % ratio == k, halves[shift][:, span], block)
            parts.append(block)
    image = dot(inverse_ref[...], jnp.concatenate(parts, axis=1), ((1,), (0,)))
    image_ref[...] = image
    left = stack_left(2.0 * image)
    right = stack_right(cols_ref[...])
    chunk = 256
    for start in range(0, begun_ref.shape[0], chunk):
        span = slice(start, start + chunk)
        further_ref[span, :] = begun_ref[span, :] - dot16(left[:, span], right, ((0,), (0,)))


def update_kernel(
    further_ref, image_ref, left_ref, coeffs_ref, coeffs_cols_ref, inverse_ref, *refs
):
    inners, (updated_ref, w_ref, buffer_ref, w_buffer_ref, sems) = refs[:-5], refs[-5:]
    inverse = inverse_ref[...]
    inner = tree_sum([part[...] for part in inners])
    right = dot(inverse, dot(inner, coeffs_cols_ref[...], ((1,), (0,))), ((1,), (0,)))
    right = stack_right(4.0 * right)
    count = sems.shape[0] - 1
    chunk = further_ref.shape[0] // count
    copies = []
    for i in range(count):
        span = slice(i * chunk, (i + 1) * chunk)
        buffer_ref[span, :] = further_ref[span, :] + dot16(left_ref[:, span], right, ((0,), (0,)))
        copies.append(
            pltpu.make_async_copy(buffer_ref.at[span, :], updated_ref.at[span, :], sems.at[i])
        )
        copies[-1].start()
    removed = dot(inverse, dot(inner, coeffs_ref[...], ((0,), (0,))), ((1,), (0,)))
    w_buffer_ref[...] = 2.0 * (image_ref[...] - removed)
    copies.append(pltpu.make_async_copy(w_buffer_ref, w_ref, sems.at[count]))
    copies[-1].start()
    for copy in copies:
        copy.wait()


def shape(*dims, dtype=jnp.float32):
    return jax.ShapeDtypeStruct(dims, dtype)


def call(kernel, outs, args, in_specs=None, out_specs=None, scratch=(), flops=0):
    return pl.pallas_call(
        kernel,
        out_shape=outs,
        in_specs=in_specs or [VMEM] * len(args),
        out_specs=out_specs or ((VMEM,) * len(outs) if isinstance(outs, tuple) else VMEM),
        scratch_shapes=scratch,
        compiler_params=PARAMS,
        cost_estimate=pl.CostEstimate(flops=flops, bytes_accessed=1 << 18, transcendentals=0),
    )(*args)


def local(matrix, panel):
    n_row, n_col = lax.axis_size("row"), lax.axis_size("col")
    ratio = n_col // n_row
    rows, width = panel.shape
    cols = matrix.shape[1]
    which = (lax.axis_index("col") // n_row).astype(jnp.int32).reshape(1)
    chunks = 8

    *mines, panel_t, terms, gram, kept = call(
        functools.partial(panel_kernel, ratio),
        (
            *[shape(width, cols)] * ratio,
            shape(width, rows),
            shape(3 * width, rows, dtype=jnp.bfloat16),
            shape(STRIP, cols),
            shape(rows, cols),
        ),
        (
            which,
            pltpu.with_memory_space_constraint(panel.T, pltpu.HBM),
            pltpu.with_memory_space_constraint(matrix, pltpu.HBM),
        ),
        in_specs=[SMEM, HBM, HBM],
        scratch=[pltpu.SemaphoreType.DMA((2 * chunks,))],
        flops=1 << 28,
    )
    message = call(
        product_kernel, shape(width + STRIP, cols), (terms, kept, gram), flops=1 << 30
    )
    step = 1
    while 2 * step < n_row:
        message = message + partner(message, "row", step)
        step *= 2
    last = partner(message, "row", step)
    product_cols, gram = call(
        finish_kernel, (shape(width, cols), shape(width, width)), (last, message), flops=1 << 24
    )
    halves = [transpose_grid(product_cols, shift) for shift in reversed(range(ratio))]
    inverse = call(factor_kernel, shape(width, width), (gram,), flops=1 << 30)
    begun, basis, left, coeffs = call(
        basis_kernel,
        (
            shape(rows, cols),
            shape(width, rows),
            shape(3 * width, rows, dtype=jnp.bfloat16),
            shape(width, rows),
        ),
        (kept, panel_t, product_cols, inverse),
        flops=1 << 30,
    )
    held, received, takes = spread_rows(mines[0], coeffs)
    halves, begun = lax.optimization_barrier((halves, begun))
    inner = call(inner_kernel, shape(width, width), (*halves, *mines[::-1]), flops=1 << 24)
    received, _ = lax.optimization_barrier((received, inner))
    basis_cols, coeffs_cols = call(
        columns_kernel,
        (shape(width, cols), shape(width, cols)),
        (inverse, received, held, takes),
        in_specs=[VMEM] * 3 + [SMEM],
        flops=1 << 24,
    )
    further, image = call(
        functools.partial(image_kernel, ratio),
        (shape(rows, cols), shape(width, rows)),
        (which, begun, basis_cols, inverse, *halves),
        in_specs=[SMEM] + [VMEM] * (3 + ratio),
        flops=1 << 30,
    )
    inners = group_parts(inner, "row", 1, n_row)[::-1]
    updated, w_rows = call(
        update_kernel,
        (shape(rows, cols), shape(width, rows)),
        (further, image, left, coeffs, coeffs_cols, inverse, *inners),
        out_specs=(HBM, HBM),
        scratch=[
            pltpu.VMEM((rows, cols), jnp.float32),
            pltpu.VMEM((width, rows), jnp.float32),
            pltpu.SemaphoreType.DMA((chunks + 1,)),
        ],
        flops=1 << 30,
    )
    return (updated, w_rows.T, basis.T)


def solution(mesh):
    return jax.shard_map(
        local,
        mesh=mesh,
        in_specs=(P("row", "col"), P("row", None)),
        out_specs=(P("row", "col"), P("row", None), P("row", None)),
        check_vma=False,
    )
```

```python
import functools

import jax
import jax.numpy as jnp
from jax import lax
from jax.experimental import pallas as pl
from jax.experimental.pallas import tpu as pltpu
from jax.sharding import PartitionSpec as P

HIGH = lax.Precision.HIGHEST
VMEM = pl.BlockSpec(memory_space=pltpu.VMEM)
SMEM = pl.BlockSpec(memory_space=pltpu.SMEM)
HBM = pl.BlockSpec(memory_space=pltpu.HBM)
PARAMS = pltpu.CompilerParams(vmem_limit_bytes=16 * 1024 * 1024)
STRIP = 8


def dot(left, right, contract, precision=HIGH):
    return lax.dot_general(
        left, right, (contract, ((), ())), precision=precision, preferred_element_type=jnp.float32
    )


def dot16(left, right, contract):
    return dot(left, right, contract, lax.Precision.DEFAULT)


def split(value, parts):
    terms = []
    for _ in range(parts):
        terms.append(value.astype(jnp.bfloat16))
        value = value - terms[-1].astype(jnp.float32)
    return terms


def partner(value, axis, step):
    size = lax.axis_size(axis)
    return lax.ppermute(value, axis, [(i, i ^ step) for i in range(size)])


def tree_sum(parts):
    while len(parts) > 1:
        parts = [parts[i] + parts[i + 1] for i in range(0, len(parts), 2)]
    return parts[0]


def group_parts(value, axis, low, high):
    parts = [value]
    while low < high:
        value = tree_sum(parts)
        radix = min(4, high // low)
        parts = [value] + [partner(value, axis, i * low) for i in range(1, radix)]
        low *= radix
    return parts


def spread_rows(value, after):
    n_row, n_col = lax.axis_size("row"), lax.axis_size("col")
    apart = lax.axis_index("row") ^ (lax.axis_index("col") % n_row)
    bits = [1] + [1 << i for i in reversed(range(1, n_row.bit_length() - 1))]
    reached = [0]
    for bit in bits:
        pairs = []
        for c in range(n_col):
            for offset in reached:
                source = (c % n_row) ^ offset
                pairs.append((source * n_col + c, (source ^ bit) * n_col + c))
        reached += [offset ^ bit for offset in reached]
        received = lax.ppermute(value, ("row", "col"), pairs)
        takes = apart & bit != 0
        if bit == bits[-1]:
            return value, received, takes.astype(jnp.int32).reshape(1)
        received, _ = lax.optimization_barrier((received, after))
        value = jnp.where(takes, received, value)


def transpose_grid(value, shift):
    n_row, n_col = lax.axis_size("row"), lax.axis_size("col")
    ratio = n_col // n_row
    pairs = []
    for r in range(n_row):
        for k in range(ratio):
            for q in range(n_row):
                column = (k + shift) % ratio * n_row + r
                row = q if shift % 2 else q ^ (n_row // 2)
                pairs.append((row * n_col + column, r * n_col + k * n_row + q))
    return lax.ppermute(value, ("row", "col"), pairs)


def copy_rows(source, target, sems, first, pieces):
    size = source.shape[0] // pieces
    copies = []
    for piece in range(pieces):
        span = slice(piece * size, (piece + 1) * size)
        copies.append(
            pltpu.make_async_copy(source.at[span, :], target.at[span, :], sems.at[first + piece])
        )
        copies[-1].start()
    return copies


def panel_kernel(ratio, which_ref, panel_ref, matrix_ref, *refs):
    mine_refs, (held_ref, terms_ref, gram_ref, kept_ref, sems) = refs[:ratio], refs[ratio:]
    width = panel_ref.shape[0]
    pieces = sems.shape[0] // 2
    panel_copies = copy_rows(panel_ref, held_ref, sems, 0, pieces)
    matrix_copies = copy_rows(matrix_ref, kept_ref, sems, pieces, pieces)
    for copy in panel_copies:
        copy.wait()
    which = which_ref[0]
    for j in range(mine_refs[0].shape[1] // width):
        start = j * ratio * width
        blocks = [held_ref[:, start + k * width : start + (k + 1) * width] for k in range(ratio)]
        for shift, mine_ref in enumerate(mine_refs):
            block = blocks[shift]
            for k in range(1, ratio):
                block = jnp.where(which == k, blocks[(k + shift) % ratio], block)
            mine_ref[:, j * width : (j + 1) * width] = block
    panel = held_ref[...]
    terms_ref[...] = jnp.concatenate(split(panel, 3), axis=0)
    to_strip(dot(panel, panel, ((1,), (1,))), gram_ref)
    for copy in matrix_copies:
        copy.wait()


def product_kernel(terms_ref, matrix_ref, gram_ref, out_ref):
    width = out_ref.shape[0] - STRIP
    rows = matrix_ref.shape[0]
    chunk = 256
    total = jnp.zeros((width, matrix_ref.shape[1]), jnp.float32)
    for start in range(0, rows, chunk):
        span = slice(start, start + chunk)
        parts = split(matrix_ref[span, :], 3)
        for i, part in enumerate(parts):
            count = 3 - i
            out = dot16(terms_ref[: count * width, span], part, ((1,), (0,)))
            for t in range(count):
                total = total + out[t * width : (t + 1) * width, :]
    out_ref[:width, :] = total
    out_ref[width:, :] = gram_ref[...]


def to_strip(value, strip_ref):
    width = value.shape[0]
    for i in range(width // STRIP):
        strip_ref[:, i * width : (i + 1) * width] = value[i * STRIP : (i + 1) * STRIP, :]


def from_strip(strip, width):
    return jnp.concatenate(
        [strip[:, i * width : (i + 1) * width] for i in range(width // STRIP)], axis=0
    )


def finish_kernel(other_ref, mine_ref, product_ref, gram_ref):
    width = product_ref.shape[0]
    product_ref[...] = mine_ref[:width, :] + other_ref[:width, :]
    gram_ref[...] = from_strip(mine_ref[width:, :] + other_ref[width:, :], width)


def factor_kernel(gram_ref, inverse_ref):
    size = inverse_ref.shape[0]
    batch = 4
    row = lax.broadcasted_iota(jnp.int32, (size, 2 * size), 0)
    lane = lax.broadcasted_iota(jnp.int32, (size, 2 * size), 1)
    eye = jnp.where(row == lane, 1.0, 0.0).astype(jnp.float32)
    table = jnp.concatenate([eye[:, :size], gram_ref[...]], axis=1)
    for first in range(0, size, batch):
        base = first // 8 * 8
        height = size - base
        low = table[base:, :]
        low_row = row[base:, :]
        cols = [
            jnp.broadcast_to(low[:, size + first + t : size + first + t + 1], (height, 2 * size))
            for t in range(batch)
        ]
        rows = [low[first - base + t : first - base + t + 1, :] for t in range(batch)]
        for t in range(batch):
            at = first - base + t
            scale = 1.0 / cols[t][at : at + 1, :]
            factor = jnp.where(low_row > first + t, cols[t] * scale, 0.0)
            for s in range(t + 1, batch):
                cols[s] = cols[s] - factor * cols[s][at : at + 1, :]
                rows[s] = rows[s] - factor[first - base + s : first - base + s + 1, :] * rows[t]
            low = low - factor * rows[t]
        table = low if base == 0 else jnp.concatenate([table[:base, :], low], axis=0)
    diagonal = jnp.sum(jnp.where(lane == row + size, table, 0.0), axis=1, keepdims=True)
    inverse_ref[...] = (table / jnp.sqrt(diagonal))[:, :size]


def stack_left(value):
    high, low = split(value, 2)
    return jnp.concatenate([high, low, high], axis=0)


def stack_right(value):
    high, low = split(value, 2)
    return jnp.concatenate([high, high, low], axis=0)


def basis_kernel(
    matrix_ref, panel_ref, product_cols_ref, inverse_ref,
    begun_ref, basis_ref, left_ref, coeffs_ref,
):
    inverse = inverse_ref[...]
    basis = dot(inverse, panel_ref[...], ((1,), (0,)))
    image_cols = dot(inverse, product_cols_ref[...], ((1,), (0,)))
    basis_ref[...] = basis
    coeffs_ref[...] = dot(inverse, basis, ((0,), (0,)))
    left = stack_left(basis)
    left_ref[...] = left
    right = stack_right(2.0 * image_cols)
    chunk = 256
    for start in range(0, matrix_ref.shape[0], chunk):
        span = slice(start, start + chunk)
        begun_ref[span, :] = matrix_ref[span, :] - dot16(left[:, span], right, ((0,), (0,)))


def columns_kernel(inverse_ref, received_ref, held_ref, takes_ref, cols_ref, coeffs_cols_ref):
    inverse = inverse_ref[...]
    panel_cols = jnp.where(takes_ref[0] != 0, received_ref[...], held_ref[...])
    cols = dot(inverse, panel_cols, ((1,), (0,)))
    cols_ref[...] = cols
    coeffs_cols_ref[...] = dot(inverse, cols, ((0,), (0,)))


def inner_kernel(*refs):
    count = len(refs) // 2
    inner_ref = refs[-1]
    inner_ref[...] = sum(
        dot(refs[count + i][...], refs[i][...], ((1,), (1,))) for i in range(count)
    )


def image_kernel(ratio, which_ref, begun_ref, cols_ref, inverse_ref, *refs):
    halves, (further_ref, image_ref) = refs[:ratio][::-1], refs[ratio:]
    width = inverse_ref.shape[0]
    which = which_ref[0]
    parts = []
    for j in range(halves[0].shape[1] // width):
        span = slice(j * width, (j + 1) * width)
        for k in range(ratio):
            block = halves[0][:, span]
            for shift in range(1, ratio):
                block = jnp.where((which + shift) % ratio == k, halves[shift][:, span], block)
            parts.append(block)
    image = dot(inverse_ref[...], jnp.concatenate(parts, axis=1), ((1,), (0,)))
    image_ref[...] = image
    left = stack_left(2.0 * image)
    right = stack_right(cols_ref[...])
    chunk = 256
    for start in range(0, begun_ref.shape[0], chunk):
        span = slice(start, start + chunk)
        further_ref[span, :] = begun_ref[span, :] - dot16(left[:, span], right, ((0,), (0,)))


def update_kernel(
    further_ref, image_ref, left_ref, coeffs_ref, coeffs_cols_ref, inverse_ref, *refs
):
    inners, (updated_ref, w_ref, buffer_ref, w_buffer_ref, sems) = refs[:-5], refs[-5:]
    inverse = inverse_ref[...]
    inner = tree_sum([part[...] for part in inners])
    right = dot(inverse, dot(inner, coeffs_cols_ref[...], ((1,), (0,))), ((1,), (0,)))
    right = stack_right(4.0 * right)
    count = sems.shape[0] - 1
    chunk = further_ref.shape[0] // count
    copies = []
    for i in range(count):
        span = slice(i * chunk, (i + 1) * chunk)
        buffer_ref[span, :] = further_ref[span, :] + dot16(left_ref[:, span], right, ((0,), (0,)))
        copies.append(
            pltpu.make_async_copy(buffer_ref.at[span, :], updated_ref.at[span, :], sems.at[i])
        )
        copies[-1].start()
    removed = dot(inverse, dot(inner, coeffs_ref[...], ((0,), (0,))), ((1,), (0,)))
    w_buffer_ref[...] = 2.0 * (image_ref[...] - removed)
    copies.append(pltpu.make_async_copy(w_buffer_ref, w_ref, sems.at[count]))
    copies[-1].start()
    for copy in copies:
        copy.wait()


def shape(*dims, dtype=jnp.float32):
    return jax.ShapeDtypeStruct(dims, dtype)


def call(kernel, outs, args, in_specs=None, out_specs=None, scratch=(), flops=0):
    return pl.pallas_call(
        kernel,
        out_shape=outs,
        in_specs=in_specs or [VMEM] * len(args),
        out_specs=out_specs or ((VMEM,) * len(outs) if isinstance(outs, tuple) else VMEM),
        scratch_shapes=scratch,
        compiler_params=PARAMS,
        cost_estimate=pl.CostEstimate(flops=flops, bytes_accessed=1 << 18, transcendentals=0),
    )(*args)


def local(matrix, panel):
    n_row, n_col = lax.axis_size("row"), lax.axis_size("col")
    ratio = n_col // n_row
    rows, width = panel.shape
    cols = matrix.shape[1]
    which = (lax.axis_index("col") // n_row).astype(jnp.int32).reshape(1)
    chunks = 8

    *mines, panel_t, terms, gram, kept = call(
        functools.partial(panel_kernel, ratio),
        (
            *[shape(width, cols)] * ratio,
            shape(width, rows),
            shape(3 * width, rows, dtype=jnp.bfloat16),
            shape(STRIP, cols),
            shape(rows, cols),
        ),
        (
            which,
            pltpu.with_memory_space_constraint(panel.T, pltpu.HBM),
            pltpu.with_memory_space_constraint(matrix, pltpu.HBM),
        ),
        in_specs=[SMEM, HBM, HBM],
        scratch=[pltpu.SemaphoreType.DMA((2 * chunks,))],
        flops=1 << 28,
    )
    message = call(
        product_kernel, shape(width + STRIP, cols), (terms, kept, gram), flops=1 << 30
    )
    step = 1
    while 2 * step < n_row:
        message = message + partner(message, "row", step)
        step *= 2
    last = partner(message, "row", step)
    product_cols, gram = call(
        finish_kernel, (shape(width, cols), shape(width, width)), (last, message), flops=1 << 24
    )
    halves = [transpose_grid(product_cols, shift) for shift in reversed(range(ratio))]
    inverse = call(factor_kernel, shape(width, width), (gram,), flops=1 << 30)
    begun, basis, left, coeffs = call(
        basis_kernel,
        (
            shape(rows, cols),
            shape(width, rows),
            shape(3 * width, rows, dtype=jnp.bfloat16),
            shape(width, rows),
        ),
        (kept, panel_t, product_cols, inverse),
        flops=1 << 30,
    )
    held, received, takes = spread_rows(mines[0], coeffs)
    halves, begun = lax.optimization_barrier((halves, begun))
    inner = call(inner_kernel, shape(width, width), (*halves, *mines[::-1]), flops=1 << 24)
    received, _ = lax.optimization_barrier((received, inner))
    basis_cols, coeffs_cols = call(
        columns_kernel,
        (shape(width, cols), shape(width, cols)),
        (inverse, received, held, takes),
        in_specs=[VMEM] * 3 + [SMEM],
        flops=1 << 24,
    )
    further, image = call(
        functools.partial(image_kernel, ratio),
        (shape(rows, cols), shape(width, rows)),
        (which, begun, basis_cols, inverse, *halves),
        in_specs=[SMEM] + [VMEM] * (3 + ratio),
        flops=1 << 30,
    )
    inners = group_parts(inner, "row", 1, n_row)[::-1]
    updated, w_rows = call(
        update_kernel,
        (shape(rows, cols), shape(width, rows)),
        (further, image, left, coeffs, coeffs_cols, inverse, *inners),
        out_specs=(HBM, HBM),
        scratch=[
            pltpu.VMEM((rows, cols), jnp.float32),
            pltpu.VMEM((width, rows), jnp.float32),
            pltpu.SemaphoreType.DMA((chunks + 1,)),
        ],
        flops=1 << 30,
    )
    return (updated, w_rows.T, basis.T)


def solution(mesh):
    return jax.shard_map(
        local,
        mesh=mesh,
        in_specs=(P("row", "col"), P("row", None)),
        out_specs=(P("row", "col"), P("row", None), P("row", None)),
        check_vma=False,
    )
```
